256 devices in a mesh: gx: 4 (over x), gy: 8 (over y, core), gz: 8 (over z).
Axes of the slice: x: 4, y: 4, z: 8, core: 2. Of those that a mesh axis runs over, the one named last changes fastest.
Arguments:
- velocity: float32 [3, 32, 256, 1024], P(None, 'gx', 'gy', 'gz'), may hold values from -6 to 6
- inverse_coef: float32 [32, 256, 1024], P('gx', 'gy', 'gz'), may hold values from 0.3 to 3
- enthalpy: float32 [32, 256, 1024], P('gx', 'gy', 'gz'), may hold values from -6 to 6
- void: float32 [32, 256, 1024], P('gx', 'gy', 'gz'), may hold values from 0.05 to 0.7
- wall_cells: int32 [4096, 128], P(('gx', 'gy', 'gz')), may hold values from 0 to 32767, as said below
- wall_normal: int32 [4096, 128], P(('gx', 'gy', 'gz')), may hold values from 0 to 5
- wall_flag: int32 [4096, 128], P(('gx', 'gy', 'gz')), may hold values from 0 to 2, as said below
Outputs:
- velocity_new: float32 [3, 32, 256, 1024], P(None, 'gx', 'gy', 'gz')
- pressure: float32 [32, 256, 1024], P('gx', 'gy', 'gz')
- enthalpy_new: float32 [32, 256, 1024], P('gx', 'gy', 'gz')
The draws below stay inside these ranges and needn't reach their ends.
Inputs may be any that keep to these rules, and one draw needn't show every extreme that they name: `wall_cells`: the indices within the 16 tile rows of one device are all distinct. `wall_flag`: on each device the live tiles come first, 1 to 16 of them, every slot of a live tile is 1 or 2 and every slot of the others 0; some device has all 16 tiles live.
All inputs are finite; a program needn't handle non-finite values.
Results may differ from the reference program's by a relative error of at most 0.0001.
Values sent between devices are 32-bit elements; how exact they have to be, the bound alone decides.
A program may use at most 128 MiB of HBM per device.

```python
import math
import jax
import jax.numpy as jnp
from jax import lax

CX = 8
CY = 32
CZ = 128
WT = 16
ITERS = 3
NX = 32
NY = 256
NZ = 1024
TILES = 4096
N_GY = 8
N_GZ = 8
DEVICES = 256


def pick_cells(key):
    first, second = jax.random.split(key)
    cells = CX * CY * CZ
    middle = jax.random.permutation(first, cells - 2)[:WT * 128 - 2] + 1
    ends = jnp.array([0, cells - 1], dtype=middle.dtype)
    picks = jnp.concatenate([ends, middle])
    return jax.random.permutation(second, picks)


def draw_wall_cells(key, part):
    key = jax.random.fold_in(key, 11)
    keys = jax.random.split(key, DEVICES)
    picks = jax.vmap(pick_cells)(keys)
    return picks.reshape(DEVICES * WT, 128).astype(jnp.int32)


def draw_wall_flag(key, part):
    key = jax.random.fold_in(key, 23)
    first, second, third = jax.random.split(key, 3)
    live = jax.random.randint(first, (DEVICES,), 1, WT + 1)
    fullest = jax.random.randint(second, (), 0, DEVICES)
    live = jnp.where(jnp.arange(DEVICES) == fullest, WT, live)
    levels = jax.random.randint(third, (DEVICES, WT, 128), 1, 3)
    slots = jnp.arange(WT)[None, :, None]
    flags = jnp.where(slots < live[:, None, None], levels, 0)
    return flags.reshape(DEVICES * WT, 128).astype(jnp.int32)


def place_ends(entries, own_key, low, top_value):
    place = [jax.random.randint(jax.random.fold_in(own_key, axis), (), 0, length) for axis, length in enumerate(entries.shape)]
    widest = entries.shape.index(max(entries.shape))
    neighbour = place[:widest] + [(place[widest] + 1) % entries.shape[widest]] + place[widest + 1:]
    return entries.at[tuple(place)].set(low).at[tuple(neighbour)].set(top_value)


def level_of(key, extent, shards, smallest, largest):
    def one(position, blocks):
        heights = jax.random.uniform(jax.random.fold_in(jax.random.fold_in(key, 6), position), (blocks,), jnp.float32, smallest / len(shards), largest / len(shards))
        return jnp.repeat(jnp.exp(heights), extent[position] // blocks).reshape((-1,) + (1,) * (len(extent) - position - 1))

    loudness = one(*shards[0])
    for cut in shards[1:]:
        loudness = loudness * one(*cut)
    return loudness


def scatter_about(own_key, extent, width, bound, pieces=(), kind=jnp.bfloat16):
    result = jax.random.normal(own_key, extent, jnp.float32) * width
    if len(pieces) > 0:
        result = level_of(own_key, extent, pieces, -0.22, 0.18) * result
    return jnp.clip(result, min=-bound, max=bound).astype(kind)


def setup_inputs(seed: int = 0) -> dict:
    streams_of = jax.random.split(jax.random.key(seed), 8)
    velocity = scatter_about(streams_of[0], (3, NX, NY, NZ), 1.0, 6.0, ((1, 4), (2, 8), (3, 8)), jnp.float32)
    inverse_coef = jnp.clip(jnp.exp(math.log(3.0) - 2.3025851 * jax.random.uniform(streams_of[1], (NX, NY, NZ), jnp.float32) ** level_of(streams_of[1], (NX, NY, NZ), ((0, 4), (1, 8), (2, 8)), -0.2, 0.2)), 0.3, 3.0)
    enthalpy = scatter_about(streams_of[2], (NX, NY, NZ), 1.0, 6.0, ((0, 4), (1, 8), (2, 8)), jnp.float32)
    void = jnp.clip(0.05 + 0.65 * jax.random.uniform(streams_of[3], (NX, NY, NZ), jnp.float32) ** level_of(streams_of[3], (NX, NY, NZ), ((0, 4), (1, 8), (2, 8)), -0.2, 0.2), 0.05, 0.7)
    wall_cells = draw_wall_cells(jax.random.fold_in(streams_of[7], 71), 0)
    wall_normal = place_ends(jax.random.randint(streams_of[5], (TILES, 128), 0, 6), jax.random.fold_in(streams_of[5], 1), 0, 5).astype(jnp.int32)
    wall_flag = draw_wall_flag(jax.random.fold_in(streams_of[7], 71), 0)
    return {"velocity": velocity, "inverse_coef": inverse_coef, "enthalpy": enthalpy, "void": void, "wall_cells": wall_cells, "wall_normal": wall_normal, "wall_flag": wall_flag}


DIFFUSE = 0.1
HEATING = 0.5
LATENT = 2.0
EXPANSION = 1.5

def shifted(padded):
    return (padded[..., 2:, 1:-1, 1:-1], padded[..., :-2, 1:-1, 1:-1], padded[..., 1:-1, 2:, 1:-1], padded[..., 1:-1, :-2, 1:-1], padded[..., 1:-1, 1:-1, 2:], padded[..., 1:-1, 1:-1, :-2])

def inner(padded):
    return padded[..., 1:-1, 1:-1, 1:-1]

def wall_flux(comps, void_cells, normal, flag):
    which = normal // 2
    select = (jnp.arange(3, dtype=jnp.int32)[:, None, None] == which[None]).astype(jnp.float32)
    parallel = lax.optimization_barrier(jnp.sum(comps * comps * (1.0 - select), axis=0))
    speed = jnp.sqrt(parallel + 0.25)
    heat_level = flag.astype(jnp.float32)
    liquid = 1.0 - void_cells
    evap = 1.5 * void_cells * heat_level * heat_level
    total = liquid * speed * heat_level + 0.6 * liquid * heat_level * jnp.sqrt(heat_level) + evap
    return (total, evap / LATENT)

def balance_terms(stacked_pad, heat_source, mass_source):
    near_h = shifted(stacked_pad[3])
    centre_h = inner(stacked_pad[3])
    laplace = near_h[0] + near_h[1] + near_h[2] + near_h[3] + near_h[4] + near_h[5] - 6.0 * centre_h
    enthalpy_new = centre_h + DIFFUSE * laplace + HEATING * heat_source
    near_u = shifted(stacked_pad[0:3])
    diverge = 0.5 * (near_u[0][0] - near_u[1][0] + (near_u[2][1] - near_u[3][1]) + (near_u[4][2] - near_u[5][2]))
    imbalance = EXPANSION * mass_source - diverge
    return (enthalpy_new, imbalance)

def apply_operator(coef_pad, field_pad):
    centre_c = inner(coef_pad)
    centre_v = inner(field_pad)
    total = jnp.zeros(centre_v.shape, jnp.float32)
    for near_c, near_v in zip(shifted(coef_pad), shifted(field_pad)):
        total = total + 0.5 * (centre_c + near_c) * (centre_v - near_v)
    return total

def correct_velocity(velocity, coef, pressure_pad):
    near = shifted(pressure_pad)
    slope = jnp.stack([0.5 * (near[0] - near[1]), 0.5 * (near[2] - near[3]), 0.5 * (near[4] - near[5])])
    return velocity - coef[None] * slope

def reference(velocity, inverse_coef, enthalpy, void, wall_cells, wall_normal, wall_flag):
    device = jnp.arange(TILES, dtype=jnp.int32) // WT
    place_x = device // (N_GY * N_GZ)
    place_y = device // N_GZ % N_GY
    place_z = device % N_GZ
    local_i = wall_cells // (CY * CZ)
    local_j = wall_cells // CZ % CY
    local_k = wall_cells % CZ
    global_flat = ((place_x[:, None] * CX + local_i) * NY + place_y[:, None] * CY + local_j) * NZ + place_z[:, None] * CZ + local_k
    flat_vel = velocity.reshape(3, -1)
    comps = flat_vel[:, global_flat]
    void_cells = void.reshape(-1)[global_flat]
    heat, evap = wall_flux(comps, void_cells, wall_normal, wall_flag)
    sources = jnp.zeros((2, NX * NY * NZ), jnp.float32)
    sources = sources.at[:, global_flat.reshape(-1)].add(jnp.stack([heat.reshape(-1), evap.reshape(-1)]))
    sources = sources.reshape(2, NX, NY, NZ)
    stacked = jnp.concatenate([velocity, enthalpy[None], inverse_coef[None]], axis=0)
    stacked_pad = jnp.pad(stacked, ((0, 0), (1, 1), (1, 1), (1, 1)))
    enthalpy_new, imbalance = balance_terms(stacked_pad, sources[0], sources[1])
    coef_pad = stacked_pad[4]
    pressure = jnp.zeros_like(imbalance)
    residual = imbalance
    direction = imbalance
    norm_now = jnp.sum(residual * residual)
    for step in range(ITERS):
        image = apply_operator(coef_pad, jnp.pad(direction, 1))
        alpha = norm_now / jnp.sum(direction * image)
        pressure = pressure + alpha * direction
        residual = residual - alpha * image
        norm_next = jnp.sum(residual * residual)
        direction = residual + norm_next / norm_now * direction
        norm_now = norm_next
    velocity_new = correct_velocity(velocity, inverse_coef, jnp.pad(pressure, 1))
    return (velocity_new, pressure, enthalpy_new)
```

```python
import jax
import jax.numpy as jnp
from jax import lax
from jax.experimental import pallas as pl
from jax.experimental.pallas import tpu as pltpu
from jax.sharding import PartitionSpec as P

MESH = pl.DeviceIdType.MESH
NGX, NGY, NGZ = 4, 8, 8
BX, BY, BZ = 8, 32, 128
SLOTS = 16
DIFFUSE = 0.1
HEATING = 0.5
EXPANSION = 1.5
SCALE = 16.0
U0, H, C, U1, U2, W0, W1, W2 = range(8)
TZ_U2, TZ_H, TZ_C, TZ_W0, TZ_W1, TZ_W2 = range(6)
ROWS = slice(8, 40)
PIVOT_FLOOR = 1e-9


def two_sum(a, b):
    s = a + b
    t = s - a
    return s, (a - (s - t)) + (b - t)


def quick_sum(a, b):
    s = a + b
    return s, b - (s - a)


def split(a):
    t = 4097.0 * a
    high = t - (t - a)
    return high, a - high


def two_mul(a, b):
    p = a * b
    ah, al = split(a)
    bh, bl = split(b)
    return p, ((ah * bh - p) + ah * bl + al * bh) + al * bl


def df_sub(a, b):
    s, e = two_sum(a[0], -b[0])
    return quick_sum(s, e + (a[1] - b[1]))


def df_mul(a, b):
    p, e = two_mul(a[0], b[0])
    return quick_sum(p, e + (a[0] * b[1] + a[1] * b[0]))


def df_div(a, b):
    q = a[0] / b[0]
    p, e = two_mul(q, b[0])
    rest = ((a[0] - p) - e) + a[1] - q * b[1]
    return quick_sum(q, rest / b[0])


def solve_moments(m):
    l10 = df_div(m[2], m[1])
    l20 = df_div(m[3], m[1])
    d1 = df_sub(m[3], df_mul(l10, m[2]))
    e12 = df_sub(m[4], df_mul(l10, m[3]))
    y1 = df_sub(m[1], df_mul(l10, m[0]))
    y2 = df_sub(m[2], df_mul(l20, m[0]))
    d2 = df_sub(m[5], df_mul(l20, m[3]))
    ok1 = d1[0] > PIVOT_FLOOR * m[3][0]
    l21 = df_div(e12, d1)
    l21 = tuple(jnp.where(ok1, v, 0.0) for v in l21)
    d2 = df_sub(d2, df_mul(l21, e12))
    y2 = df_sub(y2, df_mul(l21, y1))
    ok2 = ok1 & (d2[0] > PIVOT_FLOOR * m[5][0])
    c2 = tuple(jnp.where(ok2, v, 0.0) for v in df_div(y2, d2))
    c1 = tuple(jnp.where(ok1, v, 0.0) for v in df_div(y1, d1))
    c1 = df_sub(c1, df_mul(l21, c2))
    c0 = df_sub(df_sub(df_div(m[0], m[1]), df_mul(l10, c1)), df_mul(l20, c2))
    return c0[0], c1[0], c2[0]


def row_total(rows):
    s, e = two_sum(rows[0:8], rows[8:16])
    for step in (4, 2, 1):
        other = pltpu.roll(s, step, axis=0)
        e = e + pltpu.roll(e, step, axis=0)
        s, more = two_sum(s, other)
        e = e + more
    return s, e


def kernel(
    vel, coef, enth, void, cells, normal, flag,
    vel_out, p_out, h_out,
    field, tz, tlo, thi, cx, cy, czm, czp, av, wc, wn, wf, hot_row, hot_lane, grid,
    ho, po, vo, reduce, load_sem, store_sem, send_sem, recv_sem, sum_send, sum_recv,
):
    gx, gy, gz = lax.axis_index("gx"), lax.axis_index("gy"), lax.axis_index("gz")
    chip_y, core = gy // 2, lax.rem(gy, 2)
    has = (gx > 0, gx < NGX - 1, gy > 0, gy < NGY - 1, gz > 0, gz < NGZ - 1)
    beside = (
        (gx - 1, gy, gz), (gx + 1, gy, gz), (gx, gy - 1, gz),
        (gx, gy + 1, gz), (gx, gy, gz - 1), (gx, gy, gz + 1),
    )

    def in_plane(i, j):
        return (lax.rem(gx + i, NGX), lax.rem(chip_y + j, NGY // 2) * 2 + core, gz)

    def in_column(k, j):
        return (gx, chip_y * 2 + lax.rem(core + j, 2), lax.rem(gz + k, NGZ))

    plane = [in_plane(i, j) for i in range(NGX) for j in range(NGY // 2) if i or j]
    column = [in_column(k, j) for k in range(NGZ) for j in range(2) if k or j]
    across = (gx, lax.rem(gy + NGY - 1 + 2 * core, NGY), gz)

    barrier = pltpu.get_barrier_semaphore()
    partners = plane + column + [across]
    for partner in partners:
        pl.semaphore_signal(barrier, inc=1, device_id=partner, device_id_type=MESH)

    inner = (pl.ds(2, BX), pl.ds(8, BY))
    loads = [
        (cells, wc), (flag, wf), (normal, wn),
        (vel.at[0], field.at[(U0,) + inner]),
        (vel.at[pl.ds(1, 2)], field.at[(pl.ds(U1, 2),) + inner]),
        (coef, field.at[(C,) + inner]),
        (enth, field.at[(H,) + inner]),
        (void, av),
    ]
    loads = [pltpu.make_async_copy(s, d, load_sem.at[i]) for i, (s, d) in enumerate(loads)]
    for copy in loads:
        copy.start()

    blank = jnp.zeros((BY, BZ), jnp.float32)
    tile = jnp.zeros((8, BZ), jnp.float32)

    @pl.when(jnp.logical_not(has[0]))
    def _():
        for f in (U0, H, C, W0, W1, W2):
            field[f, 1, ROWS, :] = blank

    @pl.when(jnp.logical_not(has[1]))
    def _():
        for f in (U0, H, C, W0, W1, W2):
            field[f, 10, ROWS, :] = blank

    @pl.when(jnp.logical_not(has[2]))
    def _():
        for f in (H, C, U1, W0, W1, W2):
            for x in range(BX):
                field[f, x + 2, 7:8, :] = tile[0:1]

    @pl.when(jnp.logical_not(has[3]))
    def _():
        for f in (H, C, U1, W0, W1, W2):
            for x in range(BX):
                field[f, x + 2, 40:41, :] = tile[0:1]

    @pl.when(jnp.logical_not(has[4]))
    def _():
        for f in range(6):
            tlo[f] = tile

    @pl.when(jnp.logical_not(has[5]))
    def _():
        for f in range(6):
            thi[f] = tile

    lane8 = lax.broadcasted_iota(jnp.int32, (8, BZ), 1)
    lane32 = lax.broadcasted_iota(jnp.int32, (BY, BZ), 1)
    first, last = lane32 == 0, lane32 == BZ - 1

    def exchange(e, moves):
        copies = []
        for side, (src, dst) in enumerate(moves):
            copy = pltpu.make_async_remote_copy(
                src_ref=src, dst_ref=dst, send_sem=send_sem.at[e, side],
                recv_sem=recv_sem.at[e, side], device_id=beside[side], device_id_type=MESH,
            )
            pl.when(has[side])(copy.start)
            copies.append(copy)
        return copies

    def receive(copies):
        for side, copy in enumerate(copies):
            pl.when(has[side ^ 1])(copy.wait_recv)

    def moves_of(fx, fy, t):
        rows = pl.ds(8, BY)
        planes = pl.ds(2, BX)
        return (
            (field.at[fx, 2, rows], field.at[fx, 10, rows]),
            (field.at[fx, 9, rows], field.at[fx, 1, rows]),
            (field.at[fy, planes, 8], field.at[fy, planes, 40]),
            (field.at[fy, planes, 39], field.at[fy, planes, 7]),
            (tz.at[t], thi.at[t]),
            (tz.at[t], tlo.at[t]),
        )

    def pack(values, acc, x):
        for b in range(4):
            k = 4 * x + b
            turned = pltpu.roll(values[8 * b : 8 * b + 8], (4 * k + 2) % BZ, axis=1)
            acc = turned if acc is None else jnp.where(lane8 // 4 == k, turned, acc)
        return acc

    def joined(t):
        low = pltpu.roll(tlo[t], 1, axis=1)
        high = pltpu.roll(thi[t], BZ - 1, axis=1)
        return jnp.where(lane8 % 4 == 1, high, low)

    def around_z(values, halo, x):
        ends = jnp.concatenate(
            [pltpu.roll(halo, (2 * BZ - 4 * (4 * x + b) - 2) % BZ, axis=1) for b in range(4)], axis=0
        )
        after = jnp.where(last, ends, pltpu.roll(values, BZ - 1, axis=1))
        before = jnp.where(first, ends, pltpu.roll(values, 1, axis=1))
        return after, before

    def around_y(f, x):
        return field[f, x + 2, 9:41, :], field[f, x + 2, 7:39, :]

    def centre(f, x):
        return field[f, x + 2, ROWS, :]

    for copy in loads[0:3]:
        copy.wait()
    where = wc[...]
    row_of = where // BZ
    lane_of = where - row_of * BZ
    code = jnp.where(wf[...] > 0, wf[...] + 4 * (wn[...] // 2), 0).astype(jnp.float32)
    up256 = lax.broadcasted_iota(jnp.int32, (BX * BY, BZ), 0)
    up128 = lax.broadcasted_iota(jnp.int32, (BZ, BZ), 0)
    for s in range(SLOTS):
        hot_row[:, s * BZ : (s + 1) * BZ] = jnp.where(up256 == row_of[s : s + 1], 1.0, 0.0).astype(jnp.bfloat16)
        hot_lane[:, s * BZ : (s + 1) * BZ] = jnp.where(up128 == lane_of[s : s + 1], code[s : s + 1], 0.0).astype(jnp.bfloat16)

    for copy in loads[3:7]:
        copy.wait()
    t_u2 = t_h = t_c = None
    for x in range(BX):
        t_u2 = pack(centre(U2, x), t_u2, x)
        t_h = pack(centre(H, x), t_h, x)
        t_c = pack(centre(C, x), t_c, x)
    tz[TZ_U2] = t_u2
    tz[TZ_H] = t_h
    tz[TZ_C] = t_c
    pl.semaphore_wait(barrier, len(partners))
    ex0 = exchange(0, moves_of(pl.ds(U0, 3), pl.ds(H, 3), pl.ds(0, 3)))

    grid[...] = lax.dot_general(
        hot_row[...], hot_lane[...], (((1,), (1,)), ((), ())), preferred_element_type=jnp.float32
    )
    loads[7].wait()
    for x in range(BX):
        a = av[x]
        g = grid[x * BY : (x + 1) * BY, :]
        not_x = g > 3.5
        is_z = g > 7.5
        s = g - jnp.where(not_x, 4.0, 0.0) - jnp.where(is_z, 4.0, 0.0)
        u0, u1, u2 = centre(U0, x), centre(U1, x), centre(U2, x)
        parallel = (
            jnp.where(not_x, u0 * u0, 0.0)
            + jnp.where(not_x & jnp.logical_not(is_z), 0.0, u1 * u1)
            + jnp.where(is_z, 0.0, u2 * u2)
        )
        speed = jnp.sqrt(parallel + 0.25)
        liquid = 1.0 - a
        evap = 1.5 * a * s * s
        root = jnp.where(s > 1.5, 2.0 * 1.4142135623730951, s)
        heat = liquid * speed * s + 0.6 * liquid * root + evap
        vo[0, x] = heat
        vo[1, x] = evap

    receive(ex0)
    zu, zh, zc = joined(TZ_U2), joined(TZ_H), joined(TZ_C)
    tb = None
    for x in range(BX):
        u2p, u2m = around_z(centre(U2, x), zu, x)
        u1p, u1m = around_y(U1, x)
        u0p, u0m = field[U0, x + 3, ROWS, :], field[U0, x + 1, ROWS, :]
        diverge = 0.5 * (u0p - u0m + (u1p - u1m) + (u2p - u2m))
        b = EXPANSION * (0.5 * vo[1, x]) - diverge
        field[W0, x + 2, ROWS, :] = b
        tb = pack(b, tb, x)
    tz[TZ_W0] = tb
    ex1 = exchange(1, moves_of(W0, W0, TZ_W0))

    half = 0.5 / SCALE
    for x in range(BX):
        c = centre(C, x)
        if x == 0:
            cx[0] = half * (c + field[C, 1, ROWS, :])
        cx[x + 1] = half * (c + field[C, x + 3, ROWS, :])
        after, before = around_y(C, x)
        cy[x, 0:32] = half * (c + before)
        cy[x, 32:33] = half * (c[31:32] + after[31:32])
        after, before = around_z(c, zc, x)
        czp[x] = half * (c + after)
        czm[x] = half * (c + before)
        h = centre(H, x)
        hyp, hym = around_y(H, x)
        hzp, hzm = around_z(h, zh, x)
        laplace = field[H, x + 3, ROWS, :] + field[H, x + 1, ROWS, :] + hyp + hym + hzp + hzm - 6.0 * h
        ho[x] = h + DIFFUSE * laplace + HEATING * vo[0, x]
    store_h = pltpu.make_async_copy(ho, h_out, store_sem.at[0])
    store_h.start()

    def fold(v):
        return (v[0:8] + v[8:16]) + (v[16:24] + v[24:32])

    def plus(acc, v):
        v = fold(v)
        return v if acc is None else acc + v

    def operator(f, t, x, halo):
        v = centre(f, x)
        yp, ym = around_y(f, x)
        zp, zm = around_z(v, halo, x)
        out = cx[x + 1] * (v - field[f, x + 3, ROWS, :]) + cx[x] * (v - field[f, x + 1, ROWS, :])
        out = out + (cy[x, 1:33] * (v - yp) + cy[x, 0:32] * (v - ym))
        out = out + (czp[x] * (v - zp) + czm[x] * (v - zm))
        return v, out

    m = [None] * 6
    receive(ex1)
    z0 = joined(TZ_W0)
    tb = None
    for x in range(BX):
        v, out = operator(W0, TZ_W0, x, z0)
        field[W1, x + 2, ROWS, :] = out
        tb = pack(out, tb, x)
    tz[TZ_W1] = tb
    ex2 = exchange(2, moves_of(W1, W1, TZ_W1))
    for x in range(BX):
        v, out = centre(W0, x), centre(W1, x)
        m[0], m[1], m[2] = plus(m[0], v * v), plus(m[1], v * out), plus(m[2], out * out)
    receive(ex2)
    z1 = joined(TZ_W1)
    tb = None
    for x in range(BX):
        v, out = operator(W1, TZ_W1, x, z1)
        field[W2, x + 2, ROWS, :] = out
        tb = pack(out, tb, x)
    tz[TZ_W2] = tb
    ex3 = exchange(3, moves_of(W2, W2, TZ_W2))
    for x in range(BX):
        v, out = centre(W1, x), centre(W2, x)
        m[3], m[4] = plus(m[3], v * out), plus(m[4], out * out)
    receive(ex3)
    z2 = joined(TZ_W2)
    for x in range(BX):
        v, out = operator(W2, TZ_W2, x, z2)
        m[5] = plus(m[5], v * out)

    row = jnp.zeros((1, BZ), jnp.float32)
    for i in range(6):
        row = jnp.where(lane8[0:1] == i, jnp.sum(m[i], keepdims=True), row)

    def all_sum(phase, row, group):
        reduce[phase, 0:1, :] = row
        copies = []
        for slot, partner in enumerate(group):
            copy = pltpu.make_async_remote_copy(
                src_ref=reduce.at[phase, pl.ds(0, 1)], dst_ref=reduce.at[phase, pl.ds(slot + 1, 1)],
                send_sem=sum_send.at[phase, slot], recv_sem=sum_recv.at[phase, slot],
                device_id=partner, device_id_type=MESH,
            )
            copy.start()
            copies.append(copy)
        for copy in copies:
            copy.wait_recv()
        return copies, row_total(reduce[phase])

    sums0, (high, low) = all_sum(0, row, plane)
    row = jnp.where(lane8 < 8, high, pltpu.roll(low, 8, axis=1))[0:1]
    sums1, (high, low) = all_sum(1, row, column)
    for copies in (ex0, ex1, ex2, ex3):
        for side, copy in enumerate(copies):
            pl.when(has[side])(copy.wait_send)
    low = low + pltpu.roll(high, BZ - 8, axis=1)
    moments = [quick_sum(high[0:1, i : i + 1], low[0:1, i : i + 1]) for i in range(6)]
    c0, c1, c2 = (v * (1.0 / SCALE) for v in solve_moments(moments))

    def mix(a, b, c):
        return c0 * a + c1 * b + c2 * c

    def pressure(planes, rows):
        return mix(field[W0, planes, rows, :], field[W1, planes, rows, :], field[W2, planes, rows, :])

    for x in range(-1, BX + 1):
        field[H, x + 2, ROWS, :] = pressure(x + 2, ROWS)
    for x in range(BX):
        for y in (7, 40):
            field[H, x + 2, y : y + 1, :] = pressure(x + 2, slice(y, y + 1))
        po[x] = centre(H, x)
    store_p = pltpu.make_async_copy(po, p_out, store_sem.at[1])
    store_p.start()
    zp = mix(z0, z1, z2)
    for x in range(BX):
        c = 0.5 * centre(C, x)
        after, before = around_y(H, x)
        vo[1, x] = centre(U1, x) - c * (after - before)
        after, before = around_z(centre(H, x), zp, x)
        vo[2, x] = centre(U2, x) - c * (after - before)
        vo[0, x] = centre(U0, x) - c * (field[H, x + 3, ROWS, :] - field[H, x + 1, ROWS, :])
    store_v = pltpu.make_async_copy(vo, vel_out, store_sem.at[2])
    store_v.start()
    for copy in sums0 + sums1:
        copy.wait_send()
    store_h.wait()
    store_p.wait()
    store_v.wait()


def shards(*args):
    block = (BX, BY, BZ)
    f32 = jnp.float32
    any_ref = pl.BlockSpec(memory_space=pl.ANY)
    return tuple(
        pl.pallas_call(
            kernel,
            out_shape=(
                jax.ShapeDtypeStruct((3,) + block, f32),
                jax.ShapeDtypeStruct(block, f32),
                jax.ShapeDtypeStruct(block, f32),
            ),
            in_specs=[any_ref] * 7,
            out_specs=(any_ref,) * 3,
            scratch_shapes=[
                pltpu.VMEM((8, BX + 4, BY + 16, BZ), f32),
                pltpu.VMEM((6, 8, BZ), f32),
                pltpu.VMEM((6, 8, BZ), f32),
                pltpu.VMEM((6, 8, BZ), f32),
                pltpu.VMEM((BX + 1, BY, BZ), f32),
                pltpu.VMEM((BX, BY + 8, BZ), f32),
                pltpu.VMEM(block, f32),
                pltpu.VMEM(block, f32),
                pltpu.VMEM(block, f32),
                pltpu.VMEM((SLOTS, BZ), jnp.int32),
                pltpu.VMEM((SLOTS, BZ), jnp.int32),
                pltpu.VMEM((SLOTS, BZ), jnp.int32),
                pltpu.VMEM((BX * BY, SLOTS * BZ), jnp.bfloat16),
                pltpu.VMEM((BZ, SLOTS * BZ), jnp.bfloat16),
                pltpu.VMEM((BX * BY, BZ), f32),
                pltpu.VMEM(block, f32),
                pltpu.VMEM(block, f32),
                pltpu.VMEM((3,) + block, f32),
                pltpu.VMEM((2, 16, BZ), f32),
                pltpu.SemaphoreType.DMA((8,)),
                pltpu.SemaphoreType.DMA((3,)),
                pltpu.SemaphoreType.DMA((4, 6)),
                pltpu.SemaphoreType.DMA((4, 6)),
                pltpu.SemaphoreType.DMA((2, 15)),
                pltpu.SemaphoreType.DMA((2, 15)),
            ],
            compiler_params=pltpu.CompilerParams(
                collective_id=0, has_side_effects=True, vmem_limit_bytes=24 * 1024 * 1024
            ),
            name="simple_step",
        )(*args)
    )


def solution(mesh):
    in_specs = (
        P(None, "gx", "gy", "gz"),
        P("gx", "gy", "gz"),
        P("gx", "gy", "gz"),
        P("gx", "gy", "gz"),
        P(("gx", "gy", "gz"), None),
        P(("gx", "gy", "gz"), None),
        P(("gx", "gy", "gz"), None),
    )
    out_specs = (P(None, "gx", "gy", "gz"), P("gx", "gy", "gz"), P("gx", "gy", "gz"))
    return jax.shard_map(shards, mesh=mesh, in_specs=in_specs, out_specs=out_specs, check_vma=False)
```

```python
import jax
import jax.numpy as jnp
from jax import lax
from jax.experimental import pallas as pl
from jax.experimental.pallas import tpu as pltpu
from jax.sharding import PartitionSpec as P

MESH = pl.DeviceIdType.MESH
NGX, NGY, NGZ = 4, 8, 8
BX, BY, BZ = 8, 32, 128
SLOTS = 16
DIFFUSE = 0.1
HEATING = 0.5
EXPANSION = 1.5
SCALE = 16.0
H, C, U0, U1, U2, BP, W0, W1, W2 = range(9)
FIELDS = 9
TU0, TC, TU2, TU1, TH, TB, TW = range(7)
ROWS = slice(8, 40)
SIGNS = (-1, 1)
XZ = tuple((a, 0, c) for a in SIGNS for c in SIGNS)
YZ = tuple((0, b, c) for b in SIGNS for c in SIGNS)
XY = tuple((a, b, 0) for a in SIGNS for b in SIGNS)
SIDES = ((-1, 0, 0), (1, 0, 0), (0, -1, 0), (0, 1, 0), (0, 0, -1), (0, 0, 1)) + XY + XZ + YZ
EARLY, LATE, ENTH, IMAGE = range(4)
PIVOT_FLOOR = 1e-9


def two_sum(a, b):
    s = a + b
    t = s - a
    return s, (a - (s - t)) + (b - t)


def quick_sum(a, b):
    s = a + b
    return s, b - (s - a)


def split(a):
    t = 4097.0 * a
    high = t - (t - a)
    return high, a - high


def two_mul(a, b):
    p = a * b
    ah, al = split(a)
    bh, bl = split(b)
    return p, ((ah * bh - p) + ah * bl + al * bh) + al * bl


def df_sub(a, b):
    s, e = two_sum(a[0], -b[0])
    return quick_sum(s, e + (a[1] - b[1]))


def df_mul(a, b):
    p, e = two_mul(a[0], b[0])
    return quick_sum(p, e + (a[0] * b[1] + a[1] * b[0]))


def df_div(a, b):
    q = a[0] / b[0]
    p, e = two_mul(q, b[0])
    rest = ((a[0] - p) - e) + a[1] - q * b[1]
    return quick_sum(q, rest / b[0])


def solve_moments(m):
    l10 = df_div(m[2], m[1])
    l20 = df_div(m[3], m[1])
    d1 = df_sub(m[3], df_mul(l10, m[2]))
    e12 = df_sub(m[4], df_mul(l10, m[3]))
    y1 = df_sub(m[1], df_mul(l10, m[0]))
    y2 = df_sub(m[2], df_mul(l20, m[0]))
    d2 = df_sub(m[5], df_mul(l20, m[3]))
    ok1 = d1[0] > PIVOT_FLOOR * m[3][0]
    l21 = df_div(e12, d1)
    l21 = tuple(jnp.where(ok1, v, 0.0) for v in l21)
    d2 = df_sub(d2, df_mul(l21, e12))
    y2 = df_sub(y2, df_mul(l21, y1))
    ok2 = ok1 & (d2[0] > PIVOT_FLOOR * m[5][0])
    c2 = tuple(jnp.where(ok2, v, 0.0) for v in df_div(y2, d2))
    c1 = tuple(jnp.where(ok1, v, 0.0) for v in df_div(y1, d1))
    c1 = df_sub(c1, df_mul(l21, c2))
    c0 = df_sub(df_sub(df_div(m[0], m[1]), df_mul(l10, c1)), df_mul(l20, c2))
    return c0[0], c1[0], c2[0]


def row_total(rows):
    s, e = two_sum(rows[0:8], rows[8:16])
    for step in (4, 2, 1):
        other = pltpu.roll(s, step, axis=0)
        e = e + pltpu.roll(e, step, axis=0)
        s, more = two_sum(s, other)
        e = e + more
    return s, e


def opposite(side):
    return tuple(-v for v in side)


def messages(field, tz, tlo, thi, dz):
    xs, xd = {-1: 2, 1: 9}, {-1: 10, 1: 1}
    ys, yd = {-1: 8, 1: 39}, {-1: 40, 1: 7}
    xs2, xd2 = {-1: pl.ds(2, 2), 1: pl.ds(8, 2)}, {-1: pl.ds(10, 2), 1: pl.ds(0, 2)}
    ys2, yd2 = {-1: pl.ds(8, 2), 1: pl.ds(38, 2)}, {-1: pl.ds(40, 2), 1: pl.ds(6, 2)}
    rows, planes = pl.ds(8, BY), pl.ds(2, BX)
    table = [{}, {}, {}, {}]
    for side in SIDES:
        a, b, c = side
        far = thi if c < 0 else tlo
        slot = (XZ + YZ).index(opposite(side)) if side in XZ + YZ else None
        if side in XZ:
            early = [(tz.at[pl.ds(TU0, 3)], dz.at[slot, pl.ds(0, 3)])]
            image = [(tz.at[TW], dz.at[slot, 3])]
            late = enth = []
        elif side in YZ:
            early = [(tz.at[pl.ds(TC, 3)], dz.at[slot, pl.ds(0, 3)])]
            image = [(tz.at[TW], dz.at[slot, 3])]
            late = enth = []
        elif side in XY:
            early = [(field.at[pl.ds(C, 3), xs[a], ys[b]], field.at[pl.ds(C, 3), xd[a], yd[b]])]
            image = [(field.at[W1, xs[a], ys[b]], field.at[W1, xd[a], yd[b]])]
            late = enth = []
        elif a:
            early = [
                (field.at[C, xs2[a], rows], field.at[C, xd2[a], rows]),
                (field.at[U0, xs[a], rows], field.at[U0, xd[a], rows]),
            ]
            late = [(field.at[BP, xs[a], rows], field.at[BP, xd[a], rows])]
            enth = [(field.at[H, xs[a], rows], field.at[H, xd[a], rows])]
            image = [(field.at[W1, xs2[a], rows], field.at[W1, xd2[a], rows])]
        elif b:
            early = [
                (field.at[C, planes, ys2[b]], field.at[C, planes, yd2[b]]),
                (field.at[U1, planes, ys[b]], field.at[U1, planes, yd[b]]),
            ]
            late = [(field.at[BP, planes, ys[b]], field.at[BP, planes, yd[b]])]
            enth = [(field.at[H, planes, ys[b]], field.at[H, planes, yd[b]])]
            image = [(field.at[W1, planes, ys2[b]], field.at[W1, planes, yd2[b]])]
        else:
            early = [(tz.at[pl.ds(TC, 2)], far.at[pl.ds(TC, 2)])]
            late = [(tz.at[TB], far.at[TB])]
            enth = [(tz.at[TH], far.at[TH])]
            image = [(tz.at[TW], far.at[TW])]
        for kind, pairs in ((EARLY, early), (LATE, late), (ENTH, enth), (IMAGE, image)):
            table[kind][side] = pairs
    return table


N_MESSAGES = 22 + 6 + 6 + 18


def kernel(
    vel, coef, enth, void, cells, normal, flag,
    w_out, g_out, u_out, h_out, c_out,
    field, tz, tlo, thi, dz, cx, cy, czm, czp, zlow, av, wc, wn, wf, hot_row, hot_lane, grid,
    heat, reduce, load_sem, copy_sem, send_sem, recv_sem, sum_send, sum_recv,
):
    gx, gy, gz = lax.axis_index("gx"), lax.axis_index("gy"), lax.axis_index("gz")
    chip_y, core = gy // 2, lax.rem(gy, 2)

    def exists(side):
        found = None
        for at, step, size in zip((gx, gy, gz), side, (NGX, NGY, NGZ)):
            if step:
                inside = at > 0 if step < 0 else at < size - 1
                found = inside if found is None else found & inside
        return found

    has = {side: exists(side) for side in SIDES}

    def in_plane(i, j):
        return (lax.rem(gx + i, NGX), lax.rem(chip_y + j, NGY // 2) * 2 + core, gz)

    def in_column(k, j):
        return (gx, chip_y * 2 + lax.rem(core + j, 2), lax.rem(gz + k, NGZ))

    def far_first(pairs, n, m):
        return sorted(pairs, key=lambda p: -min(p[0], n - p[0]) - min(p[1], m - p[1]))

    plane = [in_plane(i, j) for i, j in far_first([(i, j) for i in range(NGX) for j in range(NGY // 2) if i or j], NGX, NGY // 2)]
    column = [in_column(k, j) for k, j in far_first([(k, j) for k in range(NGZ) for j in range(2) if k or j], NGZ, 2)]

    inner = (pl.ds(2, BX), pl.ds(8, BY))
    loads = [
        (cells, wc), (flag, wf), (normal, wn),
        (vel, field.at[(pl.ds(U0, 3),) + inner]),
        (void, av),
        (coef, field.at[(C,) + inner]),
        (enth, field.at[(H,) + inner]),
    ]
    loads = [pltpu.make_async_copy(s, d, load_sem.at[i]) for i, (s, d) in enumerate(loads)]
    for copy in loads:
        copy.start()

    barrier = pltpu.get_barrier_semaphore()
    for partner in column + plane:
        pl.semaphore_signal(barrier, inc=1, device_id=partner, device_id_type=MESH)
    expected = len(plane) + len(column)
    for side in SIDES:
        a, b, c = side
        if (a and not b and not c) or (c and not a and not b):
            continue
        met = has[side]
        if b and not a:
            met = met & (core == (0 if b < 0 else 1))

        @pl.when(met)
        def _():
            pl.semaphore_signal(barrier, inc=1, device_id=(gx + a, gy + b, gz + c), device_id_type=MESH)

        expected = expected + met.astype(jnp.int32)

    table = messages(field, tz, tlo, thi, dz)
    copies = [{}, {}, {}, {}]
    at = 0
    for kind in range(4):
        for side in SIDES:
            copies[kind][side] = []
            for src, dst in table[kind][side]:
                copies[kind][side].append(
                    pltpu.make_async_remote_copy(
                        src_ref=src, dst_ref=dst, send_sem=send_sem.at[at], recv_sem=recv_sem.at[at],
                        device_id=(gx + side[0], gy + side[1], gz + side[2]), device_id_type=MESH,
                    )
                )
                at += 1

    def send(kind, sides):
        for side in sides:
            if copies[kind][side]:

                @pl.when(has[side])
                def _():
                    for copy in copies[kind][side]:
                        copy.start()

    def receive(kind):
        for side in SIDES:
            if copies[kind][side]:

                @pl.when(has[opposite(side)])
                def _():
                    for copy in copies[kind][side]:
                        copy.wait_recv()

    for side in SIDES:

        @pl.when(jnp.logical_not(has[opposite(side)]))
        def _():
            for kind in range(4):
                for _, dst in table[kind][side]:
                    dst[...] = jnp.zeros(dst.shape, jnp.float32)

    lane8 = lax.broadcasted_iota(jnp.int32, (8, BZ), 1)
    sub8 = lax.broadcasted_iota(jnp.int32, (8, BZ), 0)
    lane32 = lax.broadcasted_iota(jnp.int32, (BY, BZ), 1)
    row32 = lax.broadcasted_iota(jnp.int32, (BY, BZ), 0)
    first, last = lane32 == 0, lane32 == BZ - 1
    first8, last8 = lane8 == 0, lane8 == BZ - 1
    place = lane8 % 4
    low_lane = place == 1
    y_group = lane8 // 4 % 4
    ends_half = jnp.where(first8, 0.5, jnp.where(last8, -0.5, 0.0))
    ends_half32 = jnp.where(first, 0.5, jnp.where(last, -0.5, 0.0))

    def turn(v, by, axis=1):
        size = v.shape[axis]
        return pltpu.roll(v, by % size, axis=axis) if by % size else v

    def pack(values, acc, x):
        for b in range(4):
            k = 4 * x + b
            turned = turn(values[8 * b : 8 * b + 8], 4 * k + 2)
            acc = turned if acc is None else jnp.where(lane8 // 4 == k, turned, acc)
        return acc

    def pair(low, high):
        return jnp.where(low_lane, low, high)

    def swap(v):
        return jnp.where(low_lane, turn(v, -1), turn(v, 1))

    def ends(swapped, x):
        return jnp.concatenate([turn(swapped, -4 * (4 * x + b) - 2) for b in range(4)], axis=0)

    def ends_row(swapped, b):
        row, k = (7, 3) if b < 0 else (0, 0)
        out = None
        spread = jnp.broadcast_to(swapped[row : row + 1], (8, BZ))
        for x in range(BX):
            turned = turn(spread, -4 * (4 * x + k) - 2)
            out = turned if out is None else jnp.where(sub8 == x, turned, out)
        return out

    def around_z(v, e):
        f, l = (first, last) if v.shape[0] == BY else (first8, last8)
        return jnp.where(l, e, turn(v, -1)), jnp.where(f, e, turn(v, 1))

    def around_y(f, x):
        return field[f, x + 2, 9:41, :], field[f, x + 2, 7:39, :]

    def centre(f, x):
        return field[f, x + 2, ROWS, :]

    def row_of_field(f, r):
        return field[f, 2:10, r, :]

    def diagonal(side, q):
        a, b, _ = side
        lo, hi = ((XZ + YZ).index((a, b, c)) for c in SIGNS)
        return pair(dz[lo, q], dz[hi, q])

    xm_side, xp_side, ym_side, yp_side, zm_side, zp_side = SIDES[:6]

    for copy in loads[0:3]:
        copy.wait()
    where = wc[...]
    row_at = where // BZ
    lane_at = where - row_at * BZ
    code = jnp.where(wf[...] > 0, wf[...] + 4 * (wn[...] // 2), 0).astype(jnp.float32)
    up256 = lax.broadcasted_iota(jnp.int32, (BX * BY, BZ), 0)
    up128 = lax.broadcasted_iota(jnp.int32, (BZ, BZ), 0)
    for s in range(SLOTS):
        hot_row[:, s * BZ : (s + 1) * BZ] = jnp.where(up256 == row_at[s : s + 1], 1.0, 0.0).astype(jnp.bfloat16)
        hot_lane[:, s * BZ : (s + 1) * BZ] = jnp.where(up128 == lane_at[s : s + 1], code[s : s + 1], 0.0).astype(jnp.bfloat16)
    grid[...] = lax.dot_general(
        hot_row[...], hot_lane[...], (((1,), (1,)), ((), ())), preferred_element_type=jnp.float32
    )
    for copy in loads[3:]:
        copy.wait()

    t_b = t_c = t_u0 = t_u1 = t_u2 = None
    for x in range(BX):
        a = av[x]
        g = grid[x * BY : (x + 1) * BY, :]
        not_x = g > 3.5
        is_z = g > 7.5
        s = g - jnp.where(not_x, 4.0, 0.0) - jnp.where(is_z, 4.0, 0.0)
        u0, u1, u2 = centre(U0, x), centre(U1, x), centre(U2, x)
        parallel = (
            jnp.where(not_x, u0 * u0, 0.0)
            + jnp.where(not_x & jnp.logical_not(is_z), 0.0, u1 * u1)
            + jnp.where(is_z, 0.0, u2 * u2)
        )
        speed = jnp.sqrt(parallel + 0.25)
        liquid = 1.0 - a
        evap = 1.5 * a * s * s
        root = jnp.where(s > 1.5, 2.0 * 1.4142135623730951, s)
        heat[x] = liquid * speed * s + 0.6 * liquid * root + evap
        slope = jnp.where(row32 == BY - 1, 0.0, turn(u1, -1, 0)) - jnp.where(row32 == 0, 0.0, turn(u1, 1, 0))
        slope = slope + (jnp.where(last, 0.0, turn(u2, -1)) - jnp.where(first, 0.0, turn(u2, 1)))
        if x < BX - 1:
            slope = slope + centre(U0, x + 1)
        if x > 0:
            slope = slope - centre(U0, x - 1)
        b = EXPANSION * (0.5 * evap) - 0.5 * slope
        field[BP, x + 2, ROWS, :] = b
        t_b = pack(b, t_b, x)
        t_c = pack(centre(C, x), t_c, x)
        t_u0 = pack(u0, t_u0, x)
        t_u1 = pack(u1, t_u1, x)
        t_u2 = pack(u2, t_u2, x)
    for i, t in ((TB, t_b), (TC, t_c), (TU0, t_u0), (TU1, t_u1), (TU2, t_u2)):
        tz[i] = t

    pl.semaphore_wait(barrier, expected)
    send(EARLY, XZ + YZ + XY)
    send(EARLY, SIDES[:6])
    send(LATE, SIDES[:6])

    t_h = None
    half = 0.5 / SCALE
    for x in range(BX):
        t_h = pack(centre(H, x), t_h, x)
        c = centre(C, x)
        if x < BX - 1:
            cx[x + 2] = half * (c + centre(C, x + 1))
        cy[x + 1, 0:32] = half * (c + turn(c, 1, 0))
        czp[x + 1] = half * jnp.where(last, c, c + turn(c, -1))
        czm[x + 1] = half * jnp.where(first, c, c + turn(c, 1))
    tz[TH] = t_h
    send(ENTH, SIDES[:6])

    def low_high(v):
        return v[0:8], v[8:24], v[24:32]

    def y_ends(v, f, x):
        a, m, z = low_high(v)
        a = a + jnp.where(sub8 == 0, 0.5 * field[f, x + 2, 7:8, :], 0.0)
        z = z - jnp.where(sub8 == 7, 0.5 * field[f, x + 2, 40:41, :], 0.0)
        return jnp.concatenate([a, m, z], axis=0)

    receive(EARLY)
    receive(LATE)
    s_u2 = swap(pair(tlo[TU2], thi[TU2]))
    s_c = swap(pair(tlo[TC], thi[TC]))
    for x in range(BX):
        b = centre(BP, x) + ends_half32 * ends(s_u2, x)
        b = y_ends(b, U1, x)
        if x == 0:
            b = b + 0.5 * field[U0, 1, ROWS, :]
        if x == BX - 1:
            b = b - 0.5 * field[U0, 10, ROWS, :]
        field[W0, x + 2, ROWS, :] = b
        c = centre(C, x)
        e = ends(s_c, x)
        czp[x + 1] = czp[x + 1] + jnp.where(last, half * e, 0.0)
        czm[x + 1] = czm[x + 1] + jnp.where(first, half * e, 0.0)
        cy[x + 1, 0:1] = half * (c[0:1] + field[C, x + 2, 7:8, :])
        cy[x + 1, 32:33] = half * (c[31:32] + field[C, x + 2, 40:41, :])
    cx[1] = half * (centre(C, 0) + centre(C, -1))
    cx[9] = half * (centre(C, 7) + centre(C, 8))
    for x, own, sign, side, inside in ((-1, 0, -0.5, xm_side, 7), (BX, BX - 1, 0.5, xp_side, 0)):
        b = centre(BP, x) + sign * centre(U0, own)
        b = y_ends(b, U1, x) + ends_half32 * ends(swap(diagonal(side, 2)), inside)
        field[W0, x + 2, ROWS, :] = jnp.where(has[side], b, 0.0)
    for r, own, sign, side in ((7, 8, -0.5, ym_side), (40, 39, 0.5, yp_side)):
        b = row_of_field(BP, r) + sign * row_of_field(U1, own)
        b = b + jnp.where(sub8 == 0, 0.5 * field[U0, 1, r : r + 1, :], 0.0)
        b = b - jnp.where(sub8 == 7, 0.5 * field[U0, 10, r : r + 1, :], 0.0)
        b = b + ends_half * ends_row(swap(diagonal(side, 1)), side[1])
        b = jnp.where(has[side], b, 0.0)
        for x in range(BX):
            field[W0, x + 2, r : r + 1, :] = b[x : x + 1]
    has_z = jnp.where(low_lane, has[zm_side].astype(jnp.float32), has[zp_side].astype(jnp.float32))

    def z_inside(t):
        return jnp.where(low_lane, turn(t, -1), turn(t, 1))

    def z_around_x(v, before, after):
        return (
            jnp.where(lane8 >= 112, turn(after, -16), turn(v, -16)),
            jnp.where(lane8 < 16, turn(before, 16), turn(v, 16)),
        )

    def z_around_y(v, before, after):
        up = jnp.where(y_group == 3, turn(after, 12), turn(v, -4))
        down = jnp.where(y_group == 0, turn(before, -12), turn(v, 4))
        return (
            turn(jnp.where(sub8 == 0, up, v), -1, 0),
            turn(jnp.where(sub8 == 7, down, v), 1, 0),
        )

    zero = jnp.zeros((8, BZ), jnp.float32)
    after, before = z_around_x(zero, diagonal(xm_side, 0), diagonal(xp_side, 0))
    b = pair(tlo[TB], thi[TB]) - 0.5 * (after - before)
    after, before = z_around_y(zero, diagonal(ym_side, 2), diagonal(yp_side, 2))
    b = b - 0.5 * (after - before) + jnp.where(low_lane, -0.5, 0.5) * z_inside(tz[TU2])
    s_w0 = swap(has_z * b)

    def operator(f, x, e):
        v = centre(f, x)
        yp, ym = around_y(f, x)
        zp, zm = around_z(v, e)
        out = cx[x + 2] * (v - centre(f, x + 1)) + cx[x + 1] * (v - centre(f, x - 1))
        out = out + (cy[x + 1, 1:33] * (v - yp) + cy[x + 1, 0:32] * (v - ym))
        return out + (czp[x + 1] * (v - zp) + czm[x + 1] * (v - zm))

    t_w = None
    for x in range(BX):
        out = operator(W0, x, ends(s_w0, x))
        field[W1, x + 2, ROWS, :] = out
        t_w = pack(out, t_w, x)
    tz[TW] = t_w
    send(IMAGE, XZ + YZ + XY)
    send(IMAGE, SIDES[:6])

    def fold(v):
        return (v[0:8] + v[8:16]) + (v[16:24] + v[24:32])

    def plus(acc, v):
        v = fold(v)
        return v if acc is None else acc + v

    m = [None] * 6
    for x in range(BX):
        v, out = centre(W0, x), centre(W1, x)
        m[0], m[1], m[2] = plus(m[0], v * v), plus(m[1], v * out), plus(m[2], out * out)
    for x, side, inside in ((-1, xm_side, 7), (BX, xp_side, 0)):
        c = centre(C, x)
        if x < 0:
            cx[0] = half * (c + centre(C, -2))
        else:
            cx[10] = half * (c + centre(C, 9))
        after, before = around_y(C, x)
        cy[x + 1, 0:32] = half * (c + before)
        cy[x + 1, 32:33] = half * (c[31:32] + after[31:32])
        after, before = around_z(c, ends(swap(diagonal(side, 1)), inside))
        czp[x + 1] = half * (c + after)
        czm[x + 1] = half * (c + before)
    z_edge = jnp.where(has[zm_side], 0.0, 1.0)
    y_edge = jnp.where(has[ym_side], 0.0, 1.0)
    x_edge = jnp.where(has[xm_side], 0.0, 1.0)
    for x in range(BX):
        low = jnp.where(first, czm[x + 1], 0.0) * z_edge
        low = low + jnp.where(row32 == 0, cy[x + 1, 0:32], 0.0) * y_edge
        if x == 0:
            low = low + cx[1] * x_edge
        zlow[x] = low

    receive(IMAGE)
    s_w1 = swap(pair(tlo[TW], thi[TW]))
    for x in range(BX):
        out = operator(W1, x, ends(s_w1, x))
        field[W2, x + 2, ROWS, :] = out
        v = centre(W1, x)
        m[3], m[4] = plus(m[3], v * out), plus(m[4], out * out)

    def image_plane(x, side, inside):
        out = operator(W1, x, ends(swap(diagonal(side, 3)), inside))
        field[W2, x + 2, ROWS, :] = jnp.where(has[side], out, 0.0)

    def image_row(r, beyond, own, side):
        sums = []
        c, v = row_of_field(C, r), row_of_field(W1, r)

        def term(cn, vn):
            return (c + cn) * (v - vn)

        out = term(row_of_field(C, beyond), row_of_field(W1, beyond)) + term(row_of_field(C, own), row_of_field(W1, own))
        both = []
        for f, q, values in ((C, 0, c), (W1, 3, v)):
            after = jnp.where(sub8 == 7, field[f, 10, r : r + 1, :], turn(values, -1, 0))
            before = jnp.where(sub8 == 0, field[f, 1, r : r + 1, :], turn(values, 1, 0))
            zp, zm = around_z(values, ends_row(swap(diagonal(side, q)), side[1]))
            both.append((after, before, zp, zm))
        for cn, vn in zip(*both):
            out = out + term(cn, vn)
        out = jnp.where(has[side], half * out, 0.0)
        for x in range(BX):
            field[W2, x + 2, r : r + 1, :] = out[x : x + 1]

    def image_face():
        both = []
        for t, qx, qy in ((TC, 1, 0), (TW, 3, 3)):
            lo, hi, own = tlo[t], thi[t], tz[t]
            v = pair(lo, hi)
            outer = jnp.where(low_lane, turn(lo, 1), turn(hi, -1))
            both.append(
                (v, outer, z_inside(own))
                + z_around_x(v, diagonal(xm_side, qx), diagonal(xp_side, qx))
                + z_around_y(v, diagonal(ym_side, qy), diagonal(yp_side, qy))
            )
        (c, *near_c), (v, *near_v) = both
        out = zero
        for cn, vn in zip(near_c, near_v):
            out = out + (c + cn) * (v - vn)
        return swap(has_z * (half * out))

    image_plane(BX, xp_side, 0)
    image_row(40, 41, 39, yp_side)
    s_w2 = image_face()
    for x in range(BX):
        v = centre(W2, x)
        dx = v - centre(W2, x + 1)
        dy = v - field[W2, x + 2, 9:41, :]
        dz_ = v - jnp.where(last, ends(s_w2, x), turn(v, -1))
        m[5] = plus(
            m[5],
            (cx[x + 2] * (dx * dx) + cy[x + 1, 1:33] * (dy * dy)) + (czp[x + 1] * (dz_ * dz_) + zlow[x] * (v * v)),
        )

    row = jnp.zeros((1, BZ), jnp.float32)
    for i in range(6):
        row = jnp.where(lane8[0:1] == i, jnp.sum(m[i], keepdims=True), row)

    def start_sum(phase, row, group):
        reduce[phase, 0:1, :] = row
        started = []
        for slot, partner in enumerate(group):
            copy = pltpu.make_async_remote_copy(
                src_ref=reduce.at[phase, pl.ds(0, 1)], dst_ref=reduce.at[phase, pl.ds(slot + 1, 1)],
                send_sem=sum_send.at[phase, slot], recv_sem=sum_recv.at[phase, slot],
                device_id=partner, device_id_type=MESH,
            )
            copy.start()
            started.append(copy)
        return started

    def end_sum(phase, started):
        for copy in started:
            copy.wait_recv()
        return row_total(reduce[phase])

    sums0 = start_sum(0, row, plane)
    image_plane(-1, xm_side, 7)
    image_row(7, 6, 8, ym_side)
    copy_u = pltpu.make_async_copy(field.at[(pl.ds(U0, 3),) + inner], u_out, copy_sem.at[0])
    copy_u.start()
    copy_w = pltpu.make_async_copy(field.at[(pl.ds(W0, 3),) + inner], w_out, copy_sem.at[1])
    copy_w.start()
    for i, (f, swapped) in enumerate(((W0, s_w0), (W1, s_w1), (W2, s_w2))):
        for x in range(BX):
            c = (0.5 / SCALE) * centre(C, x)
            g_out[i, 0, x] = c * (centre(f, x + 1) - centre(f, x - 1))
            after, before = around_y(f, x)
            g_out[i, 1, x] = c * (after - before)
            after, before = around_z(centre(f, x), ends(swapped, x))
            g_out[i, 2, x] = c * (after - before)
    receive(ENTH)
    s_h = swap(pair(tlo[TH], thi[TH]))
    for x in range(BX):
        h = centre(H, x)
        hyp, hym = around_y(H, x)
        hzp, hzm = around_z(h, ends(s_h, x))
        laplace = centre(H, x + 1) + centre(H, x - 1) + hyp + hym + hzp + hzm - 6.0 * h
        h_out[x] = h + DIFFUSE * laplace + HEATING * heat[x]
    copy_u.wait()
    copy_w.wait()
    for kind in range(4):
        for side in SIDES:
            if copies[kind][side]:

                @pl.when(has[side])
                def _():
                    for copy in copies[kind][side]:
                        copy.wait_send()

    high, low = end_sum(0, sums0)
    row = jnp.where(lane8 < 8, high, turn(low, 8))[0:1]
    sums1 = start_sum(1, row, column)
    high, low = end_sum(1, sums1)
    low = low + turn(high, -8)
    moments = [quick_sum(high[0:1, i : i + 1], low[0:1, i : i + 1]) for i in range(6)]
    for i, v in enumerate(solve_moments(moments)):
        c_out[i] = jnp.broadcast_to(v, (8, BZ))
    for copy in sums0 + sums1:
        copy.wait_send()


def finish(w, g, u, h, c, vel_out, p_out, h_out, vel, p, sem):
    copy_h = pltpu.make_async_copy(h, h_out, sem.at[0])
    copy_h.start()
    c0, c1, c2 = (jnp.concatenate([c[i]] * 4, axis=0) for i in range(3))
    copies = [copy_h]
    for i in range(3):
        for x in range(BX):
            vel[i, x] = u[i, x] - (c0 * g[0, i, x] + c1 * g[1, i, x] + c2 * g[2, i, x])
        copy = pltpu.make_async_copy(vel.at[i], vel_out.at[i], sem.at[1 + i])
        copy.start()
        copies.append(copy)
    scaled = tuple(v * (1.0 / SCALE) for v in (c0, c1, c2))
    for x in range(BX):
        p[x] = scaled[0] * w[0, x] + scaled[1] * w[1, x] + scaled[2] * w[2, x]
    copy_p = pltpu.make_async_copy(p, p_out, sem.at[4])
    copy_p.start()
    for copy in copies + [copy_p]:
        copy.wait()


def shards(*args):
    block = (BX, BY, BZ)
    f32 = jnp.float32
    any_ref = pl.BlockSpec(memory_space=pl.ANY)
    vmem = pl.BlockSpec(memory_space=pltpu.VMEM)
    results = pl.pallas_call(
        kernel,
        out_shape=(
            jax.ShapeDtypeStruct((3,) + block, f32),
            jax.ShapeDtypeStruct((3, 3) + block, f32),
            jax.ShapeDtypeStruct((3,) + block, f32),
            jax.ShapeDtypeStruct(block, f32),
            jax.ShapeDtypeStruct((3, 8, BZ), f32),
        ),
        in_specs=[any_ref] * 7,
        out_specs=(vmem,) * 5,
        scratch_shapes=[
            pltpu.VMEM((FIELDS, BX + 4, BY + 16, BZ), f32),
            pltpu.VMEM((7, 8, BZ), f32),
            pltpu.VMEM((7, 8, BZ), f32),
            pltpu.VMEM((7, 8, BZ), f32),
            pltpu.VMEM((8, 4, 8, BZ), f32),
            pltpu.VMEM((BX + 3, BY, BZ), f32),
            pltpu.VMEM((BX + 2, BY + 8, BZ), f32),
            pltpu.VMEM((BX + 2, BY, BZ), f32),
            pltpu.VMEM((BX + 2, BY, BZ), f32),
            pltpu.VMEM(block, f32),
            pltpu.VMEM(block, f32),
            pltpu.VMEM((SLOTS, BZ), jnp.int32),
            pltpu.VMEM((SLOTS, BZ), jnp.int32),
            pltpu.VMEM((SLOTS, BZ), jnp.int32),
            pltpu.VMEM((BX * BY, SLOTS * BZ), jnp.bfloat16),
            pltpu.VMEM((BZ, SLOTS * BZ), jnp.bfloat16),
            pltpu.VMEM((BX * BY, BZ), f32),
            pltpu.VMEM(block, f32),
            pltpu.VMEM((2, 16, BZ), f32),
            pltpu.SemaphoreType.DMA((7,)),
            pltpu.SemaphoreType.DMA((2,)),
            pltpu.SemaphoreType.DMA((N_MESSAGES,)),
            pltpu.SemaphoreType.DMA((N_MESSAGES,)),
            pltpu.SemaphoreType.DMA((2, 15)),
            pltpu.SemaphoreType.DMA((2, 15)),
        ],
        compiler_params=pltpu.CompilerParams(
            collective_id=0, has_side_effects=True, vmem_limit_bytes=32 * 1024 * 1024
        ),
        name="simple_step",
    )(*[pltpu.with_memory_space_constraint(a, pltpu.HBM) for a in args])
    results = [pltpu.with_memory_space_constraint(r, pltpu.VMEM) for r in results]
    return tuple(
        pl.pallas_call(
            finish,
            out_shape=(
                jax.ShapeDtypeStruct((3,) + block, f32),
                jax.ShapeDtypeStruct(block, f32),
                jax.ShapeDtypeStruct(block, f32),
            ),
            in_specs=[vmem] * 5,
            out_specs=(pl.BlockSpec(memory_space=pltpu.HBM),) * 3,
            scratch_shapes=[
                pltpu.VMEM((3,) + block, f32),
                pltpu.VMEM(block, f32),
                pltpu.SemaphoreType.DMA((5,)),
            ],
            compiler_params=pltpu.CompilerParams(vmem_limit_bytes=8 * 1024 * 1024),
            name="finish",
        )(*results)
    )


def solution(mesh):
    in_specs = (
        P(None, "gx", "gy", "gz"),
        P("gx", "gy", "gz"),
        P("gx", "gy", "gz"),
        P("gx", "gy", "gz"),
        P(("gx", "gy", "gz"), None),
        P(("gx", "gy", "gz"), None),
        P(("gx", "gy", "gz"), None),
    )
    out_specs = (P(None, "gx", "gy", "gz"), P("gx", "gy", "gz"), P("gx", "gy", "gz"))
    return jax.shard_map(shards, mesh=mesh, in_specs=in_specs, out_specs=out_specs, check_vma=False)
```

```python
import math

import jax
import jax.numpy as jnp
from jax import lax
from jax.experimental import pallas as pl
from jax.experimental.pallas import tpu as pltpu
from jax.sharding import PartitionSpec as P

MESH = pl.DeviceIdType.MESH
NGX, NGY, NGZ = 4, 8, 8
BX, BY, BZ = 8, 32, 128
SLOTS = 16
DIFFUSE = 0.1
HEATING = 0.5
EXPANSION = 1.5
SCALE = 16.0
H, C, U0, BP, U1, U2, W0, W1, W2 = range(9)
FIELDS = 9
TU0, TC, TU2, TB, TU1, TH, TW = range(7)
ROWS = slice(8, 40)
SIGNS = (-1, 1)
XZ = tuple((a, 0, c) for a in SIGNS for c in SIGNS)
YZ = tuple((0, b, c) for b in SIGNS for c in SIGNS)
XY = tuple((a, b, 0) for a in SIGNS for b in SIGNS)
SIDES = ((-1, 0, 0), (1, 0, 0), (0, -1, 0), (0, 1, 0), (0, 0, -1), (0, 0, 1)) + XY + XZ + YZ
FIRST, ENTH, IMAGE = range(3)
PIVOT_FLOOR = 1e-9


def two_sum(a, b):
    s = a + b
    t = s - a
    return s, (a - (s - t)) + (b - t)


def quick_sum(a, b):
    s = a + b
    return s, b - (s - a)


def split(a):
    t = 4097.0 * a
    high = t - (t - a)
    return high, a - high


def two_mul(a, b):
    p = a * b
    ah, al = split(a)
    bh, bl = split(b)
    return p, ((ah * bh - p) + ah * bl + al * bh) + al * bl


def df_sub(a, b):
    s, e = two_sum(a[0], -b[0])
    return quick_sum(s, e + (a[1] - b[1]))


def df_mul(a, b):
    p, e = two_mul(a[0], b[0])
    return quick_sum(p, e + (a[0] * b[1] + a[1] * b[0]))


def df_over(a, b, inverse):
    q = a[0] * inverse
    p, e = two_mul(q, b[0])
    rest = ((a[0] - p) - e) + (a[1] - q * b[1])
    return quick_sum(q, rest * inverse)


def solve_moments(m):
    i0 = 1.0 / m[1][0]
    l10 = df_over(m[2], m[1], i0)
    l20 = df_over(m[3], m[1], i0)
    d1 = df_sub(m[3], df_mul(l10, m[2]))
    e12 = df_sub(m[4], df_mul(l10, m[3]))
    y1 = df_sub(m[1], df_mul(l10, m[0]))
    y2 = df_sub(m[2], df_mul(l20, m[0]))
    d2 = df_sub(m[5], df_mul(l20, m[3]))
    ok1 = d1[0] > PIVOT_FLOOR * m[3][0]
    i1 = jnp.where(ok1, 1.0 / d1[0], 0.0)
    l21 = df_over(e12, d1, i1)
    d2 = df_sub(d2, df_mul(l21, e12))
    y2 = df_sub(y2, df_mul(l21, y1))
    ok2 = ok1 & (d2[0] > PIVOT_FLOOR * m[5][0])
    c2 = jnp.where(ok2, y2[0] / d2[0], 0.0)
    p, e = two_mul(e12[0], c2)
    c1 = (((y1[0] - p) - e) + (y1[1] - e12[1] * c2)) * i1
    p1, e1 = two_mul(m[2][0], c1)
    p2, e2 = two_mul(m[3][0], c2)
    s, t1 = two_sum(m[0][0], -p1)
    s, t2 = two_sum(s, -p2)
    rest = (t1 - e1) + (t2 - e2) + (m[0][1] - m[2][1] * c1 - m[3][1] * c2)
    return (s + rest) * i0, c1, c2


def row_total(rows):
    s, e = two_sum(rows[0:8], rows[8:16])
    for step in (4, 2, 1):
        other = pltpu.roll(s, step, axis=0)
        e = e + pltpu.roll(e, step, axis=0)
        s, more = two_sum(s, other)
        e = e + more
    return s, e


def opposite(side):
    return tuple(-v for v in side)


def messages(field, tz, tlo, thi, dz):
    xs, xd = {-1: 2, 1: 9}, {-1: 10, 1: 1}
    ys, yd = {-1: 8, 1: 39}, {-1: 40, 1: 7}
    xs2, xd2 = {-1: pl.ds(2, 2), 1: pl.ds(8, 2)}, {-1: pl.ds(10, 2), 1: pl.ds(0, 2)}
    ys2, yd2 = {-1: pl.ds(8, 2), 1: pl.ds(38, 2)}, {-1: pl.ds(40, 2), 1: pl.ds(6, 2)}
    rows, planes = pl.ds(8, BY), pl.ds(2, BX)
    table = [[], [], []]
    for side in XZ + YZ + XY + SIDES[:2] + SIDES[4:6] + SIDES[2:4]:
        a, b, c = side
        far = thi if c < 0 else tlo
        slot = (XZ + YZ).index(opposite(side)) if side in XZ + YZ else None
        enth = []
        if side in XZ:
            first = [(tz.at[pl.ds(TU0, 3)], dz.at[slot, pl.ds(0, 3)])]
            image = [(tz.at[TW], dz.at[slot, 4])]
        elif side in YZ:
            first = [(tz.at[pl.ds(TC, 4)], dz.at[slot, pl.ds(0, 4)])]
            image = [(tz.at[TW], dz.at[slot, 4])]
        elif side in XY:
            first = [(field.at[pl.ds(C, 4), xs[a], ys[b]], field.at[pl.ds(C, 4), xd[a], yd[b]])]
            image = [(field.at[W1, xs[a], ys[b]], field.at[W1, xd[a], yd[b]])]
        elif a:
            first = [
                (field.at[C, xs2[a], rows], field.at[C, xd2[a], rows]),
                (field.at[pl.ds(U0, 2), xs[a], rows], field.at[pl.ds(U0, 2), xd[a], rows]),
            ]
            enth = [(field.at[H, xs[a], rows], field.at[H, xd[a], rows])]
            image = [(field.at[W1, xs2[a], rows], field.at[W1, xd2[a], rows])]
        elif b:
            first = [
                (field.at[C, planes, ys2[b]], field.at[C, planes, yd2[b]]),
                (field.at[pl.ds(BP, 2), planes, ys[b]], field.at[pl.ds(BP, 2), planes, yd[b]]),
            ]
            enth = [(field.at[H, planes, ys[b]], field.at[H, planes, yd[b]])]
            image = [(field.at[W1, planes, ys2[b]], field.at[W1, planes, yd2[b]])]
        else:
            first = [(tz.at[pl.ds(TC, 3)], far.at[pl.ds(TC, 3)])]
            enth = [(tz.at[TH], far.at[TH])]
            image = [(tz.at[TW], far.at[TW])]
        for kind, pairs in ((FIRST, first), (ENTH, enth), (IMAGE, image)):
            table[kind] += [(side, src, dst) for src, dst in pairs]
    return table


def kernel(
    vel, coef, enth, void, cells, normal, flag,
    w_out, g_out, u_out, h_out, c_out,
    field, tz, tlo, thi, dz, cx, cy, czm, czp, zlow, av, wc, wn, wf, hot_row, hot_lane, grid,
    heat, reduce, tally, load_sem, copy_sem, send_sem, recv_sem, sum_send, sum_recv,
):
    gx, gy, gz = lax.axis_index("gx"), lax.axis_index("gy"), lax.axis_index("gz")
    chip_y, core = gy // 2, lax.rem(gy, 2)

    has = dict(zip(SIDES[:6], (gx > 0, gx < NGX - 1, gy > 0, gy < NGY - 1, gz > 0, gz < NGZ - 1)))

    def beside(side):
        return tuple(
            lax.rem(at + step + size, size) if step else at
            for at, step, size in zip((gx, gy, gz), side, (NGX, NGY, NGZ))
        )

    def in_plane(i, j):
        return (lax.rem(gx + i, NGX), lax.rem(chip_y + j, NGY // 2) * 2 + core, gz)

    def in_column(k, j):
        return (gx, chip_y * 2 + lax.rem(core + j, 2), lax.rem(gz + k, NGZ))

    def far_first(pairs, n, m):
        return sorted(pairs, key=lambda p: -min(p[0], n - p[0]) - min(p[1], m - p[1]))

    plane = [in_plane(i, j) for i, j in far_first([(i, j) for i in range(NGX) for j in range(NGY // 2) if i or j], NGX, NGY // 2)]
    column = [in_column(k, j) for k, j in far_first([(k, j) for k in range(NGZ) for j in range(2) if k or j], NGZ, 2)]

    inner = (pl.ds(2, BX), pl.ds(8, BY))
    loads = [
        (cells, wc), (flag, wf), (normal, wn),
        (vel.at[0], field.at[(U0,) + inner]),
        (vel.at[pl.ds(1, 2)], field.at[(pl.ds(U1, 2),) + inner]),
        (void, av),
        (coef, field.at[(C,) + inner]),
        (enth, field.at[(H,) + inner]),
    ]
    loads = [pltpu.make_async_copy(s, d, load_sem.at[i]) for i, (s, d) in enumerate(loads)]
    for copy in loads:
        copy.start()

    barrier = pltpu.get_barrier_semaphore()
    greeted = [beside(side) for side in SIDES] + plane[::-1] + column[::-1]
    for partner in greeted:
        pl.semaphore_signal(barrier, inc=1, device_id=partner, device_id_type=MESH)

    table = messages(field, tz, tlo, thi, dz)
    copies = [
        [
            pltpu.make_async_remote_copy(
                src_ref=src, dst_ref=dst, send_sem=send_sem.at[kind], recv_sem=recv_sem.at[kind],
                device_id=beside(side), device_id_type=MESH,
            )
            for side, src, dst in table[kind]
        ]
        for kind in range(3)
    ]

    def whole(kind):
        count = sum(math.prod(dst.shape) for _, _, dst in table[kind]) // BZ
        ref = tally.at[pl.ds(0, count)]
        return pltpu.make_async_remote_copy(
            src_ref=ref, dst_ref=ref, send_sem=send_sem.at[kind], recv_sem=recv_sem.at[kind],
            device_id=beside(SIDES[0]), device_id_type=MESH,
        )

    def send(kind):
        for copy in copies[kind]:
            copy.start()

    def receive(kind):
        whole(kind).wait_recv()
        for side in SIDES[:6]:
            dim = [i for i in range(3) if side[i]][0]

            @pl.when(jnp.logical_not(has[side]))
            def _():
                for to, _, dst in table[kind]:
                    if to[dim] == -side[dim]:
                        dst[...] = jnp.zeros(dst.shape, jnp.float32)

    lane8 = lax.broadcasted_iota(jnp.int32, (8, BZ), 1)
    sub8 = lax.broadcasted_iota(jnp.int32, (8, BZ), 0)
    lane32 = lax.broadcasted_iota(jnp.int32, (BY, BZ), 1)
    row32 = lax.broadcasted_iota(jnp.int32, (BY, BZ), 0)
    first, last = lane32 == 0, lane32 == BZ - 1
    first8, last8 = lane8 == 0, lane8 == BZ - 1
    place = lane8 % 4
    low_lane = place == 1
    y_group = lane8 // 4 % 4
    ends_half = jnp.where(first8, 0.5, jnp.where(last8, -0.5, 0.0))
    ends_half32 = jnp.where(first, 0.5, jnp.where(last, -0.5, 0.0))

    def turn(v, by, axis=1):
        size = v.shape[axis]
        return pltpu.roll(v, by % size, axis=axis) if by % size else v

    def pack(values, acc, x):
        for b in range(4):
            k = 4 * x + b
            turned = turn(values[8 * b : 8 * b + 8], 4 * k + 2)
            acc = turned if acc is None else jnp.where(lane8 // 4 == k, turned, acc)
        return acc

    def pair(low, high):
        return jnp.where(low_lane, low, high)

    def swap(v):
        return jnp.where(low_lane, turn(v, -1), turn(v, 1))

    def ends(swapped, x):
        return jnp.concatenate([turn(swapped, -4 * (4 * x + b) - 2) for b in range(4)], axis=0)

    def ends_row(swapped, b):
        row, k = (7, 3) if b < 0 else (0, 0)
        out = None
        spread = jnp.broadcast_to(swapped[row : row + 1], (8, BZ))
        for x in range(BX):
            turned = turn(spread, -4 * (4 * x + k) - 2)
            out = turned if out is None else jnp.where(sub8 == x, turned, out)
        return out

    def around_z(v, e):
        f, l = (first, last) if v.shape[0] == BY else (first8, last8)
        return jnp.where(l, e, turn(v, -1)), jnp.where(f, e, turn(v, 1))

    def around_y(f, x):
        return field[f, x + 2, 9:41, :], field[f, x + 2, 7:39, :]

    def centre(f, x):
        return field[f, x + 2, ROWS, :]

    def row_of_field(f, r):
        return field[f, 2:10, r, :]

    def diagonal(side, q):
        a, b, _ = side
        lo, hi = ((XZ + YZ).index((a, b, c)) for c in SIGNS)
        return pair(dz[lo, q], dz[hi, q])

    xm_side, xp_side, ym_side, yp_side, zm_side, zp_side = SIDES[:6]

    for copy in loads[0:3]:
        copy.wait()
    where = wc[...]
    row_at = where // BZ
    lane_at = where - row_at * BZ
    code = jnp.where(wf[...] > 0, wf[...] + 4 * (wn[...] // 2), 0).astype(jnp.float32)
    up256 = lax.broadcasted_iota(jnp.int32, (BX * BY, BZ), 0)
    up128 = lax.broadcasted_iota(jnp.int32, (BZ, BZ), 0)
    for s in range(SLOTS):
        hot_row[:, s * BZ : (s + 1) * BZ] = jnp.where(up256 == row_at[s : s + 1], 1.0, 0.0).astype(jnp.bfloat16)
        hot_lane[:, s * BZ : (s + 1) * BZ] = jnp.where(up128 == lane_at[s : s + 1], code[s : s + 1], 0.0).astype(jnp.bfloat16)
    grid[...] = lax.dot_general(
        hot_row[...], hot_lane[...], (((1,), (1,)), ((), ())), preferred_element_type=jnp.float32
    )
    for copy in loads[3:]:
        copy.wait()

    t_b = t_c = t_u0 = t_u1 = t_u2 = None
    for x in range(BX):
        a = av[x]
        g = grid[x * BY : (x + 1) * BY, :]
        not_x = g > 3.5
        is_z = g > 7.5
        s = g - jnp.where(not_x, 4.0, 0.0) - jnp.where(is_z, 4.0, 0.0)
        u0, u1, u2 = centre(U0, x), centre(U1, x), centre(U2, x)
        parallel = (
            jnp.where(not_x, u0 * u0, 0.0)
            + jnp.where(not_x & jnp.logical_not(is_z), 0.0, u1 * u1)
            + jnp.where(is_z, 0.0, u2 * u2)
        )
        speed = jnp.sqrt(parallel + 0.25)
        liquid = 1.0 - a
        evap = 1.5 * a * s * s
        root = jnp.where(s > 1.5, 2.0 * 1.4142135623730951, s)
        heat[x] = liquid * speed * s + 0.6 * liquid * root + evap
        slope = jnp.where(row32 == BY - 1, 0.0, turn(u1, -1, 0)) - jnp.where(row32 == 0, 0.0, turn(u1, 1, 0))
        slope = slope + (jnp.where(last, 0.0, turn(u2, -1)) - jnp.where(first, 0.0, turn(u2, 1)))
        if x < BX - 1:
            slope = slope + centre(U0, x + 1)
        if x > 0:
            slope = slope - centre(U0, x - 1)
        b = EXPANSION * (0.5 * evap) - 0.5 * slope
        field[BP, x + 2, ROWS, :] = b
        t_b = pack(b, t_b, x)
        t_c = pack(centre(C, x), t_c, x)
        t_u0 = pack(u0, t_u0, x)
        t_u1 = pack(u1, t_u1, x)
        t_u2 = pack(u2, t_u2, x)
    for i, t in ((TB, t_b), (TC, t_c), (TU0, t_u0), (TU1, t_u1), (TU2, t_u2)):
        tz[i] = t

    pl.semaphore_wait(barrier, len(greeted))
    send(FIRST)

    t_h = None
    half = 0.5 / SCALE
    for x in range(BX):
        t_h = pack(centre(H, x), t_h, x)
        c = centre(C, x)
        if x < BX - 1:
            cx[x + 2] = half * (c + centre(C, x + 1))
        cy[x + 1, 0:32] = half * (c + turn(c, 1, 0))
        czp[x + 1] = half * jnp.where(last, c, c + turn(c, -1))
        czm[x + 1] = half * jnp.where(first, c, c + turn(c, 1))
    tz[TH] = t_h
    send(ENTH)

    def low_high(v):
        return v[0:8], v[8:24], v[24:32]

    def y_ends(v, f, x):
        a, m, z = low_high(v)
        a = a + jnp.where(sub8 == 0, 0.5 * field[f, x + 2, 7:8, :], 0.0)
        z = z - jnp.where(sub8 == 7, 0.5 * field[f, x + 2, 40:41, :], 0.0)
        return jnp.concatenate([a, m, z], axis=0)

    receive(FIRST)
    s_u2 = swap(pair(tlo[TU2], thi[TU2]))
    s_c = swap(pair(tlo[TC], thi[TC]))
    for x in range(BX):
        b = centre(BP, x) + ends_half32 * ends(s_u2, x)
        b = y_ends(b, U1, x)
        if x == 0:
            b = b + 0.5 * field[U0, 1, ROWS, :]
        if x == BX - 1:
            b = b - 0.5 * field[U0, 10, ROWS, :]
        field[W0, x + 2, ROWS, :] = b
        c = centre(C, x)
        e = ends(s_c, x)
        czp[x + 1] = czp[x + 1] + jnp.where(last, half * e, 0.0)
        czm[x + 1] = czm[x + 1] + jnp.where(first, half * e, 0.0)
        cy[x + 1, 0:1] = half * (c[0:1] + field[C, x + 2, 7:8, :])
        cy[x + 1, 32:33] = half * (c[31:32] + field[C, x + 2, 40:41, :])
    cx[1] = half * (centre(C, 0) + centre(C, -1))
    cx[9] = half * (centre(C, 7) + centre(C, 8))
    for x, own, sign, side, inside in ((-1, 0, -0.5, xm_side, 7), (BX, BX - 1, 0.5, xp_side, 0)):
        b = centre(BP, x) + sign * centre(U0, own)
        b = y_ends(b, U1, x) + ends_half32 * ends(swap(diagonal(side, 2)), inside)
        field[W0, x + 2, ROWS, :] = jnp.where(has[side], b, 0.0)
    for r, own, sign, side in ((7, 8, -0.5, ym_side), (40, 39, 0.5, yp_side)):
        b = row_of_field(BP, r) + sign * row_of_field(U1, own)
        b = b + jnp.where(sub8 == 0, 0.5 * field[U0, 1, r : r + 1, :], 0.0)
        b = b - jnp.where(sub8 == 7, 0.5 * field[U0, 10, r : r + 1, :], 0.0)
        b = b + ends_half * ends_row(swap(diagonal(side, 1)), side[1])
        b = jnp.where(has[side], b, 0.0)
        for x in range(BX):
            field[W0, x + 2, r : r + 1, :] = b[x : x + 1]
    has_z = jnp.where(low_lane, has[zm_side].astype(jnp.float32), has[zp_side].astype(jnp.float32))

    def z_inside(t):
        return jnp.where(low_lane, turn(t, -1), turn(t, 1))

    def z_around_x(v, before, after):
        return (
            jnp.where(lane8 >= 112, turn(after, -16), turn(v, -16)),
            jnp.where(lane8 < 16, turn(before, 16), turn(v, 16)),
        )

    def z_around_y(v, before, after):
        up = jnp.where(y_group == 3, turn(after, 12), turn(v, -4))
        down = jnp.where(y_group == 0, turn(before, -12), turn(v, 4))
        return (
            turn(jnp.where(sub8 == 0, up, v), -1, 0),
            turn(jnp.where(sub8 == 7, down, v), 1, 0),
        )

    zero = jnp.zeros((8, BZ), jnp.float32)
    after, before = z_around_x(zero, diagonal(xm_side, 0), diagonal(xp_side, 0))
    b = pair(tlo[TB], thi[TB]) - 0.5 * (after - before)
    after, before = z_around_y(zero, diagonal(ym_side, 3), diagonal(yp_side, 3))
    b = b - 0.5 * (after - before) + jnp.where(low_lane, -0.5, 0.5) * z_inside(tz[TU2])
    s_w0 = swap(has_z * b)

    def operator(f, x, e):
        v = centre(f, x)
        yp, ym = around_y(f, x)
        zp, zm = around_z(v, e)
        out = cx[x + 2] * (v - centre(f, x + 1)) + cx[x + 1] * (v - centre(f, x - 1))
        out = out + (cy[x + 1, 1:33] * (v - yp) + cy[x + 1, 0:32] * (v - ym))
        return out + (czp[x + 1] * (v - zp) + czm[x + 1] * (v - zm))

    t_w = None
    for x in range(BX):
        out = operator(W0, x, ends(s_w0, x))
        field[W1, x + 2, ROWS, :] = out
        t_w = pack(out, t_w, x)
    tz[TW] = t_w
    send(IMAGE)

    def fold(v):
        return (v[0:8] + v[8:16]) + (v[16:24] + v[24:32])

    def plus(acc, v):
        v = fold(v)
        return v if acc is None else acc + v

    m = [None] * 6
    for x in range(BX):
        v, out = centre(W0, x), centre(W1, x)
        m[0], m[1], m[2] = plus(m[0], v * v), plus(m[1], v * out), plus(m[2], out * out)
    for x, side, inside in ((-1, xm_side, 7), (BX, xp_side, 0)):
        c = centre(C, x)
        if x < 0:
            cx[0] = half * (c + centre(C, -2))
        else:
            cx[10] = half * (c + centre(C, 9))
        after, before = around_y(C, x)
        cy[x + 1, 0:32] = half * (c + before)
        cy[x + 1, 32:33] = half * (c[31:32] + after[31:32])
        after, before = around_z(c, ends(swap(diagonal(side, 1)), inside))
        czp[x + 1] = half * (c + after)
        czm[x + 1] = half * (c + before)
    z_edge = jnp.where(has[zm_side], 0.0, 1.0)
    y_edge = jnp.where(has[ym_side], 0.0, 1.0)
    x_edge = jnp.where(has[xm_side], 0.0, 1.0)
    for x in range(BX):
        low = jnp.where(first, czm[x + 1], 0.0) * z_edge
        low = low + jnp.where(row32 == 0, cy[x + 1, 0:32], 0.0) * y_edge
        if x == 0:
            low = low + cx[1] * x_edge
        zlow[x] = low

    receive(IMAGE)
    s_w1 = swap(pair(tlo[TW], thi[TW]))
    for x in range(BX):
        out = operator(W1, x, ends(s_w1, x))
        field[W2, x + 2, ROWS, :] = out
        v = centre(W1, x)
        m[3], m[4] = plus(m[3], v * out), plus(m[4], out * out)

    def image_plane(x, side, inside):
        out = operator(W1, x, ends(swap(diagonal(side, 4)), inside))
        field[W2, x + 2, ROWS, :] = jnp.where(has[side], out, 0.0)

    def image_row(r, beyond, own, side):
        sums = []
        c, v = row_of_field(C, r), row_of_field(W1, r)

        def term(cn, vn):
            return (c + cn) * (v - vn)

        out = term(row_of_field(C, beyond), row_of_field(W1, beyond)) + term(row_of_field(C, own), row_of_field(W1, own))
        both = []
        for f, q, values in ((C, 0, c), (W1, 4, v)):
            after = jnp.where(sub8 == 7, field[f, 10, r : r + 1, :], turn(values, -1, 0))
            before = jnp.where(sub8 == 0, field[f, 1, r : r + 1, :], turn(values, 1, 0))
            zp, zm = around_z(values, ends_row(swap(diagonal(side, q)), side[1]))
            both.append((after, before, zp, zm))
        for cn, vn in zip(*both):
            out = out + term(cn, vn)
        out = jnp.where(has[side], half * out, 0.0)
        for x in range(BX):
            field[W2, x + 2, r : r + 1, :] = out[x : x + 1]

    def image_face():
        both = []
        for t, qx, qy in ((TC, 1, 0), (TW, 4, 4)):
            lo, hi, own = tlo[t], thi[t], tz[t]
            v = pair(lo, hi)
            outer = jnp.where(low_lane, turn(lo, 1), turn(hi, -1))
            both.append(
                (v, outer, z_inside(own))
                + z_around_x(v, diagonal(xm_side, qx), diagonal(xp_side, qx))
                + z_around_y(v, diagonal(ym_side, qy), diagonal(yp_side, qy))
            )
        (c, *near_c), (v, *near_v) = both
        out = zero
        for cn, vn in zip(near_c, near_v):
            out = out + (c + cn) * (v - vn)
        return swap(has_z * (half * out))

    image_plane(BX, xp_side, 0)
    image_row(40, 41, 39, yp_side)
    s_w2 = image_face()
    for x in range(BX):
        v = centre(W2, x)
        dx = v - centre(W2, x + 1)
        dy = v - field[W2, x + 2, 9:41, :]
        dz_ = v - jnp.where(last, ends(s_w2, x), turn(v, -1))
        m[5] = plus(
            m[5],
            (cx[x + 2] * (dx * dx) + cy[x + 1, 1:33] * (dy * dy)) + (czp[x + 1] * (dz_ * dz_) + zlow[x] * (v * v)),
        )

    row = jnp.zeros((1, BZ), jnp.float32)
    for i in range(6):
        row = jnp.where(lane8[0:1] == i, jnp.sum(m[i], keepdims=True), row)

    def sum_copy(phase, slot, partner):
        return pltpu.make_async_remote_copy(
            src_ref=reduce.at[phase, pl.ds(0, 1)], dst_ref=reduce.at[phase, pl.ds(slot + 1, 1)],
            send_sem=sum_send.at[phase], recv_sem=sum_recv.at[phase], device_id=partner, device_id_type=MESH,
        )

    def sum_whole(phase):
        ref = tally.at[pl.ds(0, 15)]
        return pltpu.make_async_remote_copy(
            src_ref=ref, dst_ref=ref, send_sem=sum_send.at[phase], recv_sem=sum_recv.at[phase],
            device_id=plane[0], device_id_type=MESH,
        )

    def start_sum(phase, row, group):
        reduce[phase, 0:1, :] = row
        for slot, partner in enumerate(group):
            sum_copy(phase, slot, partner).start()

    def end_sum(phase):
        sum_whole(phase).wait_recv()
        return row_total(reduce[phase])

    start_sum(0, row, plane)
    image_plane(-1, xm_side, 7)
    image_row(7, 6, 8, ym_side)
    copy_u = pltpu.make_async_copy(field.at[(U0,) + inner], u_out.at[0], copy_sem.at[0])
    copy_u.start()
    copy_v = pltpu.make_async_copy(field.at[(pl.ds(U1, 2),) + inner], u_out.at[pl.ds(1, 2)], copy_sem.at[2])
    copy_v.start()
    copy_w = pltpu.make_async_copy(field.at[(pl.ds(W0, 3),) + inner], w_out, copy_sem.at[1])
    copy_w.start()
    for i, (f, swapped) in enumerate(((W0, s_w0), (W1, s_w1), (W2, s_w2))):
        for x in range(BX):
            c = (0.5 / SCALE) * centre(C, x)
            g_out[i, 0, x] = c * (centre(f, x + 1) - centre(f, x - 1))
            after, before = around_y(f, x)
            g_out[i, 1, x] = c * (after - before)
            after, before = around_z(centre(f, x), ends(swapped, x))
            g_out[i, 2, x] = c * (after - before)
    receive(ENTH)
    s_h = swap(pair(tlo[TH], thi[TH]))
    for x in range(BX):
        h = centre(H, x)
        hyp, hym = around_y(H, x)
        hzp, hzm = around_z(h, ends(s_h, x))
        laplace = centre(H, x + 1) + centre(H, x - 1) + hyp + hym + hzp + hzm - 6.0 * h
        h_out[x] = h + DIFFUSE * laplace + HEATING * heat[x]
    copy_u.wait()
    copy_v.wait()
    copy_w.wait()
    for kind in range(3):
        whole(kind).wait_send()

    high, low = end_sum(0)
    row = jnp.where(lane8 < 8, high, turn(low, 8))[0:1]
    start_sum(1, row, column)
    high, low = end_sum(1)
    low = low + turn(high, -8)
    high, low = quick_sum(high, low)

    def spread(v, i):
        return jnp.broadcast_to(v[:, i : i + 1], (8, BZ))

    moments = [(spread(high, i), spread(low, i)) for i in range(6)]
    for i, v in enumerate(solve_moments(moments)):
        c_out[i] = v
    sum_whole(0).wait_send()
    sum_whole(1).wait_send()


def finish(w, g, u, h, c, vel_out, p_out, h_out, vel, p, sem):
    copy_h = pltpu.make_async_copy(h, h_out, sem.at[0])
    copy_h.start()
    c0, c1, c2 = (jnp.concatenate([c[i]] * 4, axis=0) for i in range(3))
    copies = [copy_h]
    for i in range(3):
        for x in range(BX):
            vel[i, x] = u[i, x] - (c0 * g[0, i, x] + c1 * g[1, i, x] + c2 * g[2, i, x])
        copy = pltpu.make_async_copy(vel.at[i], vel_out.at[i], sem.at[1 + i])
        copy.start()
        copies.append(copy)
    scaled = tuple(v * (1.0 / SCALE) for v in (c0, c1, c2))
    for x in range(BX):
        p[x] = scaled[0] * w[0, x] + scaled[1] * w[1, x] + scaled[2] * w[2, x]
    copy_p = pltpu.make_async_copy(p, p_out, sem.at[4])
    copy_p.start()
    for copy in copies + [copy_p]:
        copy.wait()


def shards(*args):
    block = (BX, BY, BZ)
    f32 = jnp.float32
    any_ref = pl.BlockSpec(memory_space=pl.ANY)
    vmem = pl.BlockSpec(memory_space=pltpu.VMEM)
    results = pl.pallas_call(
        kernel,
        out_shape=(
            jax.ShapeDtypeStruct((3,) + block, f32),
            jax.ShapeDtypeStruct((3, 3) + block, f32),
            jax.ShapeDtypeStruct((3,) + block, f32),
            jax.ShapeDtypeStruct(block, f32),
            jax.ShapeDtypeStruct((3, 8, BZ), f32),
        ),
        in_specs=[any_ref] * 7,
        out_specs=(vmem,) * 5,
        scratch_shapes=[
            pltpu.VMEM((FIELDS, BX + 4, BY + 16, BZ), f32),
            pltpu.VMEM((7, 8, BZ), f32),
            pltpu.VMEM((7, 8, BZ), f32),
            pltpu.VMEM((7, 8, BZ), f32),
            pltpu.VMEM((8, 5, 8, BZ), f32),
            pltpu.VMEM((BX + 3, BY, BZ), f32),
            pltpu.VMEM((BX + 2, BY + 8, BZ), f32),
            pltpu.VMEM((BX + 2, BY, BZ), f32),
            pltpu.VMEM((BX + 2, BY, BZ), f32),
            pltpu.VMEM(block, f32),
            pltpu.VMEM(block, f32),
            pltpu.VMEM((SLOTS, BZ), jnp.int32),
            pltpu.VMEM((SLOTS, BZ), jnp.int32),
            pltpu.VMEM((SLOTS, BZ), jnp.int32),
            pltpu.VMEM((BX * BY, SLOTS * BZ), jnp.bfloat16),
            pltpu.VMEM((BZ, SLOTS * BZ), jnp.bfloat16),
            pltpu.VMEM((BX * BY, BZ), f32),
            pltpu.VMEM(block, f32),
            pltpu.VMEM((2, 16, BZ), f32),
            pltpu.VMEM((1024, BZ), f32),
            pltpu.SemaphoreType.DMA((8,)),
            pltpu.SemaphoreType.DMA((3,)),
            pltpu.SemaphoreType.DMA((3,)),
            pltpu.SemaphoreType.DMA((3,)),
            pltpu.SemaphoreType.DMA((2,)),
            pltpu.SemaphoreType.DMA((2,)),
        ],
        compiler_params=pltpu.CompilerParams(
            collective_id=0, has_side_effects=True, vmem_limit_bytes=32 * 1024 * 1024
        ),
        name="simple_step",
    )(*[pltpu.with_memory_space_constraint(a, pltpu.HBM) for a in args])
    results = [pltpu.with_memory_space_constraint(r, pltpu.VMEM) for r in results]
    return tuple(
        pl.pallas_call(
            finish,
            out_shape=(
                jax.ShapeDtypeStruct((3,) + block, f32),
                jax.ShapeDtypeStruct(block, f32),
                jax.ShapeDtypeStruct(block, f32),
            ),
            in_specs=[vmem] * 5,
            out_specs=(pl.BlockSpec(memory_space=pltpu.HBM),) * 3,
            scratch_shapes=[
                pltpu.VMEM((3,) + block, f32),
                pltpu.VMEM(block, f32),
                pltpu.SemaphoreType.DMA((5,)),
            ],
            compiler_params=pltpu.CompilerParams(vmem_limit_bytes=8 * 1024 * 1024),
            name="finish",
        )(*results)
    )


def solution(mesh):
    in_specs = (
        P(None, "gx", "gy", "gz"),
        P("gx", "gy", "gz"),
        P("gx", "gy", "gz"),
        P("gx", "gy", "gz"),
        P(("gx", "gy", "gz"), None),
        P(("gx", "gy", "gz"), None),
        P(("gx", "gy", "gz"), None),
    )
    out_specs = (P(None, "gx", "gy", "gz"), P("gx", "gy", "gz"), P("gx", "gy", "gz"))
    return jax.shard_map(shards, mesh=mesh, in_specs=in_specs, out_specs=out_specs, check_vma=False)
```

```python
import math

import jax
import jax.numpy as jnp
from jax import lax
from jax.experimental import pallas as pl
from jax.experimental.pallas import tpu as pltpu
from jax.sharding import PartitionSpec as P

MESH = pl.DeviceIdType.MESH
NGX, NGY, NGZ = 4, 8, 8
BX, BY, BZ = 8, 32, 128
SLOTS = 16
DIFFUSE = 0.1
HEATING = 0.5
EXPANSION = 1.5
SCALE = 16.0
H, C, U0, BP, U1, U2, W0, W1, W2 = range(9)
FIELDS = 9
TU0, TC, TU2, TB, TU1, TH, TW = range(7)
ROWS = slice(8, 40)
SIGNS = (-1, 1)
XZ = tuple((a, 0, c) for a in SIGNS for c in SIGNS)
YZ = tuple((0, b, c) for b in SIGNS for c in SIGNS)
XY = tuple((a, b, 0) for a in SIGNS for b in SIGNS)
SIDES = ((-1, 0, 0), (1, 0, 0), (0, -1, 0), (0, 1, 0), (0, 0, -1), (0, 0, 1)) + XY + XZ + YZ
FIRST, ENTH, IMAGE = range(3)
PIVOT_FLOOR = 1e-9
ROOT = (0, 1, 0)
DEVICES = 256


def two_sum(a, b):
    s = a + b
    t = s - a
    return s, (a - (s - t)) + (b - t)


def quick_sum(a, b):
    s = a + b
    return s, b - (s - a)


def split(a):
    t = 4097.0 * a
    high = t - (t - a)
    return high, a - high


def two_mul(a, b):
    p = a * b
    ah, al = split(a)
    bh, bl = split(b)
    return p, ((ah * bh - p) + ah * bl + al * bh) + al * bl


def df_sub(a, b):
    s, e = two_sum(a[0], -b[0])
    return quick_sum(s, e + (a[1] - b[1]))


def df_mul(a, b):
    p, e = two_mul(a[0], b[0])
    return quick_sum(p, e + (a[0] * b[1] + a[1] * b[0]))


def df_over(a, b, inverse):
    q = a[0] * inverse
    p, e = two_mul(q, b[0])
    rest = ((a[0] - p) - e) + (a[1] - q * b[1])
    return quick_sum(q, rest * inverse)


def solve_moments(m):
    i0 = 1.0 / m[1][0]
    l10 = df_over(m[2], m[1], i0)
    l20 = df_over(m[3], m[1], i0)
    d1 = df_sub(m[3], df_mul(l10, m[2]))
    e12 = df_sub(m[4], df_mul(l10, m[3]))
    y1 = df_sub(m[1], df_mul(l10, m[0]))
    y2 = df_sub(m[2], df_mul(l20, m[0]))
    d2 = df_sub(m[5], df_mul(l20, m[3]))
    ok1 = d1[0] > PIVOT_FLOOR * m[3][0]
    i1 = jnp.where(ok1, 1.0 / d1[0], 0.0)
    l21 = df_over(e12, d1, i1)
    d2 = df_sub(d2, df_mul(l21, e12))
    y2 = df_sub(y2, df_mul(l21, y1))
    ok2 = ok1 & (d2[0] > PIVOT_FLOOR * m[5][0])
    c2 = jnp.where(ok2, y2[0] / d2[0], 0.0)
    p, e = two_mul(e12[0], c2)
    c1 = (((y1[0] - p) - e) + (y1[1] - e12[1] * c2)) * i1
    p1, e1 = two_mul(m[2][0], c1)
    p2, e2 = two_mul(m[3][0], c2)
    s, t1 = two_sum(m[0][0], -p1)
    s, t2 = two_sum(s, -p2)
    rest = (t1 - e1) + (t2 - e2) + (m[0][1] - m[2][1] * c1 - m[3][1] * c2)
    return (s + rest) * i0, c1, c2


def row_total(rows):
    parts = [(rows[i : i + 8], None) for i in range(0, rows.shape[0], 8)]
    while len(parts) > 1:
        merged = []
        for (a, low_a), (b, low_b) in zip(parts[0::2], parts[1::2]):
            s, e = two_sum(a, b)
            merged.append((s, e if low_a is None else e + (low_a + low_b)))
        parts = merged
    s, e = parts[0]
    for step in (4, 2, 1):
        other = pltpu.roll(s, step, axis=0)
        e = e + pltpu.roll(e, step, axis=0)
        s, more = two_sum(s, other)
        e = e + more
    return s, e


def opposite(side):
    return tuple(-v for v in side)


def messages(field, tz, tlo, thi, dz):
    xs, xd = {-1: 2, 1: 9}, {-1: 10, 1: 1}
    ys, yd = {-1: 8, 1: 39}, {-1: 40, 1: 7}
    xs2, xd2 = {-1: pl.ds(2, 2), 1: pl.ds(8, 2)}, {-1: pl.ds(10, 2), 1: pl.ds(0, 2)}
    ys2, yd2 = {-1: pl.ds(8, 2), 1: pl.ds(38, 2)}, {-1: pl.ds(40, 2), 1: pl.ds(6, 2)}
    rows, planes = pl.ds(8, BY), pl.ds(2, BX)
    table = [[], [], []]
    for side in XZ + YZ + XY + SIDES[:2] + SIDES[4:6] + SIDES[2:4]:
        a, b, c = side
        far = thi if c < 0 else tlo
        slot = (XZ + YZ).index(opposite(side)) if side in XZ + YZ else None
        enth = []
        if side in XZ:
            first = [(tz.at[pl.ds(TU0, 3)], dz.at[slot, pl.ds(0, 3)])]
            image = [(tz.at[TW], dz.at[slot, 4])]
        elif side in YZ:
            first = [(tz.at[pl.ds(TC, 4)], dz.at[slot, pl.ds(0, 4)])]
            image = [(tz.at[TW], dz.at[slot, 4])]
        elif side in XY:
            first = [(field.at[pl.ds(C, 4), xs[a], ys[b]], field.at[pl.ds(C, 4), xd[a], yd[b]])]
            image = [(field.at[W1, xs[a], ys[b]], field.at[W1, xd[a], yd[b]])]
        elif a:
            first = [
                (field.at[C, xs2[a], rows], field.at[C, xd2[a], rows]),
                (field.at[pl.ds(U0, 2), xs[a], rows], field.at[pl.ds(U0, 2), xd[a], rows]),
            ]
            enth = [(field.at[H, xs[a], rows], field.at[H, xd[a], rows])]
            image = [(field.at[W1, xs2[a], rows], field.at[W1, xd2[a], rows])]
        elif b:
            first = [
                (field.at[C, planes, ys2[b]], field.at[C, planes, yd2[b]]),
                (field.at[pl.ds(BP, 2), planes, ys[b]], field.at[pl.ds(BP, 2), planes, yd[b]]),
            ]
            enth = [(field.at[H, planes, ys[b]], field.at[H, planes, yd[b]])]
            image = [(field.at[W1, planes, ys2[b]], field.at[W1, planes, yd2[b]])]
        else:
            first = [(tz.at[pl.ds(TC, 3)], far.at[pl.ds(TC, 3)])]
            enth = [(tz.at[TH], far.at[TH])]
            image = [(tz.at[TW], far.at[TW])]
        for kind, pairs in ((FIRST, first), (ENTH, enth), (IMAGE, image)):
            table[kind] += [(side, src, dst) for src, dst in pairs]
    return table


def kernel(
    vel, coef, enth, void, cells, normal, flag,
    w_out, g_out, u_out, h_out, c_out,
    field, tz, tlo, thi, dz, cx, cy, czm, czp, zlow, av, wc, wn, wf, hot_row, hot_lane, grid,
    heat, reduce, direct, total, tally, load_sem, copy_sem, send_sem, recv_sem, sum_send, sum_recv, ready,
):
    gx, gy, gz = lax.axis_index("gx"), lax.axis_index("gy"), lax.axis_index("gz")
    chip_y, core = gy // 2, lax.rem(gy, 2)

    has = dict(zip(SIDES[:6], (gx > 0, gx < NGX - 1, gy > 0, gy < NGY - 1, gz > 0, gz < NGZ - 1)))

    def beside(side):
        return tuple(
            lax.rem(at + step + size, size) if step else at
            for at, step, size in zip((gx, gy, gz), side, (NGX, NGY, NGZ))
        )

    def in_plane(i, j):
        return (lax.rem(gx + i, NGX), lax.rem(chip_y + j, NGY // 2) * 2 + core, gz)

    def in_column(k, j):
        return (gx, chip_y * 2 + lax.rem(core + j, 2), lax.rem(gz + k, NGZ))

    def far_first(pairs, n, m):
        return sorted(pairs, key=lambda p: -min(p[0], n - p[0]) - min(p[1], m - p[1]))

    plane = [in_plane(i, j) for i, j in far_first([(i, j) for i in range(NGX) for j in range(NGY // 2) if i or j], NGX, NGY // 2)]
    column = [in_column(k, j) for k, j in far_first([(k, j) for k in range(NGZ) for j in range(2) if k or j], NGZ, 2)]

    inner = (pl.ds(2, BX), pl.ds(8, BY))
    loads = [
        (cells, wc), (flag, wf), (normal, wn),
        (vel.at[0], field.at[(U0,) + inner]),
        (vel.at[pl.ds(1, 2)], field.at[(pl.ds(U1, 2),) + inner]),
        (void, av),
        (coef, field.at[(C,) + inner]),
        (enth, field.at[(H,) + inner]),
    ]
    loads = [pltpu.make_async_copy(s, d, load_sem.at[i]) for i, (s, d) in enumerate(loads)]
    for copy in loads:
        copy.start()

    barrier = pltpu.get_barrier_semaphore()
    greeted = [beside(side) for side in SIDES] + plane[::-1] + column[::-1]
    for partner in greeted:
        pl.semaphore_signal(barrier, inc=1, device_id=partner, device_id_type=MESH)

    table = messages(field, tz, tlo, thi, dz)
    copies = [
        [
            pltpu.make_async_remote_copy(
                src_ref=src, dst_ref=dst, send_sem=send_sem.at[kind], recv_sem=recv_sem.at[kind],
                device_id=beside(side), device_id_type=MESH,
            )
            for side, src, dst in table[kind]
        ]
        for kind in range(3)
    ]

    def whole(kind):
        count = sum(math.prod(dst.shape) for _, _, dst in table[kind]) // BZ
        ref = tally.at[pl.ds(0, count)]
        return pltpu.make_async_remote_copy(
            src_ref=ref, dst_ref=ref, send_sem=send_sem.at[kind], recv_sem=recv_sem.at[kind],
            device_id=beside(SIDES[0]), device_id_type=MESH,
        )

    def send(kind):
        for copy in copies[kind]:
            copy.start()

    def receive(kind):
        whole(kind).wait_recv()
        for side in SIDES[:6]:
            dim = [i for i in range(3) if side[i]][0]

            @pl.when(jnp.logical_not(has[side]))
            def _():
                for to, _, dst in table[kind]:
                    if to[dim] == -side[dim]:
                        dst[...] = jnp.zeros(dst.shape, jnp.float32)

    lane8 = lax.broadcasted_iota(jnp.int32, (8, BZ), 1)
    sub8 = lax.broadcasted_iota(jnp.int32, (8, BZ), 0)
    lane32 = lax.broadcasted_iota(jnp.int32, (BY, BZ), 1)
    row32 = lax.broadcasted_iota(jnp.int32, (BY, BZ), 0)
    first, last = lane32 == 0, lane32 == BZ - 1
    first8, last8 = lane8 == 0, lane8 == BZ - 1
    place = lane8 % 4
    low_lane = place == 1
    y_group = lane8 // 4 % 4
    ends_half = jnp.where(first8, 0.5, jnp.where(last8, -0.5, 0.0))
    ends_half32 = jnp.where(first, 0.5, jnp.where(last, -0.5, 0.0))

    def turn(v, by, axis=1):
        size = v.shape[axis]
        return pltpu.roll(v, by % size, axis=axis) if by % size else v

    def pack(values, acc, x):
        for b in range(4):
            k = 4 * x + b
            turned = turn(values[8 * b : 8 * b + 8], 4 * k + 2)
            acc = turned if acc is None else jnp.where(lane8 // 4 == k, turned, acc)
        return acc

    def pair(low, high):
        return jnp.where(low_lane, low, high)

    def swap(v):
        return jnp.where(low_lane, turn(v, -1), turn(v, 1))

    def ends(swapped, x):
        return jnp.concatenate([turn(swapped, -4 * (4 * x + b) - 2) for b in range(4)], axis=0)

    def ends_row(swapped, b):
        row, k = (7, 3) if b < 0 else (0, 0)
        out = None
        spread = jnp.broadcast_to(swapped[row : row + 1], (8, BZ))
        for x in range(BX):
            turned = turn(spread, -4 * (4 * x + k) - 2)
            out = turned if out is None else jnp.where(sub8 == x, turned, out)
        return out

    def around_z(v, e):
        f, l = (first, last) if v.shape[0] == BY else (first8, last8)
        return jnp.where(l, e, turn(v, -1)), jnp.where(f, e, turn(v, 1))

    def around_y(f, x):
        return field[f, x + 2, 9:41, :], field[f, x + 2, 7:39, :]

    def centre(f, x):
        return field[f, x + 2, ROWS, :]

    def row_of_field(f, r):
        return field[f, 2:10, r, :]

    def diagonal(side, q):
        a, b, _ = side
        lo, hi = ((XZ + YZ).index((a, b, c)) for c in SIGNS)
        return pair(dz[lo, q], dz[hi, q])

    xm_side, xp_side, ym_side, yp_side, zm_side, zp_side = SIDES[:6]

    for copy in loads[0:3]:
        copy.wait()
    where = wc[...]
    row_at = where // BZ
    lane_at = where - row_at * BZ
    code = jnp.where(wf[...] > 0, wf[...] + 4 * (wn[...] // 2), 0).astype(jnp.float32)
    up256 = lax.broadcasted_iota(jnp.int32, (BX * BY, BZ), 0)
    up128 = lax.broadcasted_iota(jnp.int32, (BZ, BZ), 0)
    for s in range(SLOTS):
        hot_row[:, s * BZ : (s + 1) * BZ] = jnp.where(up256 == row_at[s : s + 1], 1.0, 0.0).astype(jnp.bfloat16)
        hot_lane[:, s * BZ : (s + 1) * BZ] = jnp.where(up128 == lane_at[s : s + 1], code[s : s + 1], 0.0).astype(jnp.bfloat16)
    grid[...] = lax.dot_general(
        hot_row[...], hot_lane[...], (((1,), (1,)), ((), ())), preferred_element_type=jnp.float32
    )
    for copy in loads[3:]:
        copy.wait()

    t_b = t_c = t_u0 = t_u1 = t_u2 = None
    for x in range(BX):
        a = av[x]
        g = grid[x * BY : (x + 1) * BY, :]
        not_x = g > 3.5
        is_z = g > 7.5
        s = g - jnp.where(not_x, 4.0, 0.0) - jnp.where(is_z, 4.0, 0.0)
        u0, u1, u2 = centre(U0, x), centre(U1, x), centre(U2, x)
        parallel = (
            jnp.where(not_x, u0 * u0, 0.0)
            + jnp.where(not_x & jnp.logical_not(is_z), 0.0, u1 * u1)
            + jnp.where(is_z, 0.0, u2 * u2)
        )
        speed = jnp.sqrt(parallel + 0.25)
        liquid = 1.0 - a
        evap = 1.5 * a * s * s
        root = jnp.where(s > 1.5, 2.0 * 1.4142135623730951, s)
        heat[x] = liquid * speed * s + 0.6 * liquid * root + evap
        slope = jnp.where(row32 == BY - 1, 0.0, turn(u1, -1, 0)) - jnp.where(row32 == 0, 0.0, turn(u1, 1, 0))
        slope = slope + (jnp.where(last, 0.0, turn(u2, -1)) - jnp.where(first, 0.0, turn(u2, 1)))
        if x < BX - 1:
            slope = slope + centre(U0, x + 1)
        if x > 0:
            slope = slope - centre(U0, x - 1)
        b = EXPANSION * (0.5 * evap) - 0.5 * slope
        field[BP, x + 2, ROWS, :] = b
        t_b = pack(b, t_b, x)
        t_c = pack(centre(C, x), t_c, x)
        t_u0 = pack(u0, t_u0, x)
        t_u1 = pack(u1, t_u1, x)
        t_u2 = pack(u2, t_u2, x)
    for i, t in ((TB, t_b), (TC, t_c), (TU0, t_u0), (TU1, t_u1), (TU2, t_u2)):
        tz[i] = t

    pl.semaphore_wait(barrier, len(greeted))
    send(FIRST)

    t_h = None
    half = 0.5 / SCALE
    for x in range(BX):
        t_h = pack(centre(H, x), t_h, x)
        c = centre(C, x)
        if x < BX - 1:
            cx[x + 2] = half * (c + centre(C, x + 1))
        cy[x + 1, 0:32] = half * (c + turn(c, 1, 0))
        czp[x + 1] = half * jnp.where(last, c, c + turn(c, -1))
        czm[x + 1] = half * jnp.where(first, c, c + turn(c, 1))
    tz[TH] = t_h
    send(ENTH)

    in_root_plane = (gz == ROOT[2]) & (core == ROOT[1] % 2)
    in_root_column = (gx == ROOT[0]) & (chip_y == ROOT[1] // 2)
    is_root = in_root_plane & in_root_column

    @pl.when(in_root_plane)
    def _():
        for partner in column:
            pl.semaphore_signal(ready, inc=1, device_id=partner, device_id_type=MESH)


    def low_high(v):
        return v[0:8], v[8:24], v[24:32]

    def y_ends(v, f, x):
        a, m, z = low_high(v)
        a = a + jnp.where(sub8 == 0, 0.5 * field[f, x + 2, 7:8, :], 0.0)
        z = z - jnp.where(sub8 == 7, 0.5 * field[f, x + 2, 40:41, :], 0.0)
        return jnp.concatenate([a, m, z], axis=0)

    receive(FIRST)
    s_u2 = swap(pair(tlo[TU2], thi[TU2]))
    s_c = swap(pair(tlo[TC], thi[TC]))
    for x in range(BX):
        b = centre(BP, x) + ends_half32 * ends(s_u2, x)
        b = y_ends(b, U1, x)
        if x == 0:
            b = b + 0.5 * field[U0, 1, ROWS, :]
        if x == BX - 1:
            b = b - 0.5 * field[U0, 10, ROWS, :]
        field[W0, x + 2, ROWS, :] = b
        c = centre(C, x)
        e = ends(s_c, x)
        czp[x + 1] = czp[x + 1] + jnp.where(last, half * e, 0.0)
        czm[x + 1] = czm[x + 1] + jnp.where(first, half * e, 0.0)
        cy[x + 1, 0:1] = half * (c[0:1] + field[C, x + 2, 7:8, :])
        cy[x + 1, 32:33] = half * (c[31:32] + field[C, x + 2, 40:41, :])
    cx[1] = half * (centre(C, 0) + centre(C, -1))
    cx[9] = half * (centre(C, 7) + centre(C, 8))
    for x, own, sign, side, inside in ((-1, 0, -0.5, xm_side, 7), (BX, BX - 1, 0.5, xp_side, 0)):
        b = centre(BP, x) + sign * centre(U0, own)
        b = y_ends(b, U1, x) + ends_half32 * ends(swap(diagonal(side, 2)), inside)
        field[W0, x + 2, ROWS, :] = jnp.where(has[side], b, 0.0)
    for r, own, sign, side in ((7, 8, -0.5, ym_side), (40, 39, 0.5, yp_side)):
        b = row_of_field(BP, r) + sign * row_of_field(U1, own)
        b = b + jnp.where(sub8 == 0, 0.5 * field[U0, 1, r : r + 1, :], 0.0)
        b = b - jnp.where(sub8 == 7, 0.5 * field[U0, 10, r : r + 1, :], 0.0)
        b = b + ends_half * ends_row(swap(diagonal(side, 1)), side[1])
        b = jnp.where(has[side], b, 0.0)
        for x in range(BX):
            field[W0, x + 2, r : r + 1, :] = b[x : x + 1]
    has_z = jnp.where(low_lane, has[zm_side].astype(jnp.float32), has[zp_side].astype(jnp.float32))

    def z_inside(t):
        return jnp.where(low_lane, turn(t, -1), turn(t, 1))

    def z_around_x(v, before, after):
        return (
            jnp.where(lane8 >= 112, turn(after, -16), turn(v, -16)),
            jnp.where(lane8 < 16, turn(before, 16), turn(v, 16)),
        )

    def z_around_y(v, before, after):
        up = jnp.where(y_group == 3, turn(after, 12), turn(v, -4))
        down = jnp.where(y_group == 0, turn(before, -12), turn(v, 4))
        return (
            turn(jnp.where(sub8 == 0, up, v), -1, 0),
            turn(jnp.where(sub8 == 7, down, v), 1, 0),
        )

    zero = jnp.zeros((8, BZ), jnp.float32)
    after, before = z_around_x(zero, diagonal(xm_side, 0), diagonal(xp_side, 0))
    b = pair(tlo[TB], thi[TB]) - 0.5 * (after - before)
    after, before = z_around_y(zero, diagonal(ym_side, 3), diagonal(yp_side, 3))
    b = b - 0.5 * (after - before) + jnp.where(low_lane, -0.5, 0.5) * z_inside(tz[TU2])
    s_w0 = swap(has_z * b)

    def operator(f, x, e):
        v = centre(f, x)
        yp, ym = around_y(f, x)
        zp, zm = around_z(v, e)
        out = cx[x + 2] * (v - centre(f, x + 1)) + cx[x + 1] * (v - centre(f, x - 1))
        out = out + (cy[x + 1, 1:33] * (v - yp) + cy[x + 1, 0:32] * (v - ym))
        return out + (czp[x + 1] * (v - zp) + czm[x + 1] * (v - zm))

    t_w = None
    for x in range(BX):
        out = operator(W0, x, ends(s_w0, x))
        field[W1, x + 2, ROWS, :] = out
        t_w = pack(out, t_w, x)
    tz[TW] = t_w
    send(IMAGE)

    def fold(v):
        return (v[0:8] + v[8:16]) + (v[16:24] + v[24:32])

    def plus(acc, v):
        v = fold(v)
        return v if acc is None else acc + v

    m = [None] * 6
    for x in range(BX):
        v, out = centre(W0, x), centre(W1, x)
        m[0], m[1], m[2] = plus(m[0], v * v), plus(m[1], v * out), plus(m[2], out * out)
    for x, side, inside in ((-1, xm_side, 7), (BX, xp_side, 0)):
        c = centre(C, x)
        if x < 0:
            cx[0] = half * (c + centre(C, -2))
        else:
            cx[10] = half * (c + centre(C, 9))
        after, before = around_y(C, x)
        cy[x + 1, 0:32] = half * (c + before)
        cy[x + 1, 32:33] = half * (c[31:32] + after[31:32])
        after, before = around_z(c, ends(swap(diagonal(side, 1)), inside))
        czp[x + 1] = half * (c + after)
        czm[x + 1] = half * (c + before)
    z_edge = jnp.where(has[zm_side], 0.0, 1.0)
    y_edge = jnp.where(has[ym_side], 0.0, 1.0)
    x_edge = jnp.where(has[xm_side], 0.0, 1.0)
    for x in range(BX):
        low = jnp.where(first, czm[x + 1], 0.0) * z_edge
        low = low + jnp.where(row32 == 0, cy[x + 1, 0:32], 0.0) * y_edge
        if x == 0:
            low = low + cx[1] * x_edge
        zlow[x] = low

    receive(IMAGE)
    s_w1 = swap(pair(tlo[TW], thi[TW]))
    for x in range(BX):
        out = operator(W1, x, ends(s_w1, x))
        field[W2, x + 2, ROWS, :] = out
        v = centre(W1, x)
        m[3], m[4] = plus(m[3], v * out), plus(m[4], out * out)

    def image_plane(x, side, inside):
        out = operator(W1, x, ends(swap(diagonal(side, 4)), inside))
        field[W2, x + 2, ROWS, :] = jnp.where(has[side], out, 0.0)

    def image_row(r, beyond, own, side):
        sums = []
        c, v = row_of_field(C, r), row_of_field(W1, r)

        def term(cn, vn):
            return (c + cn) * (v - vn)

        out = term(row_of_field(C, beyond), row_of_field(W1, beyond)) + term(row_of_field(C, own), row_of_field(W1, own))
        both = []
        for f, q, values in ((C, 0, c), (W1, 4, v)):
            after = jnp.where(sub8 == 7, field[f, 10, r : r + 1, :], turn(values, -1, 0))
            before = jnp.where(sub8 == 0, field[f, 1, r : r + 1, :], turn(values, 1, 0))
            zp, zm = around_z(values, ends_row(swap(diagonal(side, q)), side[1]))
            both.append((after, before, zp, zm))
        for cn, vn in zip(*both):
            out = out + term(cn, vn)
        out = jnp.where(has[side], half * out, 0.0)
        for x in range(BX):
            field[W2, x + 2, r : r + 1, :] = out[x : x + 1]

    def image_face():
        both = []
        for t, qx, qy in ((TC, 1, 0), (TW, 4, 4)):
            lo, hi, own = tlo[t], thi[t], tz[t]
            v = pair(lo, hi)
            outer = jnp.where(low_lane, turn(lo, 1), turn(hi, -1))
            both.append(
                (v, outer, z_inside(own))
                + z_around_x(v, diagonal(xm_side, qx), diagonal(xp_side, qx))
                + z_around_y(v, diagonal(ym_side, qy), diagonal(yp_side, qy))
            )
        (c, *near_c), (v, *near_v) = both
        out = zero
        for cn, vn in zip(near_c, near_v):
            out = out + (c + cn) * (v - vn)
        return swap(has_z * (half * out))

    image_plane(BX, xp_side, 0)
    image_row(40, 41, 39, yp_side)
    s_w2 = image_face()
    for x in range(BX):
        v = centre(W2, x)
        dx = v - centre(W2, x + 1)
        dy = v - field[W2, x + 2, 9:41, :]
        dz_ = v - jnp.where(last, ends(s_w2, x), turn(v, -1))
        m[5] = plus(
            m[5],
            (cx[x + 2] * (dx * dx) + cy[x + 1, 1:33] * (dy * dy)) + (czp[x + 1] * (dz_ * dz_) + zlow[x] * (v * v)),
        )

    row = jnp.zeros((1, BZ), jnp.float32)
    for i in range(6):
        row = jnp.where(lane8[0:1] == i, jnp.sum(m[i], keepdims=True), row)

    def sum_copy(phase, slot, partner):
        return pltpu.make_async_remote_copy(
            src_ref=reduce.at[phase, pl.ds(0, 1)], dst_ref=reduce.at[phase, pl.ds(slot + 1, 1)],
            send_sem=sum_send.at[phase], recv_sem=sum_recv.at[phase], device_id=partner, device_id_type=MESH,
        )

    def sum_whole(phase, count):
        ref = tally.at[pl.ds(0, count)]
        return pltpu.make_async_remote_copy(
            src_ref=ref, dst_ref=ref, send_sem=sum_send.at[phase], recv_sem=sum_recv.at[phase],
            device_id=plane[0], device_id_type=MESH,
        )

    def start_sum(phase, group):
        for slot, partner in enumerate(group):
            sum_copy(phase, slot, partner).start()

    me = (gx * NGY + gy) * NGZ + gz
    to_root = pltpu.make_async_remote_copy(
        src_ref=reduce.at[0, pl.ds(0, 1)], dst_ref=direct.at[me], send_sem=sum_send.at[2],
        recv_sem=sum_recv.at[2], device_id=ROOT, device_id_type=MESH,
    )

    @pl.when(jnp.logical_not(in_root_plane))
    def _():
        pl.semaphore_wait(ready, 1)

    reduce[0, 0:1, :] = row
    pl.when(jnp.logical_not(is_root))(to_root.start)
    start_sum(0, plane)
    image_plane(-1, xm_side, 7)
    image_row(7, 6, 8, ym_side)
    copy_u = pltpu.make_async_copy(field.at[(U0,) + inner], u_out.at[0], copy_sem.at[0])
    copy_u.start()
    copy_v = pltpu.make_async_copy(field.at[(pl.ds(U1, 2),) + inner], u_out.at[pl.ds(1, 2)], copy_sem.at[2])
    copy_v.start()
    copy_w = pltpu.make_async_copy(field.at[(pl.ds(W0, 3),) + inner], w_out, copy_sem.at[1])
    copy_w.start()
    for i, (f, swapped) in enumerate(((W0, s_w0), (W1, s_w1), (W2, s_w2))):
        for x in range(BX):
            c = (0.5 / SCALE) * centre(C, x)
            g_out[i, 0, x] = c * (centre(f, x + 1) - centre(f, x - 1))
            after, before = around_y(f, x)
            g_out[i, 1, x] = c * (after - before)
            after, before = around_z(centre(f, x), ends(swapped, x))
            g_out[i, 2, x] = c * (after - before)
    receive(ENTH)
    s_h = swap(pair(tlo[TH], thi[TH]))
    for x in range(BX):
        h = centre(H, x)
        hyp, hym = around_y(H, x)
        hzp, hzm = around_z(h, ends(s_h, x))
        laplace = centre(H, x + 1) + centre(H, x - 1) + hyp + hym + hzp + hzm - 6.0 * h
        h_out[x] = h + DIFFUSE * laplace + HEATING * heat[x]
    copy_u.wait()
    copy_v.wait()
    copy_w.wait()
    for kind in range(3):
        whole(kind).wait_send()

    sum_whole(0, 15).wait_recv()
    high, low = row_total(reduce[0])
    reduce[1, 0:1, :] = jnp.where(lane8 < 8, high, turn(low, 8))[0:1]

    @pl.when(jnp.logical_not(in_root_column) | is_root)
    def _():
        start_sum(1, column)

    @pl.when(in_root_column & jnp.logical_not(is_root))
    def _():
        for slot, partner in enumerate(column):
            pl.when((partner[1] != ROOT[1]) | (partner[2] != ROOT[2]))(sum_copy(1, slot, partner).start)

    @pl.when(is_root)
    def _():
        direct[(ROOT[0] * NGY + ROOT[1]) * NGZ + ROOT[2]] = row
        sum_whole(2, DEVICES - 1).wait_recv()
        high, low = row_total(direct[...].reshape(DEVICES, BZ))
        total[0] = high
        total[1] = low

    @pl.when(jnp.logical_not(is_root))
    def _():
        sum_whole(1, 15).wait_recv()
        high, low = row_total(reduce[1])
        total[0] = high
        total[1] = low + turn(high, -8)

    high, low = total[0], total[1]
    high, low = quick_sum(high, low)

    def spread(v, i):
        return jnp.broadcast_to(v[:, i : i + 1], (8, BZ))

    moments = [(spread(high, i), spread(low, i)) for i in range(6)]
    for i, v in enumerate(solve_moments(moments)):
        c_out[i] = v
    sum_whole(0, 15).wait_send()

    @pl.when(in_root_column & jnp.logical_not(is_root))
    def _():
        sum_whole(1, 14).wait_send()

    @pl.when(jnp.logical_not(in_root_column) | is_root)
    def _():
        sum_whole(1, 15).wait_send()

    pl.when(jnp.logical_not(is_root))(to_root.wait_send)


def finish(w, g, u, h, c, vel_out, p_out, h_out, vel, p, sem):
    copy_h = pltpu.make_async_copy(h, h_out, sem.at[0])
    copy_h.start()
    c0, c1, c2 = (jnp.concatenate([c[i]] * 4, axis=0) for i in range(3))
    copies = [copy_h]
    for i in range(3):
        for x in range(BX):
            vel[i, x] = u[i, x] - (c0 * g[0, i, x] + c1 * g[1, i, x] + c2 * g[2, i, x])
        copy = pltpu.make_async_copy(vel.at[i], vel_out.at[i], sem.at[1 + i])
        copy.start()
        copies.append(copy)
    scaled = tuple(v * (1.0 / SCALE) for v in (c0, c1, c2))
    for x in range(BX):
        p[x] = scaled[0] * w[0, x] + scaled[1] * w[1, x] + scaled[2] * w[2, x]
    copy_p = pltpu.make_async_copy(p, p_out, sem.at[4])
    copy_p.start()
    for copy in copies + [copy_p]:
        copy.wait()


def shards(*args):
    block = (BX, BY, BZ)
    f32 = jnp.float32
    any_ref = pl.BlockSpec(memory_space=pl.ANY)
    vmem = pl.BlockSpec(memory_space=pltpu.VMEM)
    results = pl.pallas_call(
        kernel,
        out_shape=(
            jax.ShapeDtypeStruct((3,) + block, f32),
            jax.ShapeDtypeStruct((3, 3) + block, f32),
            jax.ShapeDtypeStruct((3,) + block, f32),
            jax.ShapeDtypeStruct(block, f32),
            jax.ShapeDtypeStruct((3, 8, BZ), f32),
        ),
        in_specs=[any_ref] * 7,
        out_specs=(vmem,) * 5,
        scratch_shapes=[
            pltpu.VMEM((FIELDS, BX + 4, BY + 16, BZ), f32),
            pltpu.VMEM((7, 8, BZ), f32),
            pltpu.VMEM((7, 8, BZ), f32),
            pltpu.VMEM((7, 8, BZ), f32),
            pltpu.VMEM((8, 5, 8, BZ), f32),
            pltpu.VMEM((BX + 3, BY, BZ), f32),
            pltpu.VMEM((BX + 2, BY + 8, BZ), f32),
            pltpu.VMEM((BX + 2, BY, BZ), f32),
            pltpu.VMEM((BX + 2, BY, BZ), f32),
            pltpu.VMEM(block, f32),
            pltpu.VMEM(block, f32),
            pltpu.VMEM((SLOTS, BZ), jnp.int32),
            pltpu.VMEM((SLOTS, BZ), jnp.int32),
            pltpu.VMEM((SLOTS, BZ), jnp.int32),
            pltpu.VMEM((BX * BY, SLOTS * BZ), jnp.bfloat16),
            pltpu.VMEM((BZ, SLOTS * BZ), jnp.bfloat16),
            pltpu.VMEM((BX * BY, BZ), f32),
            pltpu.VMEM(block, f32),
            pltpu.VMEM((2, 16, BZ), f32),
            pltpu.VMEM((DEVICES, 1, BZ), f32),
            pltpu.VMEM((2, 8, BZ), f32),
            pltpu.VMEM((1024, BZ), f32),
            pltpu.SemaphoreType.DMA((8,)),
            pltpu.SemaphoreType.DMA((3,)),
            pltpu.SemaphoreType.DMA((3,)),
            pltpu.SemaphoreType.DMA((3,)),
            pltpu.SemaphoreType.DMA((3,)),
            pltpu.SemaphoreType.DMA((3,)),
            pltpu.SemaphoreType.REGULAR,
        ],
        compiler_params=pltpu.CompilerParams(
            collective_id=0, has_side_effects=True, vmem_limit_bytes=32 * 1024 * 1024
        ),
        name="simple_step",
    )(*[pltpu.with_memory_space_constraint(a, pltpu.HBM) for a in args])
    results = [pltpu.with_memory_space_constraint(r, pltpu.VMEM) for r in results]
    return tuple(
        pl.pallas_call(
            finish,
            out_shape=(
                jax.ShapeDtypeStruct((3,) + block, f32),
                jax.ShapeDtypeStruct(block, f32),
                jax.ShapeDtypeStruct(block, f32),
            ),
            in_specs=[vmem] * 5,
            out_specs=(pl.BlockSpec(memory_space=pltpu.HBM),) * 3,
            scratch_shapes=[
                pltpu.VMEM((3,) + block, f32),
                pltpu.VMEM(block, f32),
                pltpu.SemaphoreType.DMA((5,)),
            ],
            compiler_params=pltpu.CompilerParams(vmem_limit_bytes=8 * 1024 * 1024),
            name="finish",
        )(*results)
    )


def solution(mesh):
    in_specs = (
        P(None, "gx", "gy", "gz"),
        P("gx", "gy", "gz"),
        P("gx", "gy", "gz"),
        P("gx", "gy", "gz"),
        P(("gx", "gy", "gz"), None),
        P(("gx", "gy", "gz"), None),
        P(("gx", "gy", "gz"), None),
    )
    out_specs = (P(None, "gx", "gy", "gz"), P("gx", "gy", "gz"), P("gx", "gy", "gz"))
    return jax.shard_map(shards, mesh=mesh, in_specs=in_specs, out_specs=out_specs, check_vma=False)
```

```python
import math

import jax
import jax.numpy as jnp
from jax import lax
from jax.experimental import pallas as pl
from jax.experimental.pallas import tpu as pltpu
from jax.sharding import PartitionSpec as P

MESH = pl.DeviceIdType.MESH
NGX, NGY, NGZ = 4, 8, 8
BX, BY, BZ = 8, 32, 128
SLOTS = 16
DIFFUSE = 0.1
HEATING = 0.5
EXPANSION = 1.5
SCALE = 16.0
H, C, U0, BP, U1, U2, W0, W1, W2 = range(9)
FIELDS = 9
TU0, TC, TU2, TB, TU1, TH, TW = range(7)
ROWS = slice(8, 40)
SIGNS = (-1, 1)
XZ = tuple((a, 0, c) for a in SIGNS for c in SIGNS)
YZ = tuple((0, b, c) for b in SIGNS for c in SIGNS)
XY = tuple((a, b, 0) for a in SIGNS for b in SIGNS)
SIDES = ((-1, 0, 0), (1, 0, 0), (0, -1, 0), (0, 1, 0), (0, 0, -1), (0, 0, 1)) + XY + XZ + YZ
FIRST, ENTH, IMAGE = range(3)
PIVOT_FLOOR = 1e-9
ROOT = (0, 1, 0)
DEVICES = 256


def two_sum(a, b):
    s = a + b
    t = s - a
    return s, (a - (s - t)) + (b - t)


def quick_sum(a, b):
    s = a + b
    return s, b - (s - a)


def split(a):
    t = 4097.0 * a
    high = t - (t - a)
    return high, a - high


def two_mul(a, b):
    p = a * b
    ah, al = split(a)
    bh, bl = split(b)
    return p, ((ah * bh - p) + ah * bl + al * bh) + al * bl


def df_sub(a, b):
    s, e = two_sum(a[0], -b[0])
    return quick_sum(s, e + (a[1] - b[1]))


def df_mul(a, b):
    p, e = two_mul(a[0], b[0])
    return quick_sum(p, e + (a[0] * b[1] + a[1] * b[0]))


def df_over(a, b, inverse):
    q = a[0] * inverse
    p, e = two_mul(q, b[0])
    rest = ((a[0] - p) - e) + (a[1] - q * b[1])
    return quick_sum(q, rest * inverse)


def solve_moments(m):
    i0 = 1.0 / m[1][0]
    l10 = df_over(m[2], m[1], i0)
    l20 = df_over(m[3], m[1], i0)
    d1 = df_sub(m[3], df_mul(l10, m[2]))
    e12 = df_sub(m[4], df_mul(l10, m[3]))
    y1 = df_sub(m[1], df_mul(l10, m[0]))
    y2 = df_sub(m[2], df_mul(l20, m[0]))
    d2 = df_sub(m[5], df_mul(l20, m[3]))
    ok1 = d1[0] > PIVOT_FLOOR * m[3][0]
    i1 = jnp.where(ok1, 1.0 / d1[0], 0.0)
    l21 = df_over(e12, d1, i1)
    d2 = df_sub(d2, df_mul(l21, e12))
    y2 = df_sub(y2, df_mul(l21, y1))
    ok2 = ok1 & (d2[0] > PIVOT_FLOOR * m[5][0])
    c2 = jnp.where(ok2, y2[0] / d2[0], 0.0)
    p, e = two_mul(e12[0], c2)
    c1 = (((y1[0] - p) - e) + (y1[1] - e12[1] * c2)) * i1
    p1, e1 = two_mul(m[2][0], c1)
    p2, e2 = two_mul(m[3][0], c2)
    s, t1 = two_sum(m[0][0], -p1)
    s, t2 = two_sum(s, -p2)
    rest = (t1 - e1) + (t2 - e2) + (m[0][1] - m[2][1] * c1 - m[3][1] * c2)
    return (s + rest) * i0, c1, c2


def row_total(rows):
    parts = [(rows[i : i + 8], None) for i in range(0, rows.shape[0], 8)]
    while len(parts) > 1:
        merged = []
        for (a, low_a), (b, low_b) in zip(parts[0::2], parts[1::2]):
            s, e = two_sum(a, b)
            merged.append((s, e if low_a is None else e + (low_a + low_b)))
        parts = merged
    s, e = parts[0]
    for step in (4, 2, 1):
        other = pltpu.roll(s, step, axis=0)
        e = e + pltpu.roll(e, step, axis=0)
        s, more = two_sum(s, other)
        e = e + more
    return s, e


def opposite(side):
    return tuple(-v for v in side)


def messages(field, tz, tlo, thi, dz):
    xs, xd = {-1: 2, 1: 9}, {-1: 10, 1: 1}
    ys, yd = {-1: 8, 1: 39}, {-1: 40, 1: 7}
    xs2, xd2 = {-1: pl.ds(2, 2), 1: pl.ds(8, 2)}, {-1: pl.ds(10, 2), 1: pl.ds(0, 2)}
    ys2, yd2 = {-1: pl.ds(8, 2), 1: pl.ds(38, 2)}, {-1: pl.ds(40, 2), 1: pl.ds(6, 2)}
    rows, planes = pl.ds(8, BY), pl.ds(2, BX)
    table = [[], [], []]
    for side in XZ + YZ + XY + SIDES[:2] + SIDES[4:6] + SIDES[2:4]:
        a, b, c = side
        far = thi if c < 0 else tlo
        slot = (XZ + YZ).index(opposite(side)) if side in XZ + YZ else None
        enth = []
        if side in XZ:
            first = [(tz.at[pl.ds(TU0, 3)], dz.at[slot, pl.ds(0, 3)])]
            image = [(tz.at[TW], dz.at[slot, 4])]
        elif side in YZ:
            first = [(tz.at[pl.ds(TC, 4)], dz.at[slot, pl.ds(0, 4)])]
            image = [(tz.at[TW], dz.at[slot, 4])]
        elif side in XY:
            first = [(field.at[pl.ds(C, 4), xs[a], ys[b]], field.at[pl.ds(C, 4), xd[a], yd[b]])]
            image = [(field.at[W1, xs[a], ys[b]], field.at[W1, xd[a], yd[b]])]
        elif a:
            first = [
                (field.at[C, xs2[a], rows], field.at[C, xd2[a], rows]),
                (field.at[pl.ds(U0, 2), xs[a], rows], field.at[pl.ds(U0, 2), xd[a], rows]),
            ]
            enth = [(field.at[H, xs[a], rows], field.at[H, xd[a], rows])]
            image = [(field.at[W1, xs2[a], rows], field.at[W1, xd2[a], rows])]
        elif b:
            first = [
                (field.at[C, planes, ys2[b]], field.at[C, planes, yd2[b]]),
                (field.at[pl.ds(BP, 2), planes, ys[b]], field.at[pl.ds(BP, 2), planes, yd[b]]),
            ]
            enth = [(field.at[H, planes, ys[b]], field.at[H, planes, yd[b]])]
            image = [(field.at[W1, planes, ys2[b]], field.at[W1, planes, yd2[b]])]
        else:
            first = [(tz.at[pl.ds(TC, 3)], far.at[pl.ds(TC, 3)])]
            enth = [(tz.at[TH], far.at[TH])]
            image = [(tz.at[TW], far.at[TW])]
        for kind, pairs in ((FIRST, first), (ENTH, enth), (IMAGE, image)):
            table[kind] += [(side, src, dst) for src, dst in pairs]
    return table


def kernel(
    vel, coef, enth, void, cells, normal, flag,
    w_out, g_out, u_out, h_out, c_out,
    field, tz, tlo, thi, dz, cx, cy, czm, czp, zlow, av, wc, wn, wf, hot_row, hot_lane, grid,
    heat, reduce, direct, total, tally, load_sem, copy_sem, send_sem, recv_sem, sum_send, sum_recv, ready, wave,
):
    gx, gy, gz = lax.axis_index("gx"), lax.axis_index("gy"), lax.axis_index("gz")
    chip_y, core = gy // 2, lax.rem(gy, 2)

    has = dict(zip(SIDES[:6], (gx > 0, gx < NGX - 1, gy > 0, gy < NGY - 1, gz > 0, gz < NGZ - 1)))

    def beside(side):
        return tuple(
            lax.rem(at + step + size, size) if step else at
            for at, step, size in zip((gx, gy, gz), side, (NGX, NGY, NGZ))
        )

    def in_plane(i, j):
        return (lax.rem(gx + i, NGX), lax.rem(chip_y + j, NGY // 2) * 2 + core, gz)

    def in_column(k, j):
        return (gx, chip_y * 2 + lax.rem(core + j, 2), lax.rem(gz + k, NGZ))

    def far_first(pairs, n, m):
        return sorted(pairs, key=lambda p: -min(p[0], n - p[0]) - min(p[1], m - p[1]))

    plane_steps = far_first([(i, j) for i in range(NGX) for j in range(NGY // 2) if i or j], NGX, NGY // 2)
    column_steps = far_first([(k, j) for k in range(NGZ) for j in range(2) if k or j], NGZ, 2)
    plane = [in_plane(i, j) for i, j in plane_steps]
    column = [in_column(k, j) for k, j in column_steps]

    inner = (pl.ds(2, BX), pl.ds(8, BY))
    barrier = pltpu.get_barrier_semaphore()
    in_root_layer = gz == ROOT[2]
    in_root_column = (gx == ROOT[0]) & (chip_y == ROOT[1] // 2)
    is_root = in_root_layer & (gx == ROOT[0]) & (gy == ROOT[1])

    def signal(sem, partners):
        for partner in partners:
            pl.semaphore_signal(sem, inc=1, device_id=partner, device_id_type=MESH)

    near = [beside(side) for side in SIDES]
    signal(barrier, near)
    loads = [
        (cells, wc), (flag, wf), (normal, wn),
        (vel.at[0], field.at[(U0,) + inner]),
        (vel.at[pl.ds(1, 2)], field.at[(pl.ds(U1, 2),) + inner]),
        (void, av),
        (coef, field.at[(C,) + inner]),
        (enth, field.at[(H,) + inner]),
    ]
    loads = [pltpu.make_async_copy(s, d, load_sem.at[i]) for i, (s, d) in enumerate(loads)]
    for copy in loads:
        copy.start()

    @pl.when(is_root)
    def _():
        signal(barrier, [(x, y, ROOT[2]) for x in range(NGX) for y in range(NGY) if (x, y) != ROOT[:2]])

    table = messages(field, tz, tlo, thi, dz)
    copies = [
        [
            pltpu.make_async_remote_copy(
                src_ref=src, dst_ref=dst, send_sem=send_sem.at[kind], recv_sem=recv_sem.at[kind],
                device_id=beside(side), device_id_type=MESH,
            )
            for side, src, dst in table[kind]
        ]
        for kind in range(3)
    ]

    def whole(kind):
        count = sum(math.prod(dst.shape) for _, _, dst in table[kind]) // BZ
        ref = tally.at[pl.ds(0, count)]
        return pltpu.make_async_remote_copy(
            src_ref=ref, dst_ref=ref, send_sem=send_sem.at[kind], recv_sem=recv_sem.at[kind],
            device_id=beside(SIDES[0]), device_id_type=MESH,
        )

    def send(kind):
        for copy in copies[kind]:
            copy.start()

    def receive(kind):
        whole(kind).wait_recv()
        for side in SIDES[:6]:
            dim = [i for i in range(3) if side[i]][0]

            @pl.when(jnp.logical_not(has[side]))
            def _():
                for to, _, dst in table[kind]:
                    if to[dim] == -side[dim]:
                        dst[...] = jnp.zeros(dst.shape, jnp.float32)

    lane8 = lax.broadcasted_iota(jnp.int32, (8, BZ), 1)
    sub8 = lax.broadcasted_iota(jnp.int32, (8, BZ), 0)
    lane32 = lax.broadcasted_iota(jnp.int32, (BY, BZ), 1)
    row32 = lax.broadcasted_iota(jnp.int32, (BY, BZ), 0)
    first, last = lane32 == 0, lane32 == BZ - 1
    first8, last8 = lane8 == 0, lane8 == BZ - 1
    place = lane8 % 4
    low_lane = place == 1
    y_group = lane8 // 4 % 4
    ends_half = jnp.where(first8, 0.5, jnp.where(last8, -0.5, 0.0))
    ends_half32 = jnp.where(first, 0.5, jnp.where(last, -0.5, 0.0))

    def turn(v, by, axis=1):
        size = v.shape[axis]
        return pltpu.roll(v, by % size, axis=axis) if by % size else v

    def pack(values, acc, x):
        for b in range(4):
            k = 4 * x + b
            turned = turn(values[8 * b : 8 * b + 8], 4 * k + 2)
            acc = turned if acc is None else jnp.where(lane8 // 4 == k, turned, acc)
        return acc

    def pair(low, high):
        return jnp.where(low_lane, low, high)

    def swap(v):
        return jnp.where(low_lane, turn(v, -1), turn(v, 1))

    def ends(swapped, x):
        return jnp.concatenate([turn(swapped, -4 * (4 * x + b) - 2) for b in range(4)], axis=0)

    def ends_row(swapped, b):
        row, k = (7, 3) if b < 0 else (0, 0)
        out = None
        spread = jnp.broadcast_to(swapped[row : row + 1], (8, BZ))
        for x in range(BX):
            turned = turn(spread, -4 * (4 * x + k) - 2)
            out = turned if out is None else jnp.where(sub8 == x, turned, out)
        return out

    def around_z(v, e):
        f, l = (first, last) if v.shape[0] == BY else (first8, last8)
        return jnp.where(l, e, turn(v, -1)), jnp.where(f, e, turn(v, 1))

    def around_y(f, x):
        return field[f, x + 2, 9:41, :], field[f, x + 2, 7:39, :]

    def centre(f, x):
        return field[f, x + 2, ROWS, :]

    def row_of_field(f, r):
        return field[f, 2:10, r, :]

    def diagonal(side, q):
        a, b, _ = side
        lo, hi = ((XZ + YZ).index((a, b, c)) for c in SIGNS)
        return pair(dz[lo, q], dz[hi, q])

    xm_side, xp_side, ym_side, yp_side, zm_side, zp_side = SIDES[:6]

    for copy in loads[0:3]:
        copy.wait()
    where = wc[...]
    row_at = where // BZ
    lane_at = where - row_at * BZ
    code = jnp.where(wf[...] > 0, wf[...] + 4 * (wn[...] // 2), 0).astype(jnp.float32)
    up256 = lax.broadcasted_iota(jnp.int32, (BX * BY, BZ), 0)
    up128 = lax.broadcasted_iota(jnp.int32, (BZ, BZ), 0)
    for s in range(SLOTS):
        hot_row[:, s * BZ : (s + 1) * BZ] = jnp.where(up256 == row_at[s : s + 1], 1.0, 0.0).astype(jnp.bfloat16)
        hot_lane[:, s * BZ : (s + 1) * BZ] = jnp.where(up128 == lane_at[s : s + 1], code[s : s + 1], 0.0).astype(jnp.bfloat16)
    grid[...] = lax.dot_general(
        hot_row[...], hot_lane[...], (((1,), (1,)), ((), ())), preferred_element_type=jnp.float32
    )
    for copy in loads[3:]:
        copy.wait()

    t_b = t_c = t_u0 = t_u1 = t_u2 = None
    for x in range(BX):
        a = av[x]
        g = grid[x * BY : (x + 1) * BY, :]
        not_x = g > 3.5
        is_z = g > 7.5
        s = g - jnp.where(not_x, 4.0, 0.0) - jnp.where(is_z, 4.0, 0.0)
        u0, u1, u2 = centre(U0, x), centre(U1, x), centre(U2, x)
        parallel = (
            jnp.where(not_x, u0 * u0, 0.0)
            + jnp.where(not_x & jnp.logical_not(is_z), 0.0, u1 * u1)
            + jnp.where(is_z, 0.0, u2 * u2)
        )
        speed = jnp.sqrt(parallel + 0.25)
        liquid = 1.0 - a
        evap = 1.5 * a * s * s
        root = jnp.where(s > 1.5, 2.0 * 1.4142135623730951, s)
        heat[x] = liquid * speed * s + 0.6 * liquid * root + evap
        slope = jnp.where(row32 == BY - 1, 0.0, turn(u1, -1, 0)) - jnp.where(row32 == 0, 0.0, turn(u1, 1, 0))
        slope = slope + (jnp.where(last, 0.0, turn(u2, -1)) - jnp.where(first, 0.0, turn(u2, 1)))
        if x < BX - 1:
            slope = slope + centre(U0, x + 1)
        if x > 0:
            slope = slope - centre(U0, x - 1)
        b = EXPANSION * (0.5 * evap) - 0.5 * slope
        field[BP, x + 2, ROWS, :] = b
        t_b = pack(b, t_b, x)
        t_c = pack(centre(C, x), t_c, x)
        t_u0 = pack(u0, t_u0, x)
        t_u1 = pack(u1, t_u1, x)
        t_u2 = pack(u2, t_u2, x)
    for i, t in ((TB, t_b), (TC, t_c), (TU0, t_u0), (TU1, t_u1), (TU2, t_u2)):
        tz[i] = t

    pl.semaphore_wait(barrier, len(near) + (in_root_layer & jnp.logical_not(is_root)).astype(jnp.int32))
    send(FIRST)
    signal(wave.at[0], [beside(side) for side in SIDES[:6]])

    t_h = None
    half = 0.5 / SCALE
    for x in range(BX):
        t_h = pack(centre(H, x), t_h, x)
        c = centre(C, x)
        if x < BX - 1:
            cx[x + 2] = half * (c + centre(C, x + 1))
        cy[x + 1, 0:32] = half * (c + turn(c, 1, 0))
        czp[x + 1] = half * jnp.where(last, c, c + turn(c, -1))
        czm[x + 1] = half * jnp.where(first, c, c + turn(c, 1))
    tz[TH] = t_h
    send(ENTH)

    pl.semaphore_wait(wave.at[0], 6)
    second = [(0, 2, 0), (0, -2, 0), (0, 0, 2), (0, 0, -2)]
    signal(wave.at[1], [beside(step) for step in second])

    def low_high(v):
        return v[0:8], v[8:24], v[24:32]

    def y_ends(v, f, x):
        a, m, z = low_high(v)
        a = a + jnp.where(sub8 == 0, 0.5 * field[f, x + 2, 7:8, :], 0.0)
        z = z - jnp.where(sub8 == 7, 0.5 * field[f, x + 2, 40:41, :], 0.0)
        return jnp.concatenate([a, m, z], axis=0)

    has_z = jnp.where(low_lane, has[zm_side].astype(jnp.float32), has[zp_side].astype(jnp.float32))

    def z_inside(t):
        return jnp.where(low_lane, turn(t, -1), turn(t, 1))

    def z_around_x(v, before, after):
        return (
            jnp.where(lane8 >= 112, turn(after, -16), turn(v, -16)),
            jnp.where(lane8 < 16, turn(before, 16), turn(v, 16)),
        )

    def z_around_y(v, before, after):
        up = jnp.where(y_group == 3, turn(after, 12), turn(v, -4))
        down = jnp.where(y_group == 0, turn(before, -12), turn(v, 4))
        return (
            turn(jnp.where(sub8 == 0, up, v), -1, 0),
            turn(jnp.where(sub8 == 7, down, v), 1, 0),
        )

    zero = jnp.zeros((8, BZ), jnp.float32)
    receive(FIRST)
    after, before = z_around_x(zero, diagonal(xm_side, 0), diagonal(xp_side, 0))
    b = pair(tlo[TB], thi[TB]) - 0.5 * (after - before)
    after, before = z_around_y(zero, diagonal(ym_side, 3), diagonal(yp_side, 3))
    b = b - 0.5 * (after - before) + jnp.where(low_lane, -0.5, 0.5) * z_inside(tz[TU2])
    s_w0 = swap(has_z * b)

    s_u2 = swap(pair(tlo[TU2], thi[TU2]))
    s_c = swap(pair(tlo[TC], thi[TC]))
    for x in range(BX):
        b = centre(BP, x) + ends_half32 * ends(s_u2, x)
        b = y_ends(b, U1, x)
        if x == 0:
            b = b + 0.5 * field[U0, 1, ROWS, :]
        if x == BX - 1:
            b = b - 0.5 * field[U0, 10, ROWS, :]
        field[W0, x + 2, ROWS, :] = b
        c = centre(C, x)
        e = ends(s_c, x)
        czp[x + 1] = czp[x + 1] + jnp.where(last, half * e, 0.0)
        czm[x + 1] = czm[x + 1] + jnp.where(first, half * e, 0.0)
        cy[x + 1, 0:1] = half * (c[0:1] + field[C, x + 2, 7:8, :])
        cy[x + 1, 32:33] = half * (c[31:32] + field[C, x + 2, 40:41, :])
    cx[1] = half * (centre(C, 0) + centre(C, -1))
    cx[9] = half * (centre(C, 7) + centre(C, 8))
    for x, own, sign, side, inside in ((-1, 0, -0.5, xm_side, 7), (BX, BX - 1, 0.5, xp_side, 0)):
        b = centre(BP, x) + sign * centre(U0, own)
        b = y_ends(b, U1, x) + ends_half32 * ends(swap(diagonal(side, 2)), inside)
        field[W0, x + 2, ROWS, :] = jnp.where(has[side], b, 0.0)
    for r, own, sign, side in ((7, 8, -0.5, ym_side), (40, 39, 0.5, yp_side)):
        b = row_of_field(BP, r) + sign * row_of_field(U1, own)
        b = b + jnp.where(sub8 == 0, 0.5 * field[U0, 1, r : r + 1, :], 0.0)
        b = b - jnp.where(sub8 == 7, 0.5 * field[U0, 10, r : r + 1, :], 0.0)
        b = b + ends_half * ends_row(swap(diagonal(side, 1)), side[1])
        b = jnp.where(has[side], b, 0.0)
        for x in range(BX):
            field[W0, x + 2, r : r + 1, :] = b[x : x + 1]
    def operator(f, x, e):
        v = centre(f, x)
        yp, ym = around_y(f, x)
        zp, zm = around_z(v, e)
        out = cx[x + 2] * (v - centre(f, x + 1)) + cx[x + 1] * (v - centre(f, x - 1))
        out = out + (cy[x + 1, 1:33] * (v - yp) + cy[x + 1, 0:32] * (v - ym))
        return out + (czp[x + 1] * (v - zp) + czm[x + 1] * (v - zm))

    t_w = None
    for x in range(BX):
        out = operator(W0, x, ends(s_w0, x))
        field[W1, x + 2, ROWS, :] = out
        t_w = pack(out, t_w, x)
    tz[TW] = t_w
    send(IMAGE)

    def fold(v):
        return (v[0:8] + v[8:16]) + (v[16:24] + v[24:32])

    def plus(acc, v):
        v = fold(v)
        return v if acc is None else acc + v

    m = [None] * 6
    for x in range(BX):
        v, out = centre(W0, x), centre(W1, x)
        m[0], m[1], m[2] = plus(m[0], v * v), plus(m[1], v * out), plus(m[2], out * out)
    for x, side, inside in ((-1, xm_side, 7), (BX, xp_side, 0)):
        c = centre(C, x)
        if x < 0:
            cx[0] = half * (c + centre(C, -2))
        else:
            cx[10] = half * (c + centre(C, 9))
        after, before = around_y(C, x)
        cy[x + 1, 0:32] = half * (c + before)
        cy[x + 1, 32:33] = half * (c[31:32] + after[31:32])
        after, before = around_z(c, ends(swap(diagonal(side, 1)), inside))
        czp[x + 1] = half * (c + after)
        czm[x + 1] = half * (c + before)
    z_edge = jnp.where(has[zm_side], 0.0, 1.0)
    y_edge = jnp.where(has[ym_side], 0.0, 1.0)
    x_edge = jnp.where(has[xm_side], 0.0, 1.0)
    for x in range(BX):
        low = jnp.where(first, czm[x + 1], 0.0) * z_edge
        low = low + jnp.where(row32 == 0, cy[x + 1, 0:32], 0.0) * y_edge
        if x == 0:
            low = low + cx[1] * x_edge
        zlow[x] = low

    def face_values(t, qx, qy):
        lo, hi, own = tlo[t], thi[t], tz[t]
        v = pair(lo, hi)
        outer = jnp.where(low_lane, turn(lo, 1), turn(hi, -1))
        return (
            (v, outer, z_inside(own))
            + z_around_x(v, diagonal(xm_side, qx), diagonal(xp_side, qx))
            + z_around_y(v, diagonal(ym_side, qy), diagonal(yp_side, qy))
        )

    def row_values(f, q, r, beyond, own, side):
        v = row_of_field(f, r)
        after = jnp.where(sub8 == 7, field[f, 10, r : r + 1, :], turn(v, -1, 0))
        before = jnp.where(sub8 == 0, field[f, 1, r : r + 1, :], turn(v, 1, 0))
        zp, zm = around_z(v, ends_row(swap(diagonal(side, q)), side[1]))
        return v, row_of_field(f, beyond), row_of_field(f, own), after, before, zp, zm

    def weights(values, mask):
        c, *near_c = values
        return [mask * (half * (c + cn)) for cn in near_c]

    def applied(weight, values):
        v, *near_v = values
        terms = [w * (v - vn) for w, vn in zip(weight, near_v)]
        return ((terms[0] + terms[1]) + (terms[2] + terms[3])) + (terms[4] + terms[5])

    face_weights = weights(face_values(TC, 1, 0), has_z)
    rows_beyond = ((7, 6, 8, ym_side), (40, 41, 39, yp_side))
    row_weights = [weights(row_values(C, 0, *at), has[at[3]].astype(jnp.float32)) for at in rows_beyond]

    def image_row(at):
        out = applied(row_weights[at], row_values(W1, 4, *rows_beyond[at]))
        r = rows_beyond[at][0]
        for x in range(BX):
            field[W2, x + 2, r : r + 1, :] = out[x : x + 1]

    pl.semaphore_wait(wave.at[1], len(second))
    signal(wave.at[2], [in_plane(i, 0) for i in range(1, NGX)] + [in_column(0, 1)])

    @pl.when(in_root_layer)
    def _():
        signal(ready, [in_column(k, 0) for k in range(1, NGZ)])

    receive(IMAGE)
    s_w2 = swap(applied(face_weights, face_values(TW, 4, 4)))
    image_row(1)
    s_w1 = swap(pair(tlo[TW], thi[TW]))
    for x in range(BX):
        out = operator(W1, x, ends(s_w1, x))
        field[W2, x + 2, ROWS, :] = out
        v = centre(W1, x)
        m[3], m[4] = plus(m[3], v * out), plus(m[4], out * out)

    def image_plane(x, side, inside):
        out = operator(W1, x, ends(swap(diagonal(side, 4)), inside))
        field[W2, x + 2, ROWS, :] = jnp.where(has[side], out, 0.0)

    image_plane(BX, xp_side, 0)
    for x in range(BX):
        v = centre(W2, x)
        dx = v - centre(W2, x + 1)
        dy = v - field[W2, x + 2, 9:41, :]
        dz_ = v - jnp.where(last, ends(s_w2, x), turn(v, -1))
        m[5] = plus(
            m[5],
            (cx[x + 2] * (dx * dx) + cy[x + 1, 1:33] * (dy * dy)) + (czp[x + 1] * (dz_ * dz_) + zlow[x] * (v * v)),
        )

    row = jnp.zeros((1, BZ), jnp.float32)
    for i in range(6):
        row = jnp.where(lane8[0:1] == i, jnp.sum(m[i], keepdims=True), row)

    def sum_copy(phase, slot, partner):
        return pltpu.make_async_remote_copy(
            src_ref=reduce.at[phase, pl.ds(0, 1)], dst_ref=reduce.at[phase, pl.ds(slot + 1, 1)],
            send_sem=sum_send.at[phase], recv_sem=sum_recv.at[phase], device_id=partner, device_id_type=MESH,
        )

    def sum_whole(phase, count):
        ref = tally.at[pl.ds(0, count)]
        return pltpu.make_async_remote_copy(
            src_ref=ref, dst_ref=ref, send_sem=sum_send.at[phase], recv_sem=sum_recv.at[phase],
            device_id=plane[0], device_id_type=MESH,
        )

    def start_sum(phase, group):
        for slot, partner in enumerate(group):
            sum_copy(phase, slot, partner).start()

    me = (gx * NGY + gy) * NGZ + gz
    to_root = pltpu.make_async_remote_copy(
        src_ref=reduce.at[0, pl.ds(0, 1)], dst_ref=direct.at[me], send_sem=sum_send.at[2],
        recv_sem=sum_recv.at[2], device_id=ROOT, device_id_type=MESH,
    )

    reduce[0, 0:1, :] = row
    pl.semaphore_wait(wave.at[2], NGX)
    start_sum(0, plane)

    @pl.when(jnp.logical_not(in_root_layer))
    def _():
        pl.semaphore_wait(ready, 1)

    pl.when(jnp.logical_not(is_root))(to_root.start)
    image_plane(-1, xm_side, 7)
    image_row(0)
    copy_u = pltpu.make_async_copy(field.at[(U0,) + inner], u_out.at[0], copy_sem.at[0])
    copy_u.start()
    copy_v = pltpu.make_async_copy(field.at[(pl.ds(U1, 2),) + inner], u_out.at[pl.ds(1, 2)], copy_sem.at[2])
    copy_v.start()
    copy_w = pltpu.make_async_copy(field.at[(pl.ds(W0, 3),) + inner], w_out, copy_sem.at[1])
    copy_w.start()
    for i, (f, swapped) in enumerate(((W0, s_w0), (W1, s_w1), (W2, s_w2))):
        for x in range(BX):
            c = (0.5 / SCALE) * centre(C, x)
            g_out[i, 0, x] = c * (centre(f, x + 1) - centre(f, x - 1))
            after, before = around_y(f, x)
            g_out[i, 1, x] = c * (after - before)
            after, before = around_z(centre(f, x), ends(swapped, x))
            g_out[i, 2, x] = c * (after - before)
    receive(ENTH)
    s_h = swap(pair(tlo[TH], thi[TH]))
    for x in range(BX):
        h = centre(H, x)
        hyp, hym = around_y(H, x)
        hzp, hzm = around_z(h, ends(s_h, x))
        laplace = centre(H, x + 1) + centre(H, x - 1) + hyp + hym + hzp + hzm - 6.0 * h
        h_out[x] = h + DIFFUSE * laplace + HEATING * heat[x]
    copy_u.wait()
    copy_v.wait()
    copy_w.wait()
    for kind in range(3):
        whole(kind).wait_send()

    sum_whole(0, 15).wait_recv()
    high, low = row_total(reduce[0])
    reduce[1, 0:1, :] = jnp.where(lane8 < 8, high, turn(low, 8))[0:1]

    @pl.when(jnp.logical_not(in_root_column) | is_root)
    def _():
        start_sum(1, column)

    @pl.when(in_root_column & jnp.logical_not(is_root))
    def _():
        for slot, partner in enumerate(column):
            pl.when((partner[1] != ROOT[1]) | (partner[2] != ROOT[2]))(sum_copy(1, slot, partner).start)

    @pl.when(is_root)
    def _():
        direct[(ROOT[0] * NGY + ROOT[1]) * NGZ + ROOT[2]] = row
        sum_whole(2, DEVICES - 1).wait_recv()
        high, low = row_total(direct[...].reshape(DEVICES, BZ))
        total[0] = high
        total[1] = low

    @pl.when(jnp.logical_not(is_root))
    def _():
        sum_whole(1, 15).wait_recv()
        high, low = row_total(reduce[1])
        total[0] = high
        total[1] = low + turn(high, -8)

    high, low = total[0], total[1]
    high, low = quick_sum(high, low)

    def spread(v, i):
        return jnp.broadcast_to(v[:, i : i + 1], (8, BZ))

    moments = [(spread(high, i), spread(low, i)) for i in range(6)]
    for i, v in enumerate(solve_moments(moments)):
        c_out[i] = v
    sum_whole(0, 15).wait_send()

    @pl.when(in_root_column & jnp.logical_not(is_root))
    def _():
        sum_whole(1, 14).wait_send()

    @pl.when(jnp.logical_not(in_root_column) | is_root)
    def _():
        sum_whole(1, 15).wait_send()

    pl.when(jnp.logical_not(is_root))(to_root.wait_send)


def finish(w, g, u, h, c, vel_out, p_out, h_out, vel, p, sem):
    copy_h = pltpu.make_async_copy(h, h_out, sem.at[0])
    copy_h.start()
    c0, c1, c2 = (jnp.concatenate([c[i]] * 4, axis=0) for i in range(3))
    copies = [copy_h]
    for i in range(3):
        for x in range(BX):
            vel[i, x] = u[i, x] - (c0 * g[0, i, x] + c1 * g[1, i, x] + c2 * g[2, i, x])
        copy = pltpu.make_async_copy(vel.at[i], vel_out.at[i], sem.at[1 + i])
        copy.start()
        copies.append(copy)
    scaled = tuple(v * (1.0 / SCALE) for v in (c0, c1, c2))
    for x in range(BX):
        p[x] = scaled[0] * w[0, x] + scaled[1] * w[1, x] + scaled[2] * w[2, x]
    copy_p = pltpu.make_async_copy(p, p_out, sem.at[4])
    copy_p.start()
    for copy in copies + [copy_p]:
        copy.wait()


def shards(*args):
    block = (BX, BY, BZ)
    f32 = jnp.float32
    any_ref = pl.BlockSpec(memory_space=pl.ANY)
    vmem = pl.BlockSpec(memory_space=pltpu.VMEM)
    results = pl.pallas_call(
        kernel,
        out_shape=(
            jax.ShapeDtypeStruct((3,) + block, f32),
            jax.ShapeDtypeStruct((3, 3) + block, f32),
            jax.ShapeDtypeStruct((3,) + block, f32),
            jax.ShapeDtypeStruct(block, f32),
            jax.ShapeDtypeStruct((3, 8, BZ), f32),
        ),
        in_specs=[any_ref] * 7,
        out_specs=(vmem,) * 5,
        scratch_shapes=[
            pltpu.VMEM((FIELDS, BX + 4, BY + 16, BZ), f32),
            pltpu.VMEM((7, 8, BZ), f32),
            pltpu.VMEM((7, 8, BZ), f32),
            pltpu.VMEM((7, 8, BZ), f32),
            pltpu.VMEM((8, 5, 8, BZ), f32),
            pltpu.VMEM((BX + 3, BY, BZ), f32),
            pltpu.VMEM((BX + 2, BY + 8, BZ), f32),
            pltpu.VMEM((BX + 2, BY, BZ), f32),
            pltpu.VMEM((BX + 2, BY, BZ), f32),
            pltpu.VMEM(block, f32),
            pltpu.VMEM(block, f32),
            pltpu.VMEM((SLOTS, BZ), jnp.int32),
            pltpu.VMEM((SLOTS, BZ), jnp.int32),
            pltpu.VMEM((SLOTS, BZ), jnp.int32),
            pltpu.VMEM((BX * BY, SLOTS * BZ), jnp.bfloat16),
            pltpu.VMEM((BZ, SLOTS * BZ), jnp.bfloat16),
            pltpu.VMEM((BX * BY, BZ), f32),
            pltpu.VMEM(block, f32),
            pltpu.VMEM((2, 16, BZ), f32),
            pltpu.VMEM((DEVICES, 1, BZ), f32),
            pltpu.VMEM((2, 8, BZ), f32),
            pltpu.VMEM((1024, BZ), f32),
            pltpu.SemaphoreType.DMA((8,)),
            pltpu.SemaphoreType.DMA((3,)),
            pltpu.SemaphoreType.DMA((3,)),
            pltpu.SemaphoreType.DMA((3,)),
            pltpu.SemaphoreType.DMA((3,)),
            pltpu.SemaphoreType.DMA((3,)),
            pltpu.SemaphoreType.REGULAR,
            pltpu.SemaphoreType.REGULAR((3,)),
        ],
        compiler_params=pltpu.CompilerParams(
            collective_id=0, has_side_effects=True, vmem_limit_bytes=32 * 1024 * 1024
        ),
        name="simple_step",
    )(*[pltpu.with_memory_space_constraint(a, pltpu.HBM) for a in args])
    results = [pltpu.with_memory_space_constraint(r, pltpu.VMEM) for r in results]
    return tuple(
        pl.pallas_call(
            finish,
            out_shape=(
                jax.ShapeDtypeStruct((3,) + block, f32),
                jax.ShapeDtypeStruct(block, f32),
                jax.ShapeDtypeStruct(block, f32),
            ),
            in_specs=[vmem] * 5,
            out_specs=(pl.BlockSpec(memory_space=pltpu.HBM),) * 3,
            scratch_shapes=[
                pltpu.VMEM((3,) + block, f32),
                pltpu.VMEM(block, f32),
                pltpu.SemaphoreType.DMA((5,)),
            ],
            compiler_params=pltpu.CompilerParams(vmem_limit_bytes=8 * 1024 * 1024),
            name="finish",
        )(*results)
    )


def solution(mesh):
    in_specs = (
        P(None, "gx", "gy", "gz"),
        P("gx", "gy", "gz"),
        P("gx", "gy", "gz"),
        P("gx", "gy", "gz"),
        P(("gx", "gy", "gz"), None),
        P(("gx", "gy", "gz"), None),
        P(("gx", "gy", "gz"), None),
    )
    out_specs = (P(None, "gx", "gy", "gz"), P("gx", "gy", "gz"), P("gx", "gy", "gz"))
    return jax.shard_map(shards, mesh=mesh, in_specs=in_specs, out_specs=out_specs, check_vma=False)
```

```python
import math

import jax
import jax.numpy as jnp
from jax import lax
from jax.experimental import pallas as pl
from jax.experimental.pallas import tpu as pltpu
from jax.sharding import PartitionSpec as P

MESH = pl.DeviceIdType.MESH
NGX, NGY, NGZ = 4, 8, 8
BX, BY, BZ = 8, 32, 128
SLOTS = 16
DIFFUSE = 0.1
HEATING = 0.5
EXPANSION = 1.5
SCALE = 16.0
H, C, U0, BP, U1, U2, W0, W1, W2 = range(9)
FIELDS = 9
TU0, TC, TU2, TB, TU1, TH, TW = range(7)
ROWS = slice(8, 40)
SIGNS = (-1, 1)
XZ = tuple((a, 0, c) for a in SIGNS for c in SIGNS)
YZ = tuple((0, b, c) for b in SIGNS for c in SIGNS)
XY = tuple((a, b, 0) for a in SIGNS for b in SIGNS)
SIDES = ((-1, 0, 0), (1, 0, 0), (0, -1, 0), (0, 1, 0), (0, 0, -1), (0, 0, 1)) + XY + XZ + YZ
FIRST, ENTH, IMAGE = range(3)
PIVOT_FLOOR = 1e-9
EARLY_CHIPS = ((0, 0), (1, 0), (3, 0), (2, 0), (0, 1))
EARLY = tuple((x, 2 * y + c, 0) for x, y in EARLY_CHIPS for c in (1, 0))
DEVICES = 256


def two_sum(a, b):
    s = a + b
    t = s - a
    return s, (a - (s - t)) + (b - t)


def quick_sum(a, b):
    s = a + b
    return s, b - (s - a)


def split(a):
    t = 4097.0 * a
    high = t - (t - a)
    return high, a - high


def two_mul(a, b):
    p = a * b
    ah, al = split(a)
    bh, bl = split(b)
    return p, ((ah * bh - p) + ah * bl + al * bh) + al * bl


def df_sub(a, b):
    s, e = two_sum(a[0], -b[0])
    return quick_sum(s, e + (a[1] - b[1]))


def df_mul(a, b):
    p, e = two_mul(a[0], b[0])
    return quick_sum(p, e + (a[0] * b[1] + a[1] * b[0]))


def df_over(a, b, inverse):
    q = a[0] * inverse
    p, e = two_mul(q, b[0])
    rest = ((a[0] - p) - e) + (a[1] - q * b[1])
    return quick_sum(q, rest * inverse)


def solve_moments(m):
    i0 = 1.0 / m[1][0]
    l10 = df_over(m[2], m[1], i0)
    l20 = df_over(m[3], m[1], i0)
    d1 = df_sub(m[3], df_mul(l10, m[2]))
    e12 = df_sub(m[4], df_mul(l10, m[3]))
    y1 = df_sub(m[1], df_mul(l10, m[0]))
    y2 = df_sub(m[2], df_mul(l20, m[0]))
    d2 = df_sub(m[5], df_mul(l20, m[3]))
    ok1 = d1[0] > PIVOT_FLOOR * m[3][0]
    i1 = jnp.where(ok1, 1.0 / d1[0], 0.0)
    l21 = df_over(e12, d1, i1)
    d2 = df_sub(d2, df_mul(l21, e12))
    y2 = df_sub(y2, df_mul(l21, y1))
    ok2 = ok1 & (d2[0] > PIVOT_FLOOR * m[5][0])
    c2 = jnp.where(ok2, y2[0] / d2[0], 0.0)
    p, e = two_mul(e12[0], c2)
    c1 = (((y1[0] - p) - e) + (y1[1] - e12[1] * c2)) * i1
    p1, e1 = two_mul(m[2][0], c1)
    p2, e2 = two_mul(m[3][0], c2)
    s, t1 = two_sum(m[0][0], -p1)
    s, t2 = two_sum(s, -p2)
    rest = (t1 - e1) + (t2 - e2) + (m[0][1] - m[2][1] * c1 - m[3][1] * c2)
    return (s + rest) * i0, c1, c2


def row_total(rows):
    parts = [(rows[i : i + 8], None) for i in range(0, rows.shape[0], 8)]
    while len(parts) > 1:
        merged = []
        for (a, low_a), (b, low_b) in zip(parts[0::2], parts[1::2]):
            s, e = two_sum(a, b)
            merged.append((s, e if low_a is None else e + (low_a + low_b)))
        parts = merged
    s, e = parts[0]
    for step in (4, 2, 1):
        other = pltpu.roll(s, step, axis=0)
        e = e + pltpu.roll(e, step, axis=0)
        s, more = two_sum(s, other)
        e = e + more
    return s, e


def opposite(side):
    return tuple(-v for v in side)


def messages(field, tz, tlo, thi, dz):
    xs, xd = {-1: 2, 1: 9}, {-1: 10, 1: 1}
    ys, yd = {-1: 8, 1: 39}, {-1: 40, 1: 7}
    xs2, xd2 = {-1: pl.ds(2, 2), 1: pl.ds(8, 2)}, {-1: pl.ds(10, 2), 1: pl.ds(0, 2)}
    ys2, yd2 = {-1: pl.ds(8, 2), 1: pl.ds(38, 2)}, {-1: pl.ds(40, 2), 1: pl.ds(6, 2)}
    rows, planes = pl.ds(8, BY), pl.ds(2, BX)
    table = [[], [], []]
    for side in XZ + YZ + XY + SIDES[:2] + SIDES[4:6] + SIDES[2:4]:
        a, b, c = side
        far = thi if c < 0 else tlo
        slot = (XZ + YZ).index(opposite(side)) if side in XZ + YZ else None
        enth = []
        if side in XZ:
            first = [(tz.at[pl.ds(TU0, 3)], dz.at[slot, pl.ds(0, 3)])]
            image = [(tz.at[TW], dz.at[slot, 4])]
        elif side in YZ:
            first = [(tz.at[pl.ds(TC, 4)], dz.at[slot, pl.ds(0, 4)])]
            image = [(tz.at[TW], dz.at[slot, 4])]
        elif side in XY:
            first = [(field.at[pl.ds(C, 4), xs[a], ys[b]], field.at[pl.ds(C, 4), xd[a], yd[b]])]
            image = [(field.at[W1, xs[a], ys[b]], field.at[W1, xd[a], yd[b]])]
        elif a:
            first = [
                (field.at[C, xs2[a], rows], field.at[C, xd2[a], rows]),
                (field.at[pl.ds(U0, 2), xs[a], rows], field.at[pl.ds(U0, 2), xd[a], rows]),
            ]
            enth = [(field.at[H, xs[a], rows], field.at[H, xd[a], rows])]
            image = [(field.at[W1, xs2[a], rows], field.at[W1, xd2[a], rows])]
        elif b:
            first = [
                (field.at[C, planes, ys2[b]], field.at[C, planes, yd2[b]]),
                (field.at[pl.ds(BP, 2), planes, ys[b]], field.at[pl.ds(BP, 2), planes, yd[b]]),
            ]
            enth = [(field.at[H, planes, ys[b]], field.at[H, planes, yd[b]])]
            image = [(field.at[W1, planes, ys2[b]], field.at[W1, planes, yd2[b]])]
        else:
            first = [(tz.at[pl.ds(TC, 3)], far.at[pl.ds(TC, 3)])]
            enth = [(tz.at[TH], far.at[TH])]
            image = [(tz.at[TW], far.at[TW])]
        for kind, pairs in ((FIRST, first), (ENTH, enth), (IMAGE, image)):
            table[kind] += [(side, src, dst) for src, dst in pairs]
    return table


def kernel(
    vel, coef, enth, void, cells, normal, flag,
    w_out, g_out, u_out, h_out, c_out,
    field, tz, tlo, thi, dz, cx, cy, czm, czp, zlow, av, wc, wn, wf, hot_row, hot_lane, grid,
    heat, reduce, direct, total, tally, load_sem, copy_sem, send_sem, recv_sem, sum_send, sum_recv, ready, wave,
):
    gx, gy, gz = lax.axis_index("gx"), lax.axis_index("gy"), lax.axis_index("gz")
    chip_y, core = gy // 2, lax.rem(gy, 2)

    has = dict(zip(SIDES[:6], (gx > 0, gx < NGX - 1, gy > 0, gy < NGY - 1, gz > 0, gz < NGZ - 1)))

    def beside(side):
        return tuple(
            lax.rem(at + step + size, size) if step else at
            for at, step, size in zip((gx, gy, gz), side, (NGX, NGY, NGZ))
        )

    def in_plane(i, j):
        return (lax.rem(gx + i, NGX), lax.rem(chip_y + j, NGY // 2) * 2 + core, gz)

    def in_column(k, j):
        return (gx, chip_y * 2 + lax.rem(core + j, 2), lax.rem(gz + k, NGZ))

    def far_first(pairs, n, m):
        return sorted(pairs, key=lambda p: -min(p[0], n - p[0]) - min(p[1], m - p[1]))

    plane_steps = far_first([(i, j) for i in range(NGX) for j in range(NGY // 2) if i or j], NGX, NGY // 2)
    column_steps = far_first([(k, j) for k in range(NGZ) for j in range(2) if k or j], NGZ, 2)
    plane = [in_plane(i, j) for i, j in plane_steps]
    column = [in_column(k, j) for k, j in column_steps]

    inner = (pl.ds(2, BX), pl.ds(8, BY))
    barrier = pltpu.get_barrier_semaphore()
    in_layer = gz == 0
    in_early_column = ((gx == 0) & (chip_y < 2)) | (chip_y == 0)
    is_early = in_layer & in_early_column

    def signal(sem, partners):
        for partner in partners:
            pl.semaphore_signal(sem, inc=1, device_id=partner, device_id_type=MESH)

    near = [beside(side) for side in SIDES]
    signal(barrier, near)
    loads = [
        (cells, wc), (flag, wf), (normal, wn),
        (vel.at[0], field.at[(U0,) + inner]),
        (vel.at[pl.ds(1, 2)], field.at[(pl.ds(U1, 2),) + inner]),
        (void, av),
        (coef, field.at[(C,) + inner]),
        (enth, field.at[(H,) + inner]),
    ]
    loads = [pltpu.make_async_copy(s, d, load_sem.at[i]) for i, (s, d) in enumerate(loads)]
    for copy in loads:
        copy.start()

    table = messages(field, tz, tlo, thi, dz)
    copies = [
        [
            pltpu.make_async_remote_copy(
                src_ref=src, dst_ref=dst, send_sem=send_sem.at[kind], recv_sem=recv_sem.at[kind],
                device_id=beside(side), device_id_type=MESH,
            )
            for side, src, dst in table[kind]
        ]
        for kind in range(3)
    ]

    def whole(kind):
        count = sum(math.prod(dst.shape) for _, _, dst in table[kind]) // BZ
        ref = tally.at[pl.ds(0, count)]
        return pltpu.make_async_remote_copy(
            src_ref=ref, dst_ref=ref, send_sem=send_sem.at[kind], recv_sem=recv_sem.at[kind],
            device_id=beside(SIDES[0]), device_id_type=MESH,
        )

    def send(kind):
        for copy in copies[kind]:
            copy.start()

    def receive(kind):
        whole(kind).wait_recv()
        for side in SIDES[:6]:
            dim = [i for i in range(3) if side[i]][0]

            @pl.when(jnp.logical_not(has[side]))
            def _():
                for to, _, dst in table[kind]:
                    if to[dim] == -side[dim]:
                        dst[...] = jnp.zeros(dst.shape, jnp.float32)

    lane8 = lax.broadcasted_iota(jnp.int32, (8, BZ), 1)
    sub8 = lax.broadcasted_iota(jnp.int32, (8, BZ), 0)
    lane32 = lax.broadcasted_iota(jnp.int32, (BY, BZ), 1)
    row32 = lax.broadcasted_iota(jnp.int32, (BY, BZ), 0)
    first, last = lane32 == 0, lane32 == BZ - 1
    first8, last8 = lane8 == 0, lane8 == BZ - 1
    place = lane8 % 4
    low_lane = place == 1
    y_group = lane8 // 4 % 4
    ends_half = jnp.where(first8, 0.5, jnp.where(last8, -0.5, 0.0))
    ends_half32 = jnp.where(first, 0.5, jnp.where(last, -0.5, 0.0))

    def turn(v, by, axis=1):
        size = v.shape[axis]
        return pltpu.roll(v, by % size, axis=axis) if by % size else v

    def pack(values, acc, x):
        for b in range(4):
            k = 4 * x + b
            turned = turn(values[8 * b : 8 * b + 8], 4 * k + 2)
            acc = turned if acc is None else jnp.where(lane8 // 4 == k, turned, acc)
        return acc

    def pair(low, high):
        return jnp.where(low_lane, low, high)

    def swap(v):
        return jnp.where(low_lane, turn(v, -1), turn(v, 1))

    def ends(swapped, x):
        return jnp.concatenate([turn(swapped, -4 * (4 * x + b) - 2) for b in range(4)], axis=0)

    def ends_row(swapped, b):
        row, k = (7, 3) if b < 0 else (0, 0)
        out = None
        spread = jnp.broadcast_to(swapped[row : row + 1], (8, BZ))
        for x in range(BX):
            turned = turn(spread, -4 * (4 * x + k) - 2)
            out = turned if out is None else jnp.where(sub8 == x, turned, out)
        return out

    def around_z(v, e):
        f, l = (first, last) if v.shape[0] == BY else (first8, last8)
        return jnp.where(l, e, turn(v, -1)), jnp.where(f, e, turn(v, 1))

    def around_y(f, x):
        return field[f, x + 2, 9:41, :], field[f, x + 2, 7:39, :]

    def centre(f, x):
        return field[f, x + 2, ROWS, :]

    def row_of_field(f, r):
        return field[f, 2:10, r, :]

    def diagonal(side, q):
        a, b, _ = side
        lo, hi = ((XZ + YZ).index((a, b, c)) for c in SIGNS)
        return pair(dz[lo, q], dz[hi, q])

    xm_side, xp_side, ym_side, yp_side, zm_side, zp_side = SIDES[:6]

    for copy in loads[0:3]:
        copy.wait()
    where = wc[...]
    row_at = where // BZ
    lane_at = where - row_at * BZ
    code = jnp.where(wf[...] > 0, wf[...] + 4 * (wn[...] // 2), 0).astype(jnp.float32)
    up256 = lax.broadcasted_iota(jnp.int32, (BX * BY, BZ), 0)
    up128 = lax.broadcasted_iota(jnp.int32, (BZ, BZ), 0)
    for s in range(SLOTS):
        hot_row[:, s * BZ : (s + 1) * BZ] = jnp.where(up256 == row_at[s : s + 1], 1.0, 0.0).astype(jnp.bfloat16)
        hot_lane[:, s * BZ : (s + 1) * BZ] = jnp.where(up128 == lane_at[s : s + 1], code[s : s + 1], 0.0).astype(jnp.bfloat16)
    grid[...] = lax.dot_general(
        hot_row[...], hot_lane[...], (((1,), (1,)), ((), ())), preferred_element_type=jnp.float32
    )
    for copy in loads[3:]:
        copy.wait()

    t_b = t_c = t_u0 = t_u1 = t_u2 = None
    for x in range(BX):
        a = av[x]
        g = grid[x * BY : (x + 1) * BY, :]
        not_x = g > 3.5
        is_z = g > 7.5
        s = g - jnp.where(not_x, 4.0, 0.0) - jnp.where(is_z, 4.0, 0.0)
        u0, u1, u2 = centre(U0, x), centre(U1, x), centre(U2, x)
        parallel = (
            jnp.where(not_x, u0 * u0, 0.0)
            + jnp.where(not_x & jnp.logical_not(is_z), 0.0, u1 * u1)
            + jnp.where(is_z, 0.0, u2 * u2)
        )
        speed = jnp.sqrt(parallel + 0.25)
        liquid = 1.0 - a
        evap = 1.5 * a * s * s
        root = jnp.where(s > 1.5, 2.0 * 1.4142135623730951, s)
        heat[x] = liquid * speed * s + 0.6 * liquid * root + evap
        slope = jnp.where(row32 == BY - 1, 0.0, turn(u1, -1, 0)) - jnp.where(row32 == 0, 0.0, turn(u1, 1, 0))
        slope = slope + (jnp.where(last, 0.0, turn(u2, -1)) - jnp.where(first, 0.0, turn(u2, 1)))
        if x < BX - 1:
            slope = slope + centre(U0, x + 1)
        if x > 0:
            slope = slope - centre(U0, x - 1)
        b = EXPANSION * (0.5 * evap) - 0.5 * slope
        field[BP, x + 2, ROWS, :] = b
        t_b = pack(b, t_b, x)
        t_c = pack(centre(C, x), t_c, x)
        t_u0 = pack(u0, t_u0, x)
        t_u1 = pack(u1, t_u1, x)
        t_u2 = pack(u2, t_u2, x)
    for i, t in ((TB, t_b), (TC, t_c), (TU0, t_u0), (TU1, t_u1), (TU2, t_u2)):
        tz[i] = t

    pl.semaphore_wait(barrier, len(near))
    send(FIRST)
    signal(wave.at[0], [beside(side) for side in SIDES[:6]])

    t_h = None
    half = 0.5 / SCALE
    for x in range(BX):
        t_h = pack(centre(H, x), t_h, x)
        c = centre(C, x)
        if x < BX - 1:
            cx[x + 2] = half * (c + centre(C, x + 1))
        cy[x + 1, 0:32] = half * (c + turn(c, 1, 0))
        czp[x + 1] = half * jnp.where(last, c, c + turn(c, -1))
        czm[x + 1] = half * jnp.where(first, c, c + turn(c, 1))
    tz[TH] = t_h
    send(ENTH)

    pl.semaphore_wait(wave.at[0], 6)
    second = [(0, 2, 0), (0, -2, 0), (0, 0, 2), (0, 0, -2)]
    signal(wave.at[1], [beside(step) for step in second])

    def low_high(v):
        return v[0:8], v[8:24], v[24:32]

    def y_ends(v, f, x):
        a, m, z = low_high(v)
        a = a + jnp.where(sub8 == 0, 0.5 * field[f, x + 2, 7:8, :], 0.0)
        z = z - jnp.where(sub8 == 7, 0.5 * field[f, x + 2, 40:41, :], 0.0)
        return jnp.concatenate([a, m, z], axis=0)

    has_z = jnp.where(low_lane, has[zm_side].astype(jnp.float32), has[zp_side].astype(jnp.float32))

    def z_inside(t):
        return jnp.where(low_lane, turn(t, -1), turn(t, 1))

    def z_around_x(v, before, after):
        return (
            jnp.where(lane8 >= 112, turn(after, -16), turn(v, -16)),
            jnp.where(lane8 < 16, turn(before, 16), turn(v, 16)),
        )

    def z_around_y(v, before, after):
        up = jnp.where(y_group == 3, turn(after, 12), turn(v, -4))
        down = jnp.where(y_group == 0, turn(before, -12), turn(v, 4))
        return (
            turn(jnp.where(sub8 == 0, up, v), -1, 0),
            turn(jnp.where(sub8 == 7, down, v), 1, 0),
        )

    zero = jnp.zeros((8, BZ), jnp.float32)
    receive(FIRST)
    after, before = z_around_x(zero, diagonal(xm_side, 0), diagonal(xp_side, 0))
    b = pair(tlo[TB], thi[TB]) - 0.5 * (after - before)
    after, before = z_around_y(zero, diagonal(ym_side, 3), diagonal(yp_side, 3))
    b = b - 0.5 * (after - before) + jnp.where(low_lane, -0.5, 0.5) * z_inside(tz[TU2])
    s_w0 = swap(has_z * b)

    s_u2 = swap(pair(tlo[TU2], thi[TU2]))
    s_c = swap(pair(tlo[TC], thi[TC]))
    for x in range(BX):
        b = centre(BP, x) + ends_half32 * ends(s_u2, x)
        b = y_ends(b, U1, x)
        if x == 0:
            b = b + 0.5 * field[U0, 1, ROWS, :]
        if x == BX - 1:
            b = b - 0.5 * field[U0, 10, ROWS, :]
        field[W0, x + 2, ROWS, :] = b
        c = centre(C, x)
        e = ends(s_c, x)
        czp[x + 1] = czp[x + 1] + jnp.where(last, half * e, 0.0)
        czm[x + 1] = czm[x + 1] + jnp.where(first, half * e, 0.0)
        cy[x + 1, 0:1] = half * (c[0:1] + field[C, x + 2, 7:8, :])
        cy[x + 1, 32:33] = half * (c[31:32] + field[C, x + 2, 40:41, :])
    cx[1] = half * (centre(C, 0) + centre(C, -1))
    cx[9] = half * (centre(C, 7) + centre(C, 8))
    for x, own, sign, side, inside in ((-1, 0, -0.5, xm_side, 7), (BX, BX - 1, 0.5, xp_side, 0)):
        b = centre(BP, x) + sign * centre(U0, own)
        b = y_ends(b, U1, x) + ends_half32 * ends(swap(diagonal(side, 2)), inside)
        field[W0, x + 2, ROWS, :] = jnp.where(has[side], b, 0.0)
    for r, own, sign, side in ((7, 8, -0.5, ym_side), (40, 39, 0.5, yp_side)):
        b = row_of_field(BP, r) + sign * row_of_field(U1, own)
        b = b + jnp.where(sub8 == 0, 0.5 * field[U0, 1, r : r + 1, :], 0.0)
        b = b - jnp.where(sub8 == 7, 0.5 * field[U0, 10, r : r + 1, :], 0.0)
        b = b + ends_half * ends_row(swap(diagonal(side, 1)), side[1])
        b = jnp.where(has[side], b, 0.0)
        for x in range(BX):
            field[W0, x + 2, r : r + 1, :] = b[x : x + 1]
    def operator(f, x, e):
        v = centre(f, x)
        yp, ym = around_y(f, x)
        zp, zm = around_z(v, e)
        out = cx[x + 2] * (v - centre(f, x + 1)) + cx[x + 1] * (v - centre(f, x - 1))
        out = out + (cy[x + 1, 1:33] * (v - yp) + cy[x + 1, 0:32] * (v - ym))
        return out + (czp[x + 1] * (v - zp) + czm[x + 1] * (v - zm))

    t_w = None
    for x in range(BX):
        out = operator(W0, x, ends(s_w0, x))
        field[W1, x + 2, ROWS, :] = out
        t_w = pack(out, t_w, x)
    tz[TW] = t_w
    send(IMAGE)

    def fold(v):
        return (v[0:8] + v[8:16]) + (v[16:24] + v[24:32])

    def plus(acc, v):
        v = fold(v)
        return v if acc is None else acc + v

    m = [None] * 6
    for x in range(BX):
        v, out = centre(W0, x), centre(W1, x)
        m[0], m[1], m[2] = plus(m[0], v * v), plus(m[1], v * out), plus(m[2], out * out)
    for x, side, inside in ((-1, xm_side, 7), (BX, xp_side, 0)):
        c = centre(C, x)
        if x < 0:
            cx[0] = half * (c + centre(C, -2))
        else:
            cx[10] = half * (c + centre(C, 9))
        after, before = around_y(C, x)
        cy[x + 1, 0:32] = half * (c + before)
        cy[x + 1, 32:33] = half * (c[31:32] + after[31:32])
        after, before = around_z(c, ends(swap(diagonal(side, 1)), inside))
        czp[x + 1] = half * (c + after)
        czm[x + 1] = half * (c + before)
    z_edge = jnp.where(has[zm_side], 0.0, 1.0)
    y_edge = jnp.where(has[ym_side], 0.0, 1.0)
    x_edge = jnp.where(has[xm_side], 0.0, 1.0)
    for x in range(BX):
        low = jnp.where(first, czm[x + 1], 0.0) * z_edge
        low = low + jnp.where(row32 == 0, cy[x + 1, 0:32], 0.0) * y_edge
        if x == 0:
            low = low + cx[1] * x_edge
        zlow[x] = low

    def face_values(t, qx, qy):
        lo, hi, own = tlo[t], thi[t], tz[t]
        v = pair(lo, hi)
        outer = jnp.where(low_lane, turn(lo, 1), turn(hi, -1))
        return (
            (v, outer, z_inside(own))
            + z_around_x(v, diagonal(xm_side, qx), diagonal(xp_side, qx))
            + z_around_y(v, diagonal(ym_side, qy), diagonal(yp_side, qy))
        )

    def row_values(f, q, r, beyond, own, side):
        v = row_of_field(f, r)
        after = jnp.where(sub8 == 7, field[f, 10, r : r + 1, :], turn(v, -1, 0))
        before = jnp.where(sub8 == 0, field[f, 1, r : r + 1, :], turn(v, 1, 0))
        zp, zm = around_z(v, ends_row(swap(diagonal(side, q)), side[1]))
        return v, row_of_field(f, beyond), row_of_field(f, own), after, before, zp, zm

    def weights(values, mask):
        c, *near_c = values
        return [mask * (half * (c + cn)) for cn in near_c]

    def applied(weight, values):
        v, *near_v = values
        terms = [w * (v - vn) for w, vn in zip(weight, near_v)]
        return ((terms[0] + terms[1]) + (terms[2] + terms[3])) + (terms[4] + terms[5])

    face_weights = weights(face_values(TC, 1, 0), has_z)
    rows_beyond = ((7, 6, 8, ym_side), (40, 41, 39, yp_side))
    row_weights = [weights(row_values(C, 0, *at), has[at[3]].astype(jnp.float32)) for at in rows_beyond]

    def image_row(at):
        out = applied(row_weights[at], row_values(W1, 4, *rows_beyond[at]))
        r = rows_beyond[at][0]
        for x in range(BX):
            field[W2, x + 2, r : r + 1, :] = out[x : x + 1]

    pl.semaphore_wait(wave.at[1], len(second))
    signal(wave.at[2], [in_plane(i, 0) for i in range(1, NGX)] + [in_column(0, 1)])

    @pl.when(in_layer)
    def _():
        pl.semaphore_wait(wave.at[2], NGX)
        signal(ready, [in_column(k, 0) for k in range(1, NGZ)])

    receive(IMAGE)
    s_w2 = swap(applied(face_weights, face_values(TW, 4, 4)))
    image_row(1)
    s_w1 = swap(pair(tlo[TW], thi[TW]))
    for x in range(BX):
        out = operator(W1, x, ends(s_w1, x))
        field[W2, x + 2, ROWS, :] = out
        v = centre(W1, x)
        m[3], m[4] = plus(m[3], v * out), plus(m[4], out * out)

    def image_plane(x, side, inside):
        out = operator(W1, x, ends(swap(diagonal(side, 4)), inside))
        field[W2, x + 2, ROWS, :] = jnp.where(has[side], out, 0.0)

    image_plane(BX, xp_side, 0)
    for x in range(BX):
        v = centre(W2, x)
        dx = v - centre(W2, x + 1)
        dy = v - field[W2, x + 2, 9:41, :]
        dz_ = v - jnp.where(last, ends(s_w2, x), turn(v, -1))
        m[5] = plus(
            m[5],
            (cx[x + 2] * (dx * dx) + cy[x + 1, 1:33] * (dy * dy)) + (czp[x + 1] * (dz_ * dz_) + zlow[x] * (v * v)),
        )

    row = jnp.zeros((1, BZ), jnp.float32)
    for i in range(6):
        row = jnp.where(lane8[0:1] == i, jnp.sum(m[i], keepdims=True), row)

    def sum_copy(phase, slot, partner):
        return pltpu.make_async_remote_copy(
            src_ref=reduce.at[phase, pl.ds(0, 1)], dst_ref=reduce.at[phase, pl.ds(slot + 1, 1)],
            send_sem=sum_send.at[phase], recv_sem=sum_recv.at[phase], device_id=partner, device_id_type=MESH,
        )

    def sum_whole(phase, count):
        ref = tally.at[pl.ds(0, count)]
        return pltpu.make_async_remote_copy(
            src_ref=ref, dst_ref=ref, send_sem=sum_send.at[phase], recv_sem=sum_recv.at[phase],
            device_id=plane[0], device_id_type=MESH,
        )

    def start_sum(phase, group):
        for slot, partner in enumerate(group):
            sum_copy(phase, slot, partner).start()

    me = (gx * NGY + gy) * NGZ + gz
    to_early = [
        pltpu.make_async_remote_copy(
            src_ref=reduce.at[0, pl.ds(0, 1)], dst_ref=direct.at[pl.ds(me, 1)], send_sem=sum_send.at[2],
            recv_sem=sum_recv.at[2], device_id=device, device_id_type=MESH,
        )
        for device in EARLY
    ]
    reduce[0, 0:1, :] = row

    @pl.when(in_layer)
    def _():
        start_sum(0, plane)

    @pl.when(jnp.logical_not(in_layer))
    def _():
        pl.semaphore_wait(wave.at[2], NGX)
        start_sum(0, plane)
        pl.semaphore_wait(ready, 1)

    for device, copy in zip(EARLY, to_early):
        pl.when((gx != device[0]) | (gy != device[1]) | (gz != device[2]))(copy.start)

    image_plane(-1, xm_side, 7)
    image_row(0)
    copy_u = pltpu.make_async_copy(field.at[(U0,) + inner], u_out.at[0], copy_sem.at[0])
    copy_u.start()
    copy_v = pltpu.make_async_copy(field.at[(pl.ds(U1, 2),) + inner], u_out.at[pl.ds(1, 2)], copy_sem.at[2])
    copy_v.start()
    copy_w = pltpu.make_async_copy(field.at[(pl.ds(W0, 3),) + inner], w_out, copy_sem.at[1])
    copy_w.start()
    for i, (f, swapped) in enumerate(((W0, s_w0), (W1, s_w1), (W2, s_w2))):
        for x in range(BX):
            c = (0.5 / SCALE) * centre(C, x)
            g_out[i, 0, x] = c * (centre(f, x + 1) - centre(f, x - 1))
            after, before = around_y(f, x)
            g_out[i, 1, x] = c * (after - before)
            after, before = around_z(centre(f, x), ends(swapped, x))
            g_out[i, 2, x] = c * (after - before)
    receive(ENTH)
    s_h = swap(pair(tlo[TH], thi[TH]))
    for x in range(BX):
        h = centre(H, x)
        hyp, hym = around_y(H, x)
        hzp, hzm = around_z(h, ends(s_h, x))
        laplace = centre(H, x + 1) + centre(H, x - 1) + hyp + hym + hzp + hzm - 6.0 * h
        h_out[x] = h + DIFFUSE * laplace + HEATING * heat[x]
    copy_u.wait()
    copy_v.wait()
    copy_w.wait()
    for kind in range(3):
        whole(kind).wait_send()

    sum_whole(0, 15).wait_recv()
    high, low = row_total(reduce[0])
    reduce[1, 0:1, :] = jnp.where(lane8 < 8, high, turn(low, 8))[0:1]

    @pl.when(jnp.logical_not(in_early_column))
    def _():
        start_sum(1, column)

    @pl.when(in_early_column)
    def _():
        for slot, partner in enumerate(column):
            pl.when(partner[2] != 0)(sum_copy(1, slot, partner).start)

    @pl.when(is_early)
    def _():
        direct[pl.ds(me, 1), :] = row
        sum_whole(2, DEVICES - 1).wait_recv()
        high, low = row_total(direct[...])
        total[0] = high
        total[1] = low

    @pl.when(jnp.logical_not(is_early))
    def _():
        sum_whole(1, 15).wait_recv()
        high, low = row_total(reduce[1])
        total[0] = high
        total[1] = low + turn(high, -8)

    high, low = total[0], total[1]
    high, low = quick_sum(high, low)

    def spread(v, i):
        return jnp.broadcast_to(v[:, i : i + 1], (8, BZ))

    moments = [(spread(high, i), spread(low, i)) for i in range(6)]
    for i, v in enumerate(solve_moments(moments)):
        c_out[i] = v
    sum_whole(0, 15).wait_send()

    @pl.when(jnp.logical_not(in_early_column))
    def _():
        sum_whole(1, 15).wait_send()
        sum_whole(2, len(EARLY)).wait_send()

    @pl.when(in_early_column & in_layer)
    def _():
        sum_whole(1, 14).wait_send()
        sum_whole(2, len(EARLY) - 1).wait_send()

    @pl.when(in_early_column & jnp.logical_not(in_layer))
    def _():
        sum_whole(1, 13).wait_send()
        sum_whole(2, len(EARLY)).wait_send()


def finish(w, g, u, h, c, vel_out, p_out, h_out, vel, p, sem):
    copy_h = pltpu.make_async_copy(h, h_out, sem.at[0])
    copy_h.start()
    c0, c1, c2 = (jnp.concatenate([c[i]] * 4, axis=0) for i in range(3))
    copies = [copy_h]
    for i in range(3):
        for x in range(BX):
            vel[i, x] = u[i, x] - (c0 * g[0, i, x] + c1 * g[1, i, x] + c2 * g[2, i, x])
        copy = pltpu.make_async_copy(vel.at[i], vel_out.at[i], sem.at[1 + i])
        copy.start()
        copies.append(copy)
    scaled = tuple(v * (1.0 / SCALE) for v in (c0, c1, c2))
    for x in range(BX):
        p[x] = scaled[0] * w[0, x] + scaled[1] * w[1, x] + scaled[2] * w[2, x]
    copy_p = pltpu.make_async_copy(p, p_out, sem.at[4])
    copy_p.start()
    for copy in copies + [copy_p]:
        copy.wait()


def shards(*args):
    block = (BX, BY, BZ)
    f32 = jnp.float32
    any_ref = pl.BlockSpec(memory_space=pl.ANY)
    vmem = pl.BlockSpec(memory_space=pltpu.VMEM)
    results = pl.pallas_call(
        kernel,
        out_shape=(
            jax.ShapeDtypeStruct((3,) + block, f32),
            jax.ShapeDtypeStruct((3, 3) + block, f32),
            jax.ShapeDtypeStruct((3,) + block, f32),
            jax.ShapeDtypeStruct(block, f32),
            jax.ShapeDtypeStruct((3, 8, BZ), f32),
        ),
        in_specs=[any_ref] * 7,
        out_specs=(vmem,) * 5,
        scratch_shapes=[
            pltpu.VMEM((FIELDS, BX + 4, BY + 16, BZ), f32),
            pltpu.VMEM((7, 8, BZ), f32),
            pltpu.VMEM((7, 8, BZ), f32),
            pltpu.VMEM((7, 8, BZ), f32),
            pltpu.VMEM((8, 5, 8, BZ), f32),
            pltpu.VMEM((BX + 3, BY, BZ), f32),
            pltpu.VMEM((BX + 2, BY + 8, BZ), f32),
            pltpu.VMEM((BX + 2, BY, BZ), f32),
            pltpu.VMEM((BX + 2, BY, BZ), f32),
            pltpu.VMEM(block, f32),
            pltpu.VMEM(block, f32),
            pltpu.VMEM((SLOTS, BZ), jnp.int32),
            pltpu.VMEM((SLOTS, BZ), jnp.int32),
            pltpu.VMEM((SLOTS, BZ), jnp.int32),
            pltpu.VMEM((BX * BY, SLOTS * BZ), jnp.bfloat16),
            pltpu.VMEM((BZ, SLOTS * BZ), jnp.bfloat16),
            pltpu.VMEM((BX * BY, BZ), f32),
            pltpu.VMEM(block, f32),
            pltpu.VMEM((2, 16, BZ), f32),
            pltpu.VMEM((DEVICES, BZ), f32),
            pltpu.VMEM((2, 8, BZ), f32),
            pltpu.VMEM((1024, BZ), f32),
            pltpu.SemaphoreType.DMA((8,)),
            pltpu.SemaphoreType.DMA((3,)),
            pltpu.SemaphoreType.DMA((3,)),
            pltpu.SemaphoreType.DMA((3,)),
            pltpu.SemaphoreType.DMA((3,)),
            pltpu.SemaphoreType.DMA((3,)),
            pltpu.SemaphoreType.REGULAR,
            pltpu.SemaphoreType.REGULAR((3,)),
        ],
        compiler_params=pltpu.CompilerParams(
            collective_id=0, has_side_effects=True, vmem_limit_bytes=32 * 1024 * 1024
        ),
        name="simple_step",
    )(*[pltpu.with_memory_space_constraint(a, pltpu.HBM) for a in args])
    results = [pltpu.with_memory_space_constraint(r, pltpu.VMEM) for r in results]
    return tuple(
        pl.pallas_call(
            finish,
            out_shape=(
                jax.ShapeDtypeStruct((3,) + block, f32),
                jax.ShapeDtypeStruct(block, f32),
                jax.ShapeDtypeStruct(block, f32),
            ),
            in_specs=[vmem] * 5,
            out_specs=(pl.BlockSpec(memory_space=pltpu.HBM),) * 3,
            scratch_shapes=[
                pltpu.VMEM((3,) + block, f32),
                pltpu.VMEM(block, f32),
                pltpu.SemaphoreType.DMA((5,)),
            ],
            compiler_params=pltpu.CompilerParams(vmem_limit_bytes=8 * 1024 * 1024),
            name="finish",
        )(*results)
    )


def solution(mesh):
    in_specs = (
        P(None, "gx", "gy", "gz"),
        P("gx", "gy", "gz"),
        P("gx", "gy", "gz"),
        P("gx", "gy", "gz"),
        P(("gx", "gy", "gz"), None),
        P(("gx", "gy", "gz"), None),
        P(("gx", "gy", "gz"), None),
    )
    out_specs = (P(None, "gx", "gy", "gz"), P("gx", "gy", "gz"), P("gx", "gy", "gz"))
    return jax.shard_map(shards, mesh=mesh, in_specs=in_specs, out_specs=out_specs, check_vma=False)
```

```python
import math

import jax
import jax.numpy as jnp
from jax import lax
from jax.experimental import pallas as pl
from jax.experimental.pallas import tpu as pltpu
from jax.sharding import PartitionSpec as P

MESH = pl.DeviceIdType.MESH
NGX, NGY, NGZ = 4, 8, 8
BX, BY, BZ = 8, 32, 128
SLOTS = 16
DIFFUSE = 0.1
HEATING = 0.5
EXPANSION = 1.5
SCALE = 16.0
H, C, U0, BP, U1, U2, W0, W1, W2 = range(9)
FIELDS = 9
TU0, TU2, TU1, TB, TC, TH, TW = range(7)
ROWS = slice(8, 40)
SIGNS = (-1, 1)
XZ = tuple((a, 0, c) for a in SIGNS for c in SIGNS)
YZ = tuple((0, b, c) for b in SIGNS for c in SIGNS)
XY = tuple((a, b, 0) for a in SIGNS for b in SIGNS)
SIDES = ((-1, 0, 0), (1, 0, 0), (0, -1, 0), (0, 1, 0), (0, 0, -1), (0, 0, 1)) + XY + XZ + YZ
FIRST, OUTER, ENTH, IMAGE = range(4)
PIVOT_FLOOR = 1e-9
EARLY_CHIPS = ((0, 0), (1, 0), (3, 0), (2, 0), (0, 1))
EARLY = tuple((x, 2 * y + c, 0) for x, y in EARLY_CHIPS for c in (1, 0))
DEVICES = 256


def two_sum(a, b):
    s = a + b
    t = s - a
    return s, (a - (s - t)) + (b - t)


def quick_sum(a, b):
    s = a + b
    return s, b - (s - a)


def split(a):
    t = 4097.0 * a
    high = t - (t - a)
    return high, a - high


def two_mul(a, b):
    p = a * b
    ah, al = split(a)
    bh, bl = split(b)
    return p, ((ah * bh - p) + ah * bl + al * bh) + al * bl


def df_sub(a, b):
    s, e = two_sum(a[0], -b[0])
    return quick_sum(s, e + (a[1] - b[1]))


def df_mul(a, b):
    p, e = two_mul(a[0], b[0])
    return quick_sum(p, e + (a[0] * b[1] + a[1] * b[0]))


def df_over(a, b, inverse):
    q = a[0] * inverse
    p, e = two_mul(q, b[0])
    rest = ((a[0] - p) - e) + (a[1] - q * b[1])
    return quick_sum(q, rest * inverse)


def solve_moments(m):
    i0 = 1.0 / m[1][0]
    l10 = df_over(m[2], m[1], i0)
    l20 = df_over(m[3], m[1], i0)
    d1 = df_sub(m[3], df_mul(l10, m[2]))
    e12 = df_sub(m[4], df_mul(l10, m[3]))
    y1 = df_sub(m[1], df_mul(l10, m[0]))
    y2 = df_sub(m[2], df_mul(l20, m[0]))
    d2 = df_sub(m[5], df_mul(l20, m[3]))
    ok1 = d1[0] > PIVOT_FLOOR * m[3][0]
    i1 = jnp.where(ok1, 1.0 / d1[0], 0.0)
    l21 = df_over(e12, d1, i1)
    d2 = df_sub(d2, df_mul(l21, e12))
    y2 = df_sub(y2, df_mul(l21, y1))
    ok2 = ok1 & (d2[0] > PIVOT_FLOOR * m[5][0])
    c2 = jnp.where(ok2, y2[0] / d2[0], 0.0)
    p, e = two_mul(e12[0], c2)
    c1 = (((y1[0] - p) - e) + (y1[1] - e12[1] * c2)) * i1
    p1, e1 = two_mul(m[2][0], c1)
    p2, e2 = two_mul(m[3][0], c2)
    s, t1 = two_sum(m[0][0], -p1)
    s, t2 = two_sum(s, -p2)
    rest = (t1 - e1) + (t2 - e2) + (m[0][1] - m[2][1] * c1 - m[3][1] * c2)
    return (s + rest) * i0, c1, c2


def row_total(rows):
    parts = [(rows[i : i + 8], None) for i in range(0, rows.shape[0], 8)]
    while len(parts) > 1:
        merged = []
        for (a, low_a), (b, low_b) in zip(parts[0::2], parts[1::2]):
            s, e = two_sum(a, b)
            merged.append((s, e if low_a is None else e + (low_a + low_b)))
        parts = merged
    s, e = parts[0]
    for step in (4, 2, 1):
        other = pltpu.roll(s, step, axis=0)
        e = e + pltpu.roll(e, step, axis=0)
        s, more = two_sum(s, other)
        e = e + more
    return s, e


def opposite(side):
    return tuple(-v for v in side)


def messages(field, tz, tlo, thi, dz):
    xs, xd = {-1: 2, 1: 9}, {-1: 10, 1: 1}
    xs1, xd1 = {-1: 3, 1: 8}, {-1: 11, 1: 0}
    ys, yd = {-1: 8, 1: 39}, {-1: 40, 1: 7}
    xs2, xd2 = {-1: pl.ds(2, 2), 1: pl.ds(8, 2)}, {-1: pl.ds(10, 2), 1: pl.ds(0, 2)}
    ys2, yd2 = {-1: pl.ds(8, 2), 1: pl.ds(38, 2)}, {-1: pl.ds(40, 2), 1: pl.ds(6, 2)}
    rows, planes = pl.ds(8, BY), pl.ds(2, BX)
    table = [[], [], [], []]
    for side in XZ + YZ + XY + SIDES[:2] + SIDES[4:6] + SIDES[2:4]:
        a, b, c = side
        far = thi if c < 0 else tlo
        slot = (XZ + YZ).index(opposite(side)) if side in XZ + YZ else None
        enth = outer = []
        if side in XZ:
            first = [(tz.at[pl.ds(TU0, 2)], dz.at[slot, pl.ds(0, 2)])]
            outer = [(tz.at[TC], dz.at[slot, 2])]
            image = [(tz.at[TW], dz.at[slot, 4])]
        elif side in YZ:
            first = [(tz.at[pl.ds(TU2, 2)], dz.at[slot, pl.ds(0, 2)])]
            outer = [(tz.at[TC], dz.at[slot, 2])]
            image = [(tz.at[TW], dz.at[slot, 4])]
        elif side in XY:
            first = [(field.at[pl.ds(U0, 3), xs[a], ys[b]], field.at[pl.ds(U0, 3), xd[a], yd[b]])]
            outer = [(field.at[C, xs[a], ys[b]], field.at[C, xd[a], yd[b]])]
            image = [(field.at[W1, xs[a], ys[b]], field.at[W1, xd[a], yd[b]])]
        elif a:
            first = [(field.at[pl.ds(C, 3), xs[a], rows], field.at[pl.ds(C, 3), xd[a], rows])]
            outer = [(field.at[C, xs1[a], rows], field.at[C, xd1[a], rows])]
            enth = [(field.at[H, xs[a], rows], field.at[H, xd[a], rows])]
            image = [(field.at[W1, xs2[a], rows], field.at[W1, xd2[a], rows])]
        elif b:
            first = [
                (field.at[C, planes, ys2[b]], field.at[C, planes, yd2[b]]),
                (field.at[pl.ds(BP, 2), planes, ys[b]], field.at[pl.ds(BP, 2), planes, yd[b]]),
            ]
            enth = [(field.at[H, planes, ys[b]], field.at[H, planes, yd[b]])]
            image = [(field.at[W1, planes, ys2[b]], field.at[W1, planes, yd2[b]])]
        else:
            first = [(tz.at[pl.ds(TU2, 4)], far.at[pl.ds(TU2, 4)])]
            enth = [(tz.at[TH], far.at[TH])]
            image = [(tz.at[TW], far.at[TW])]
        for kind, pairs in ((FIRST, first), (OUTER, outer), (ENTH, enth), (IMAGE, image)):
            table[kind] += [(side, src, dst) for src, dst in pairs]
    return table


def kernel(
    vel, coef, enth, void, cells, normal, flag,
    w_out, g_out, u_out, h_out, c_out,
    field, tz, tlo, thi, dz, cx, cy, czm, czp, zlow, av, wc, wn, wf, hot_row, hot_lane, grid,
    heat, reduce, direct, total, tally, load_sem, copy_sem, send_sem, recv_sem, sum_send, sum_recv, ready, wave,
):
    gx, gy, gz = lax.axis_index("gx"), lax.axis_index("gy"), lax.axis_index("gz")
    chip_y, core = gy // 2, lax.rem(gy, 2)

    has = dict(zip(SIDES[:6], (gx > 0, gx < NGX - 1, gy > 0, gy < NGY - 1, gz > 0, gz < NGZ - 1)))

    def beside(side):
        return tuple(
            lax.rem(at + step + size, size) if step else at
            for at, step, size in zip((gx, gy, gz), side, (NGX, NGY, NGZ))
        )

    def in_plane(i, j):
        return (lax.rem(gx + i, NGX), lax.rem(chip_y + j, NGY // 2) * 2 + core, gz)

    def in_column(k, j):
        return (gx, chip_y * 2 + lax.rem(core + j, 2), lax.rem(gz + k, NGZ))

    def far_first(pairs, n, m):
        return sorted(pairs, key=lambda p: -min(p[0], n - p[0]) - min(p[1], m - p[1]))

    plane_steps = far_first([(i, j) for i in range(NGX) for j in range(NGY // 2) if i or j], NGX, NGY // 2)
    column_steps = far_first([(k, j) for k in range(NGZ) for j in range(2) if k or j], NGZ, 2)
    plane = [in_plane(i, j) for i, j in plane_steps]
    column = [in_column(k, j) for k, j in column_steps]

    inner = (pl.ds(2, BX), pl.ds(8, BY))
    barrier = pltpu.get_barrier_semaphore()
    in_layer = gz == 0
    in_early_column = ((gx == 0) & (chip_y < 2)) | (chip_y == 0)
    is_early = in_layer & in_early_column

    def signal(sem, partners):
        for partner in partners:
            pl.semaphore_signal(sem, inc=1, device_id=partner, device_id_type=MESH)

    near = [beside(side) for side in XZ + YZ + XY + SIDES[4:6] + SIDES[:4]]
    signal(barrier, near)
    loads = [
        (cells, wc), (flag, wf), (normal, wn),
        (vel.at[0], field.at[(U0,) + inner]),
        (vel.at[pl.ds(1, 2)], field.at[(pl.ds(U1, 2),) + inner]),
        (void, av),
        (coef, field.at[(C,) + inner]),
        (enth, field.at[(H,) + inner]),
    ]
    loads = [pltpu.make_async_copy(s, d, load_sem.at[i]) for i, (s, d) in enumerate(loads)]
    for copy in loads:
        copy.start()

    for device in EARLY:

        @pl.when((gx == device[0]) & (gy == device[1]) & in_layer)
        def _():
            signal(barrier, [(x, y, 0) for x in range(NGX) for y in range(NGY) if (x, y) != device[:2]])

    table = messages(field, tz, tlo, thi, dz)
    copies = [
        [
            pltpu.make_async_remote_copy(
                src_ref=src, dst_ref=dst, send_sem=send_sem.at[kind], recv_sem=recv_sem.at[kind],
                device_id=beside(side), device_id_type=MESH,
            )
            for side, src, dst in table[kind]
        ]
        for kind in range(4)
    ]

    def whole(kind):
        count = sum(math.prod(dst.shape) for _, _, dst in table[kind]) // BZ
        ref = tally.at[pl.ds(0, count)]
        return pltpu.make_async_remote_copy(
            src_ref=ref, dst_ref=ref, send_sem=send_sem.at[kind], recv_sem=recv_sem.at[kind],
            device_id=beside(SIDES[0]), device_id_type=MESH,
        )

    def send(kind):
        for copy in copies[kind]:
            copy.start()

    def receive(kind):
        whole(kind).wait_recv()
        for side in SIDES[:6]:
            dim = [i for i in range(3) if side[i]][0]

            @pl.when(jnp.logical_not(has[side]))
            def _():
                for to, _, dst in table[kind]:
                    if to[dim] == -side[dim]:
                        dst[...] = jnp.zeros(dst.shape, jnp.float32)

    lane8 = lax.broadcasted_iota(jnp.int32, (8, BZ), 1)
    sub8 = lax.broadcasted_iota(jnp.int32, (8, BZ), 0)
    lane32 = lax.broadcasted_iota(jnp.int32, (BY, BZ), 1)
    row32 = lax.broadcasted_iota(jnp.int32, (BY, BZ), 0)
    first, last = lane32 == 0, lane32 == BZ - 1
    first8, last8 = lane8 == 0, lane8 == BZ - 1
    place = lane8 % 4
    low_lane = place == 1
    y_group = lane8 // 4 % 4
    ends_half = jnp.where(first8, 0.5, jnp.where(last8, -0.5, 0.0))
    ends_half32 = jnp.where(first, 0.5, jnp.where(last, -0.5, 0.0))

    def turn(v, by, axis=1):
        size = v.shape[axis]
        return pltpu.roll(v, by % size, axis=axis) if by % size else v

    def pack(values, acc, x):
        for b in range(4):
            k = 4 * x + b
            turned = turn(values[8 * b : 8 * b + 8], 4 * k + 2)
            acc = turned if acc is None else jnp.where(lane8 // 4 == k, turned, acc)
        return acc

    def pair(low, high):
        return jnp.where(low_lane, low, high)

    def swap(v):
        return jnp.where(low_lane, turn(v, -1), turn(v, 1))

    def ends(swapped, x):
        return jnp.concatenate([turn(swapped, -4 * (4 * x + b) - 2) for b in range(4)], axis=0)

    def ends_row(swapped, b):
        row, k = (7, 3) if b < 0 else (0, 0)
        out = None
        spread = jnp.broadcast_to(swapped[row : row + 1], (8, BZ))
        for x in range(BX):
            turned = turn(spread, -4 * (4 * x + k) - 2)
            out = turned if out is None else jnp.where(sub8 == x, turned, out)
        return out

    def around_z(v, e):
        f, l = (first, last) if v.shape[0] == BY else (first8, last8)
        return jnp.where(l, e, turn(v, -1)), jnp.where(f, e, turn(v, 1))

    def around_y(f, x):
        return field[f, x + 2, 9:41, :], field[f, x + 2, 7:39, :]

    def centre(f, x):
        return field[f, x + 2, ROWS, :]

    def row_of_field(f, r):
        return field[f, 2:10, r, :]

    def diagonal(side, q):
        a, b, _ = side
        lo, hi = ((XZ + YZ).index((a, b, c)) for c in SIGNS)
        return pair(dz[lo, q], dz[hi, q])

    xm_side, xp_side, ym_side, yp_side, zm_side, zp_side = SIDES[:6]

    for copy in loads[0:3]:
        copy.wait()
    where = wc[...]
    row_at = where // BZ
    lane_at = where - row_at * BZ
    code = jnp.where(wf[...] > 0, wf[...] + 4 * (wn[...] // 2), 0).astype(jnp.float32)
    up256 = lax.broadcasted_iota(jnp.int32, (BX * BY, BZ), 0)
    up128 = lax.broadcasted_iota(jnp.int32, (BZ, BZ), 0)
    for s in range(SLOTS):
        hot_row[:, s * BZ : (s + 1) * BZ] = jnp.where(up256 == row_at[s : s + 1], 1.0, 0.0).astype(jnp.bfloat16)
        hot_lane[:, s * BZ : (s + 1) * BZ] = jnp.where(up128 == lane_at[s : s + 1], code[s : s + 1], 0.0).astype(jnp.bfloat16)
    grid[...] = lax.dot_general(
        hot_row[...], hot_lane[...], (((1,), (1,)), ((), ())), preferred_element_type=jnp.float32
    )
    for copy in loads[3:]:
        copy.wait()

    t_b = t_c = t_u0 = t_u1 = t_u2 = None
    for x in range(BX):
        a = av[x]
        g = grid[x * BY : (x + 1) * BY, :]
        not_x = g > 3.5
        is_z = g > 7.5
        s = g - jnp.where(not_x, 4.0, 0.0) - jnp.where(is_z, 4.0, 0.0)
        u0, u1, u2 = centre(U0, x), centre(U1, x), centre(U2, x)
        parallel = (
            jnp.where(not_x, u0 * u0, 0.0)
            + jnp.where(not_x & jnp.logical_not(is_z), 0.0, u1 * u1)
            + jnp.where(is_z, 0.0, u2 * u2)
        )
        speed = jnp.sqrt(parallel + 0.25)
        liquid = 1.0 - a
        evap = 1.5 * a * s * s
        root = jnp.where(s > 1.5, 2.0 * 1.4142135623730951, s)
        heat[x] = liquid * speed * s + 0.6 * liquid * root + evap
        slope = jnp.where(row32 == BY - 1, 0.0, turn(u1, -1, 0)) - jnp.where(row32 == 0, 0.0, turn(u1, 1, 0))
        slope = slope + (jnp.where(last, 0.0, turn(u2, -1)) - jnp.where(first, 0.0, turn(u2, 1)))
        if x < BX - 1:
            slope = slope + centre(U0, x + 1)
        if x > 0:
            slope = slope - centre(U0, x - 1)
        b = EXPANSION * (0.5 * evap) - 0.5 * slope
        field[BP, x + 2, ROWS, :] = b
        t_b = pack(b, t_b, x)
        t_c = pack(centre(C, x), t_c, x)
        t_u0 = pack(u0, t_u0, x)
        t_u1 = pack(u1, t_u1, x)
        t_u2 = pack(u2, t_u2, x)
    for i, t in ((TB, t_b), (TC, t_c), (TU0, t_u0), (TU1, t_u1), (TU2, t_u2)):
        tz[i] = t

    greeters = jnp.where(in_layer, len(EARLY) - is_early.astype(jnp.int32), 0)
    pl.semaphore_wait(barrier, len(near) + greeters)
    send(FIRST)
    send(OUTER)
    signal(wave.at[0], [beside(side) for side in SIDES[:4]])
    signal(wave.at[3], [beside(side) for side in SIDES[4:6]])

    t_h = None
    half = 0.5 / SCALE
    for x in range(BX):
        t_h = pack(centre(H, x), t_h, x)
        c = centre(C, x)
        if x < BX - 1:
            cx[x + 2] = half * (c + centre(C, x + 1))
        cy[x + 1, 0:32] = half * (c + turn(c, 1, 0))
        czp[x + 1] = half * jnp.where(last, c, c + turn(c, -1))
        czm[x + 1] = half * jnp.where(first, c, c + turn(c, 1))
    tz[TH] = t_h
    send(ENTH)

    pl.semaphore_wait(wave.at[0], 4)
    signal(wave.at[1], [beside((0, 2, 0)), beside((0, -2, 0))])
    pl.semaphore_wait(wave.at[3], 2)
    signal(wave.at[4], [beside((0, 0, 2)), beside((0, 0, -2))])

    def low_high(v):
        return v[0:8], v[8:24], v[24:32]

    def y_ends(v, f, x):
        a, m, z = low_high(v)
        a = a + jnp.where(sub8 == 0, 0.5 * field[f, x + 2, 7:8, :], 0.0)
        z = z - jnp.where(sub8 == 7, 0.5 * field[f, x + 2, 40:41, :], 0.0)
        return jnp.concatenate([a, m, z], axis=0)

    has_z = jnp.where(low_lane, has[zm_side].astype(jnp.float32), has[zp_side].astype(jnp.float32))

    def z_inside(t):
        return jnp.where(low_lane, turn(t, -1), turn(t, 1))

    def z_around_x(v, before, after):
        return (
            jnp.where(lane8 >= 112, turn(after, -16), turn(v, -16)),
            jnp.where(lane8 < 16, turn(before, 16), turn(v, 16)),
        )

    def z_around_y(v, before, after):
        up = jnp.where(y_group == 3, turn(after, 12), turn(v, -4))
        down = jnp.where(y_group == 0, turn(before, -12), turn(v, 4))
        return (
            turn(jnp.where(sub8 == 0, up, v), -1, 0),
            turn(jnp.where(sub8 == 7, down, v), 1, 0),
        )

    zero = jnp.zeros((8, BZ), jnp.float32)
    receive(FIRST)
    after, before = z_around_x(zero, diagonal(xm_side, 0), diagonal(xp_side, 0))
    b = pair(tlo[TB], thi[TB]) - 0.5 * (after - before)
    after, before = z_around_y(zero, diagonal(ym_side, 1), diagonal(yp_side, 1))
    b = b - 0.5 * (after - before) + jnp.where(low_lane, -0.5, 0.5) * z_inside(tz[TU2])
    s_w0 = swap(has_z * b)

    s_u2 = swap(pair(tlo[TU2], thi[TU2]))
    s_c = swap(pair(tlo[TC], thi[TC]))
    for x in range(BX):
        b = centre(BP, x) + ends_half32 * ends(s_u2, x)
        b = y_ends(b, U1, x)
        if x == 0:
            b = b + 0.5 * field[U0, 1, ROWS, :]
        if x == BX - 1:
            b = b - 0.5 * field[U0, 10, ROWS, :]
        field[W0, x + 2, ROWS, :] = b
        c = centre(C, x)
        e = ends(s_c, x)
        czp[x + 1] = czp[x + 1] + jnp.where(last, half * e, 0.0)
        czm[x + 1] = czm[x + 1] + jnp.where(first, half * e, 0.0)
        cy[x + 1, 0:1] = half * (c[0:1] + field[C, x + 2, 7:8, :])
        cy[x + 1, 32:33] = half * (c[31:32] + field[C, x + 2, 40:41, :])
    cx[1] = half * (centre(C, 0) + centre(C, -1))
    cx[9] = half * (centre(C, 7) + centre(C, 8))
    for x, own, sign, side, inside in ((-1, 0, -0.5, xm_side, 7), (BX, BX - 1, 0.5, xp_side, 0)):
        b = centre(BP, x) + sign * centre(U0, own)
        b = y_ends(b, U1, x) + ends_half32 * ends(swap(diagonal(side, 1)), inside)
        field[W0, x + 2, ROWS, :] = jnp.where(has[side], b, 0.0)
    for r, own, sign, side in ((7, 8, -0.5, ym_side), (40, 39, 0.5, yp_side)):
        b = row_of_field(BP, r) + sign * row_of_field(U1, own)
        b = b + jnp.where(sub8 == 0, 0.5 * field[U0, 1, r : r + 1, :], 0.0)
        b = b - jnp.where(sub8 == 7, 0.5 * field[U0, 10, r : r + 1, :], 0.0)
        b = b + ends_half * ends_row(swap(diagonal(side, 0)), side[1])
        b = jnp.where(has[side], b, 0.0)
        for x in range(BX):
            field[W0, x + 2, r : r + 1, :] = b[x : x + 1]
    def operator(f, x, e):
        v = centre(f, x)
        yp, ym = around_y(f, x)
        zp, zm = around_z(v, e)
        out = cx[x + 2] * (v - centre(f, x + 1)) + cx[x + 1] * (v - centre(f, x - 1))
        out = out + (cy[x + 1, 1:33] * (v - yp) + cy[x + 1, 0:32] * (v - ym))
        return out + (czp[x + 1] * (v - zp) + czm[x + 1] * (v - zm))

    t_w = None
    for x in range(BX):
        out = operator(W0, x, ends(s_w0, x))
        field[W1, x + 2, ROWS, :] = out
        t_w = pack(out, t_w, x)
    tz[TW] = t_w
    send(IMAGE)
    pl.semaphore_wait(wave.at[1], 2)
    signal(wave.at[2], [in_plane(i, 0) for i in range(1, NGX)])

    @pl.when(in_layer)
    def _():
        pl.semaphore_wait(wave.at[4], 2)
        signal(ready, [in_column(k, 0) for k in range(1, NGZ)])


    def fold(v):
        return (v[0:8] + v[8:16]) + (v[16:24] + v[24:32])

    def plus(acc, v):
        v = fold(v)
        return v if acc is None else acc + v

    m = [None] * 6
    for x in range(BX):
        v, out = centre(W0, x), centre(W1, x)
        m[0], m[1], m[2] = plus(m[0], v * v), plus(m[1], v * out), plus(m[2], out * out)
    receive(OUTER)
    for x, side, inside in ((-1, xm_side, 7), (BX, xp_side, 0)):
        c = centre(C, x)
        if x < 0:
            cx[0] = half * (c + centre(C, -2))
        else:
            cx[10] = half * (c + centre(C, 9))
        after, before = around_y(C, x)
        cy[x + 1, 0:32] = half * (c + before)
        cy[x + 1, 32:33] = half * (c[31:32] + after[31:32])
        after, before = around_z(c, ends(swap(diagonal(side, 2)), inside))
        czp[x + 1] = half * (c + after)
        czm[x + 1] = half * (c + before)
    z_edge = jnp.where(has[zm_side], 0.0, 1.0)
    y_edge = jnp.where(has[ym_side], 0.0, 1.0)
    x_edge = jnp.where(has[xm_side], 0.0, 1.0)
    for x in range(BX):
        low = jnp.where(first, czm[x + 1], 0.0) * z_edge
        low = low + jnp.where(row32 == 0, cy[x + 1, 0:32], 0.0) * y_edge
        if x == 0:
            low = low + cx[1] * x_edge
        zlow[x] = low

    def face_values(t, qx, qy):
        lo, hi, own = tlo[t], thi[t], tz[t]
        v = pair(lo, hi)
        outer = jnp.where(low_lane, turn(lo, 1), turn(hi, -1))
        return (
            (v, outer, z_inside(own))
            + z_around_x(v, diagonal(xm_side, qx), diagonal(xp_side, qx))
            + z_around_y(v, diagonal(ym_side, qy), diagonal(yp_side, qy))
        )

    def row_values(f, q, r, beyond, own, side):
        v = row_of_field(f, r)
        after = jnp.where(sub8 == 7, field[f, 10, r : r + 1, :], turn(v, -1, 0))
        before = jnp.where(sub8 == 0, field[f, 1, r : r + 1, :], turn(v, 1, 0))
        zp, zm = around_z(v, ends_row(swap(diagonal(side, q)), side[1]))
        return v, row_of_field(f, beyond), row_of_field(f, own), after, before, zp, zm

    def weights(values, mask):
        c, *near_c = values
        return [mask * (half * (c + cn)) for cn in near_c]

    def applied(weight, values):
        v, *near_v = values
        terms = [w * (v - vn) for w, vn in zip(weight, near_v)]
        return ((terms[0] + terms[1]) + (terms[2] + terms[3])) + (terms[4] + terms[5])

    face_weights = weights(face_values(TC, 2, 2), has_z)
    rows_beyond = ((7, 6, 8, ym_side), (40, 41, 39, yp_side))
    row_weights = [weights(row_values(C, 2, *at), has[at[3]].astype(jnp.float32)) for at in rows_beyond]

    def image_row(at):
        out = applied(row_weights[at], row_values(W1, 4, *rows_beyond[at]))
        r = rows_beyond[at][0]
        for x in range(BX):
            field[W2, x + 2, r : r + 1, :] = out[x : x + 1]


    receive(IMAGE)
    s_w2 = swap(applied(face_weights, face_values(TW, 4, 4)))
    image_row(1)
    s_w1 = swap(pair(tlo[TW], thi[TW]))
    for x in range(BX):
        out = operator(W1, x, ends(s_w1, x))
        field[W2, x + 2, ROWS, :] = out
        v = centre(W1, x)
        m[3], m[4] = plus(m[3], v * out), plus(m[4], out * out)

    def image_plane(x, side, inside):
        out = operator(W1, x, ends(swap(diagonal(side, 4)), inside))
        field[W2, x + 2, ROWS, :] = jnp.where(has[side], out, 0.0)

    image_plane(BX, xp_side, 0)
    for x in range(BX):
        v = centre(W2, x)
        dx = v - centre(W2, x + 1)
        dy = v - field[W2, x + 2, 9:41, :]
        dz_ = v - jnp.where(last, ends(s_w2, x), turn(v, -1))
        m[5] = plus(
            m[5],
            (cx[x + 2] * (dx * dx) + cy[x + 1, 1:33] * (dy * dy)) + (czp[x + 1] * (dz_ * dz_) + zlow[x] * (v * v)),
        )

    row = jnp.zeros((1, BZ), jnp.float32)
    for i in range(6):
        row = jnp.where(lane8[0:1] == i, jnp.sum(m[i], keepdims=True), row)

    def sum_copy(phase, slot, partner):
        return pltpu.make_async_remote_copy(
            src_ref=reduce.at[phase, pl.ds(0, 1)], dst_ref=reduce.at[phase, pl.ds(slot + 1, 1)],
            send_sem=sum_send.at[phase], recv_sem=sum_recv.at[phase], device_id=partner, device_id_type=MESH,
        )

    def sum_whole(phase, count):
        ref = tally.at[pl.ds(0, count)]
        return pltpu.make_async_remote_copy(
            src_ref=ref, dst_ref=ref, send_sem=sum_send.at[phase], recv_sem=sum_recv.at[phase],
            device_id=plane[0], device_id_type=MESH,
        )

    def start_sum(phase, group):
        for slot, partner in enumerate(group):
            sum_copy(phase, slot, partner).start()

    me = (gx * NGY + gy) * NGZ + gz
    to_early = [
        pltpu.make_async_remote_copy(
            src_ref=reduce.at[0, pl.ds(0, 1)], dst_ref=direct.at[pl.ds(me, 1)], send_sem=sum_send.at[2],
            recv_sem=sum_recv.at[2], device_id=device, device_id_type=MESH,
        )
        for device in EARLY
    ]
    reduce[0, 0:1, :] = row

    pl.semaphore_wait(wave.at[2], NGX - 1)
    start_sum(0, plane)

    @pl.when(jnp.logical_not(in_layer))
    def _():
        pl.semaphore_wait(wave.at[4], 2)
        pl.semaphore_wait(ready, 1)

    for device, copy in zip(EARLY, to_early):
        pl.when((gx != device[0]) | (gy != device[1]) | (gz != device[2]))(copy.start)
    signal(wave.at[5], [in_column(0, 1)])

    image_plane(-1, xm_side, 7)
    image_row(0)
    copy_u = pltpu.make_async_copy(field.at[(U0,) + inner], u_out.at[0], copy_sem.at[0])
    copy_u.start()
    copy_v = pltpu.make_async_copy(field.at[(pl.ds(U1, 2),) + inner], u_out.at[pl.ds(1, 2)], copy_sem.at[2])
    copy_v.start()
    copy_w = pltpu.make_async_copy(field.at[(pl.ds(W0, 3),) + inner], w_out, copy_sem.at[1])
    copy_w.start()
    for i, (f, swapped) in enumerate(((W0, s_w0), (W1, s_w1), (W2, s_w2))):
        for x in range(BX):
            c = (0.5 / SCALE) * centre(C, x)
            g_out[i, 0, x] = c * (centre(f, x + 1) - centre(f, x - 1))
            after, before = around_y(f, x)
            g_out[i, 1, x] = c * (after - before)
            after, before = around_z(centre(f, x), ends(swapped, x))
            g_out[i, 2, x] = c * (after - before)
    receive(ENTH)
    s_h = swap(pair(tlo[TH], thi[TH]))
    for x in range(BX):
        h = centre(H, x)
        hyp, hym = around_y(H, x)
        hzp, hzm = around_z(h, ends(s_h, x))
        laplace = centre(H, x + 1) + centre(H, x - 1) + hyp + hym + hzp + hzm - 6.0 * h
        h_out[x] = h + DIFFUSE * laplace + HEATING * heat[x]
    copy_u.wait()
    copy_v.wait()
    copy_w.wait()
    for kind in range(4):
        whole(kind).wait_send()

    pl.semaphore_wait(wave.at[5], 1)
    sum_whole(0, 15).wait_recv()
    high, low = row_total(reduce[0])
    reduce[1, 0:1, :] = jnp.where(lane8 < 8, high, turn(low, 8))[0:1]

    @pl.when(jnp.logical_not(in_early_column))
    def _():
        start_sum(1, column)

    @pl.when(in_early_column)
    def _():
        for slot, partner in enumerate(column):
            pl.when(partner[2] != 0)(sum_copy(1, slot, partner).start)

    @pl.when(is_early)
    def _():
        direct[pl.ds(me, 1), :] = row
        sum_whole(2, DEVICES - 1).wait_recv()
        high, low = row_total(direct[...])
        total[0] = high
        total[1] = low

    @pl.when(jnp.logical_not(is_early))
    def _():
        sum_whole(1, 15).wait_recv()
        high, low = row_total(reduce[1])
        total[0] = high
        total[1] = low + turn(high, -8)

    high, low = total[0], total[1]
    high, low = quick_sum(high, low)

    def spread(v, i):
        return jnp.broadcast_to(v[:, i : i + 1], (8, BZ))

    moments = [(spread(high, i), spread(low, i)) for i in range(6)]
    for i, v in enumerate(solve_moments(moments)):
        c_out[i] = v
    sum_whole(0, 15).wait_send()

    @pl.when(jnp.logical_not(in_early_column))
    def _():
        sum_whole(1, 15).wait_send()
        sum_whole(2, len(EARLY)).wait_send()

    @pl.when(in_early_column & in_layer)
    def _():
        sum_whole(1, 14).wait_send()
        sum_whole(2, len(EARLY) - 1).wait_send()

    @pl.when(in_early_column & jnp.logical_not(in_layer))
    def _():
        sum_whole(1, 13).wait_send()
        sum_whole(2, len(EARLY)).wait_send()


def finish(w, g, u, h, c, vel_out, p_out, h_out, vel, p, sem):
    copy_h = pltpu.make_async_copy(h, h_out, sem.at[0])
    copy_h.start()
    c0, c1, c2 = (jnp.concatenate([c[i]] * 4, axis=0) for i in range(3))
    copies = [copy_h]
    for i in range(3):
        for x in range(BX):
            vel[i, x] = u[i, x] - (c0 * g[0, i, x] + c1 * g[1, i, x] + c2 * g[2, i, x])
        copy = pltpu.make_async_copy(vel.at[i], vel_out.at[i], sem.at[1 + i])
        copy.start()
        copies.append(copy)
    scaled = tuple(v * (1.0 / SCALE) for v in (c0, c1, c2))
    for x in range(BX):
        p[x] = scaled[0] * w[0, x] + scaled[1] * w[1, x] + scaled[2] * w[2, x]
    copy_p = pltpu.make_async_copy(p, p_out, sem.at[4])
    copy_p.start()
    for copy in copies + [copy_p]:
        copy.wait()


def shards(*args):
    block = (BX, BY, BZ)
    f32 = jnp.float32
    any_ref = pl.BlockSpec(memory_space=pl.ANY)
    vmem = pl.BlockSpec(memory_space=pltpu.VMEM)
    results = pl.pallas_call(
        kernel,
        out_shape=(
            jax.ShapeDtypeStruct((3,) + block, f32),
            jax.ShapeDtypeStruct((3, 3) + block, f32),
            jax.ShapeDtypeStruct((3,) + block, f32),
            jax.ShapeDtypeStruct(block, f32),
            jax.ShapeDtypeStruct((3, 8, BZ), f32),
        ),
        in_specs=[any_ref] * 7,
        out_specs=(vmem,) * 5,
        scratch_shapes=[
            pltpu.VMEM((FIELDS, BX + 4, BY + 16, BZ), f32),
            pltpu.VMEM((7, 8, BZ), f32),
            pltpu.VMEM((7, 8, BZ), f32),
            pltpu.VMEM((7, 8, BZ), f32),
            pltpu.VMEM((8, 5, 8, BZ), f32),
            pltpu.VMEM((BX + 3, BY, BZ), f32),
            pltpu.VMEM((BX + 2, BY + 8, BZ), f32),
            pltpu.VMEM((BX + 2, BY, BZ), f32),
            pltpu.VMEM((BX + 2, BY, BZ), f32),
            pltpu.VMEM(block, f32),
            pltpu.VMEM(block, f32),
            pltpu.VMEM((SLOTS, BZ), jnp.int32),
            pltpu.VMEM((SLOTS, BZ), jnp.int32),
            pltpu.VMEM((SLOTS, BZ), jnp.int32),
            pltpu.VMEM((BX * BY, SLOTS * BZ), jnp.bfloat16),
            pltpu.VMEM((BZ, SLOTS * BZ), jnp.bfloat16),
            pltpu.VMEM((BX * BY, BZ), f32),
            pltpu.VMEM(block, f32),
            pltpu.VMEM((2, 16, BZ), f32),
            pltpu.VMEM((DEVICES, BZ), f32),
            pltpu.VMEM((2, 8, BZ), f32),
            pltpu.VMEM((1024, BZ), f32),
            pltpu.SemaphoreType.DMA((8,)),
            pltpu.SemaphoreType.DMA((3,)),
            pltpu.SemaphoreType.DMA((4,)),
            pltpu.SemaphoreType.DMA((4,)),
            pltpu.SemaphoreType.DMA((3,)),
            pltpu.SemaphoreType.DMA((3,)),
            pltpu.SemaphoreType.REGULAR,
            pltpu.SemaphoreType.REGULAR((6,)),
        ],
        compiler_params=pltpu.CompilerParams(
            collective_id=0, has_side_effects=True, vmem_limit_bytes=32 * 1024 * 1024
        ),
        name="simple_step",
    )(*[pltpu.with_memory_space_constraint(a, pltpu.HBM) for a in args])
    results = [pltpu.with_memory_space_constraint(r, pltpu.VMEM) for r in results]
    return tuple(
        pl.pallas_call(
            finish,
            out_shape=(
                jax.ShapeDtypeStruct((3,) + block, f32),
                jax.ShapeDtypeStruct(block, f32),
                jax.ShapeDtypeStruct(block, f32),
            ),
            in_specs=[vmem] * 5,
            out_specs=(pl.BlockSpec(memory_space=pltpu.HBM),) * 3,
            scratch_shapes=[
                pltpu.VMEM((3,) + block, f32),
                pltpu.VMEM(block, f32),
                pltpu.SemaphoreType.DMA((5,)),
            ],
            compiler_params=pltpu.CompilerParams(vmem_limit_bytes=8 * 1024 * 1024),
            name="finish",
        )(*results)
    )


def solution(mesh):
    in_specs = (
        P(None, "gx", "gy", "gz"),
        P("gx", "gy", "gz"),
        P("gx", "gy", "gz"),
        P("gx", "gy", "gz"),
        P(("gx", "gy", "gz"), None),
        P(("gx", "gy", "gz"), None),
        P(("gx", "gy", "gz"), None),
    )
    out_specs = (P(None, "gx", "gy", "gz"), P("gx", "gy", "gz"), P("gx", "gy", "gz"))
    return jax.shard_map(shards, mesh=mesh, in_specs=in_specs, out_specs=out_specs, check_vma=False)
```

```python
import math

import jax
import jax.numpy as jnp
from jax import lax
from jax.experimental import pallas as pl
from jax.experimental.pallas import tpu as pltpu
from jax.sharding import PartitionSpec as P

MESH = pl.DeviceIdType.MESH
NGX, NGY, NGZ = 4, 8, 8
BX, BY, BZ = 8, 32, 128
SLOTS = 16
DIFFUSE = 0.1
HEATING = 0.5
EXPANSION = 1.5
SCALE = 16.0
H, C, U0, BP, U1, U2, W0, W1, W2 = range(9)
FIELDS = 9
TU0, TU2, TU1, TB, TC, TH, TW = range(7)
ROWS = slice(8, 40)
SIGNS = (-1, 1)
XZ = tuple((a, 0, c) for a in SIGNS for c in SIGNS)
YZ = tuple((0, b, c) for b in SIGNS for c in SIGNS)
XY = tuple((a, b, 0) for a in SIGNS for b in SIGNS)
SIDES = ((-1, 0, 0), (1, 0, 0), (0, -1, 0), (0, 1, 0), (0, 0, -1), (0, 0, 1)) + XY + XZ + YZ
FIRST, OUTER, ENTH, IMAGE = range(4)
PIVOT_FLOOR = 1e-9
EARLY_CHIPS = ((0, 0), (1, 0), (3, 0), (2, 0), (0, 1))
EARLY = tuple((x, 2 * y + c, 0) for x, y in EARLY_CHIPS for c in (1, 0))
DEVICES = 256


def two_sum(a, b):
    s = a + b
    t = s - a
    return s, (a - (s - t)) + (b - t)


def quick_sum(a, b):
    s = a + b
    return s, b - (s - a)


def split(a):
    t = 4097.0 * a
    high = t - (t - a)
    return high, a - high


def two_mul(a, b):
    p = a * b
    ah, al = split(a)
    bh, bl = split(b)
    return p, ((ah * bh - p) + ah * bl + al * bh) + al * bl


def df_sub(a, b):
    s, e = two_sum(a[0], -b[0])
    return quick_sum(s, e + (a[1] - b[1]))


def df_mul(a, b):
    p, e = two_mul(a[0], b[0])
    return quick_sum(p, e + (a[0] * b[1] + a[1] * b[0]))


def df_over(a, b, inverse):
    q = a[0] * inverse
    p, e = two_mul(q, b[0])
    rest = ((a[0] - p) - e) + (a[1] - q * b[1])
    return quick_sum(q, rest * inverse)


def solve_moments(m):
    i0 = 1.0 / m[1][0]
    l10 = df_over(m[2], m[1], i0)
    l20 = df_over(m[3], m[1], i0)
    d1 = df_sub(m[3], df_mul(l10, m[2]))
    e12 = df_sub(m[4], df_mul(l10, m[3]))
    y1 = df_sub(m[1], df_mul(l10, m[0]))
    y2 = df_sub(m[2], df_mul(l20, m[0]))
    d2 = df_sub(m[5], df_mul(l20, m[3]))
    ok1 = d1[0] > PIVOT_FLOOR * m[3][0]
    i1 = jnp.where(ok1, 1.0 / d1[0], 0.0)
    l21 = df_over(e12, d1, i1)
    d2 = df_sub(d2, df_mul(l21, e12))
    y2 = df_sub(y2, df_mul(l21, y1))
    ok2 = ok1 & (d2[0] > PIVOT_FLOOR * m[5][0])
    c2 = jnp.where(ok2, y2[0] / d2[0], 0.0)
    p, e = two_mul(e12[0], c2)
    c1 = (((y1[0] - p) - e) + (y1[1] - e12[1] * c2)) * i1
    p1, e1 = two_mul(m[2][0], c1)
    p2, e2 = two_mul(m[3][0], c2)
    s, t1 = two_sum(m[0][0], -p1)
    s, t2 = two_sum(s, -p2)
    rest = (t1 - e1) + (t2 - e2) + (m[0][1] - m[2][1] * c1 - m[3][1] * c2)
    return (s + rest) * i0, c1, c2


def row_total(rows):
    parts = [(rows[i : i + 8], None) for i in range(0, rows.shape[0], 8)]
    while len(parts) > 1:
        merged = []
        for (a, low_a), (b, low_b) in zip(parts[0::2], parts[1::2]):
            s, e = two_sum(a, b)
            merged.append((s, e if low_a is None else e + (low_a + low_b)))
        parts = merged
    s, e = parts[0]
    for step in (4, 2, 1):
        other = pltpu.roll(s, step, axis=0)
        e = e + pltpu.roll(e, step, axis=0)
        s, more = two_sum(s, other)
        e = e + more
    return s, e


def opposite(side):
    return tuple(-v for v in side)


def messages(field, tz, tlo, thi, dz):
    xs, xd = {-1: 2, 1: 9}, {-1: 10, 1: 1}
    xs1, xd1 = {-1: 3, 1: 8}, {-1: 11, 1: 0}
    ys, yd = {-1: 8, 1: 39}, {-1: 40, 1: 7}
    xs2, xd2 = {-1: pl.ds(2, 2), 1: pl.ds(8, 2)}, {-1: pl.ds(10, 2), 1: pl.ds(0, 2)}
    ys2, yd2 = {-1: pl.ds(8, 2), 1: pl.ds(38, 2)}, {-1: pl.ds(40, 2), 1: pl.ds(6, 2)}
    rows, planes = pl.ds(8, BY), pl.ds(2, BX)
    table = [[], [], [], []]
    for side in XZ + YZ + XY + SIDES[:2] + SIDES[4:6] + SIDES[2:4]:
        a, b, c = side
        far = thi if c < 0 else tlo
        slot = (XZ + YZ).index(opposite(side)) if side in XZ + YZ else None
        enth = outer = []
        if side in XZ:
            first = [(tz.at[pl.ds(TU0, 2)], dz.at[slot, pl.ds(0, 2)])]
            outer = [(tz.at[TC], dz.at[slot, 2])]
            image = [(tz.at[TW], dz.at[slot, 4])]
        elif side in YZ:
            first = [(tz.at[pl.ds(TU2, 2)], dz.at[slot, pl.ds(0, 2)])]
            outer = [(tz.at[TC], dz.at[slot, 2])]
            image = [(tz.at[TW], dz.at[slot, 4])]
        elif side in XY:
            first = [(field.at[pl.ds(U0, 3), xs[a], ys[b]], field.at[pl.ds(U0, 3), xd[a], yd[b]])]
            outer = [(field.at[C, xs[a], ys[b]], field.at[C, xd[a], yd[b]])]
            image = [(field.at[W1, xs[a], ys[b]], field.at[W1, xd[a], yd[b]])]
        elif a:
            first = [(field.at[pl.ds(C, 3), xs[a], rows], field.at[pl.ds(C, 3), xd[a], rows])]
            outer = [(field.at[C, xs1[a], rows], field.at[C, xd1[a], rows])]
            enth = [(field.at[H, xs[a], rows], field.at[H, xd[a], rows])]
            image = [(field.at[W1, xs2[a], rows], field.at[W1, xd2[a], rows])]
        elif b:
            first = [
                (field.at[C, planes, ys2[b]], field.at[C, planes, yd2[b]]),
                (field.at[pl.ds(BP, 2), planes, ys[b]], field.at[pl.ds(BP, 2), planes, yd[b]]),
            ]
            enth = [(field.at[H, planes, ys[b]], field.at[H, planes, yd[b]])]
            image = [(field.at[W1, planes, ys2[b]], field.at[W1, planes, yd2[b]])]
        else:
            first = [(tz.at[pl.ds(TU2, 4)], far.at[pl.ds(TU2, 4)])]
            enth = [(tz.at[TH], far.at[TH])]
            image = [(tz.at[TW], far.at[TW])]
        for kind, pairs in ((FIRST, first), (OUTER, outer), (ENTH, enth), (IMAGE, image)):
            table[kind] += [(side, src, dst) for src, dst in pairs]
    return table


def kernel(
    vel, coef, enth, void, cells, normal, flag,
    w_out, g_out, u_out, h_out, c_out,
    field, tz, tlo, thi, dz, cx, cy, czm, czp, zlow, av, wc, wn, wf, hot_row, hot_lane, grid,
    heat, reduce, direct, total, tally, load_sem, copy_sem, send_sem, recv_sem, sum_send, sum_recv, ready, wave,
):
    gx, gy, gz = lax.axis_index("gx"), lax.axis_index("gy"), lax.axis_index("gz")
    chip_y, core = gy // 2, lax.rem(gy, 2)

    has = dict(zip(SIDES[:6], (gx > 0, gx < NGX - 1, gy > 0, gy < NGY - 1, gz > 0, gz < NGZ - 1)))

    def beside(side):
        return tuple(
            lax.rem(at + step + size, size) if step else at
            for at, step, size in zip((gx, gy, gz), side, (NGX, NGY, NGZ))
        )

    def in_plane(i, j):
        return (lax.rem(gx + i, NGX), lax.rem(chip_y + j, NGY // 2) * 2 + core, gz)

    def in_column(k, j):
        return (gx, chip_y * 2 + lax.rem(core + j, 2), lax.rem(gz + k, NGZ))

    def far_first(pairs, n, m):
        return sorted(pairs, key=lambda p: -min(p[0], n - p[0]) - min(p[1], m - p[1]))

    plane_steps = far_first([(i, j) for i in range(NGX) for j in range(NGY // 2) if i or j], NGX, NGY // 2)
    column_steps = far_first([(k, j) for k in range(NGZ) for j in range(2) if k or j], NGZ, 2)
    plane = [in_plane(i, j) for i, j in plane_steps]
    column = [in_column(k, j) for k, j in column_steps]

    inner = (pl.ds(2, BX), pl.ds(8, BY))
    barrier = pltpu.get_barrier_semaphore()
    in_layer = gz == 0
    in_early_column = ((gx == 0) & (chip_y < 2)) | (chip_y == 0)
    is_early = in_layer & in_early_column

    def signal(sem, partners):
        for partner in partners:
            pl.semaphore_signal(sem, inc=1, device_id=partner, device_id_type=MESH)

    near = [beside(side) for side in XZ + YZ + XY + SIDES[4:6] + SIDES[:4]]
    signal(barrier, near)
    loads = [
        (cells, wc), (flag, wf), (normal, wn),
        (vel.at[0], field.at[(U0,) + inner]),
        (vel.at[pl.ds(1, 2)], field.at[(pl.ds(U1, 2),) + inner]),
        (void, av),
        (coef, field.at[(C,) + inner]),
        (enth, field.at[(H,) + inner]),
    ]
    loads = [pltpu.make_async_copy(s, d, load_sem.at[i]) for i, (s, d) in enumerate(loads)]
    for copy in loads:
        copy.start()

    for device in EARLY:

        @pl.when((gx == device[0]) & (gy == device[1]) & in_layer)
        def _():
            signal(barrier, [(x, y, 0) for x in range(NGX) for y in range(NGY) if (x, y) != device[:2]])

    table = messages(field, tz, tlo, thi, dz)
    copies = [
        [
            pltpu.make_async_remote_copy(
                src_ref=src, dst_ref=dst, send_sem=send_sem.at[kind], recv_sem=recv_sem.at[kind],
                device_id=beside(side), device_id_type=MESH,
            )
            for side, src, dst in table[kind]
        ]
        for kind in range(4)
    ]

    def whole(kind):
        count = sum(math.prod(dst.shape) for _, _, dst in table[kind]) // BZ
        ref = tally.at[pl.ds(0, count)]
        return pltpu.make_async_remote_copy(
            src_ref=ref, dst_ref=ref, send_sem=send_sem.at[kind], recv_sem=recv_sem.at[kind],
            device_id=beside(SIDES[0]), device_id_type=MESH,
        )

    def send(kind):
        for copy in copies[kind]:
            copy.start()

    def receive(kind):
        whole(kind).wait_recv()
        for side in SIDES[:6]:
            dim = [i for i in range(3) if side[i]][0]

            @pl.when(jnp.logical_not(has[side]))
            def _():
                for to, _, dst in table[kind]:
                    if to[dim] == -side[dim]:
                        dst[...] = jnp.zeros(dst.shape, jnp.float32)

    lane8 = lax.broadcasted_iota(jnp.int32, (8, BZ), 1)
    sub8 = lax.broadcasted_iota(jnp.int32, (8, BZ), 0)
    lane32 = lax.broadcasted_iota(jnp.int32, (BY, BZ), 1)
    row32 = lax.broadcasted_iota(jnp.int32, (BY, BZ), 0)
    first, last = lane32 == 0, lane32 == BZ - 1
    first8, last8 = lane8 == 0, lane8 == BZ - 1
    place = lane8 % 4
    low_lane = place == 1
    y_group = lane8 // 4 % 4
    ends_half = jnp.where(first8, 0.5, jnp.where(last8, -0.5, 0.0))
    ends_half32 = jnp.where(first, 0.5, jnp.where(last, -0.5, 0.0))

    def turn(v, by, axis=1):
        size = v.shape[axis]
        return pltpu.roll(v, by % size, axis=axis) if by % size else v

    def pack(values, acc, x):
        for b in range(4):
            k = 4 * x + b
            turned = turn(values[8 * b : 8 * b + 8], 4 * k + 2)
            acc = turned if acc is None else jnp.where(lane8 // 4 == k, turned, acc)
        return acc

    def pair(low, high):
        return jnp.where(low_lane, low, high)

    def swap(v):
        return jnp.where(low_lane, turn(v, -1), turn(v, 1))

    def ends(swapped, x):
        return jnp.concatenate([turn(swapped, -4 * (4 * x + b) - 2) for b in range(4)], axis=0)

    def ends_row(swapped, b):
        row, k = (7, 3) if b < 0 else (0, 0)
        out = None
        spread = jnp.broadcast_to(swapped[row : row + 1], (8, BZ))
        for x in range(BX):
            turned = turn(spread, -4 * (4 * x + k) - 2)
            out = turned if out is None else jnp.where(sub8 == x, turned, out)
        return out

    def around_z(v, e):
        f, l = (first, last) if v.shape[0] == BY else (first8, last8)
        return jnp.where(l, e, turn(v, -1)), jnp.where(f, e, turn(v, 1))

    def around_y(f, x):
        return field[f, x + 2, 9:41, :], field[f, x + 2, 7:39, :]

    def centre(f, x):
        return field[f, x + 2, ROWS, :]

    def row_of_field(f, r):
        return field[f, 2:10, r, :]

    def diagonal(side, q):
        a, b, _ = side
        lo, hi = ((XZ + YZ).index((a, b, c)) for c in SIGNS)
        return pair(dz[lo, q], dz[hi, q])

    xm_side, xp_side, ym_side, yp_side, zm_side, zp_side = SIDES[:6]

    for copy in loads[0:3]:
        copy.wait()
    where = wc[...]
    row_at = where // BZ
    lane_at = where - row_at * BZ
    code = jnp.where(wf[...] > 0, wf[...] + 4 * (wn[...] // 2), 0).astype(jnp.float32)
    up256 = lax.broadcasted_iota(jnp.int32, (BX * BY, BZ), 0)
    up128 = lax.broadcasted_iota(jnp.int32, (BZ, BZ), 0)
    for s in range(SLOTS):
        hot_row[:, s * BZ : (s + 1) * BZ] = jnp.where(up256 == row_at[s : s + 1], 1.0, 0.0).astype(jnp.bfloat16)
        hot_lane[:, s * BZ : (s + 1) * BZ] = jnp.where(up128 == lane_at[s : s + 1], code[s : s + 1], 0.0).astype(jnp.bfloat16)
    grid[...] = lax.dot_general(
        hot_row[...], hot_lane[...], (((1,), (1,)), ((), ())), preferred_element_type=jnp.float32
    )
    for copy in loads[3:]:
        copy.wait()

    t_b = t_c = t_u0 = t_u1 = t_u2 = None
    for x in range(BX):
        a = av[x]
        g = grid[x * BY : (x + 1) * BY, :]
        not_x = g > 3.5
        is_z = g > 7.5
        s = g - jnp.where(not_x, 4.0, 0.0) - jnp.where(is_z, 4.0, 0.0)
        u0, u1, u2 = centre(U0, x), centre(U1, x), centre(U2, x)
        parallel = (
            jnp.where(not_x, u0 * u0, 0.0)
            + jnp.where(not_x & jnp.logical_not(is_z), 0.0, u1 * u1)
            + jnp.where(is_z, 0.0, u2 * u2)
        )
        speed = jnp.sqrt(parallel + 0.25)
        liquid = 1.0 - a
        evap = 1.5 * a * s * s
        root = jnp.where(s > 1.5, 2.0 * 1.4142135623730951, s)
        heat[x] = liquid * speed * s + 0.6 * liquid * root + evap
        slope = jnp.where(row32 == BY - 1, 0.0, turn(u1, -1, 0)) - jnp.where(row32 == 0, 0.0, turn(u1, 1, 0))
        slope = slope + (jnp.where(last, 0.0, turn(u2, -1)) - jnp.where(first, 0.0, turn(u2, 1)))
        if x < BX - 1:
            slope = slope + centre(U0, x + 1)
        if x > 0:
            slope = slope - centre(U0, x - 1)
        b = EXPANSION * (0.5 * evap) - 0.5 * slope
        field[BP, x + 2, ROWS, :] = b
        t_b = pack(b, t_b, x)
        t_c = pack(centre(C, x), t_c, x)
        t_u0 = pack(u0, t_u0, x)
        t_u1 = pack(u1, t_u1, x)
        t_u2 = pack(u2, t_u2, x)
    for i, t in ((TB, t_b), (TC, t_c), (TU0, t_u0), (TU1, t_u1), (TU2, t_u2)):
        tz[i] = t

    greeters = jnp.where(in_layer, len(EARLY) - is_early.astype(jnp.int32), 0)
    pl.semaphore_wait(barrier, len(near) + greeters)
    send(FIRST)
    send(OUTER)
    signal(wave.at[0], [beside(side) for side in SIDES[:4]])
    signal(wave.at[3], [beside(side) for side in SIDES[4:6]])

    t_h = None
    half = 0.5 / SCALE
    for x in range(BX):
        t_h = pack(centre(H, x), t_h, x)
        c = centre(C, x)
        if x < BX - 1:
            cx[x + 2] = half * (c + centre(C, x + 1))
        cy[x + 1, 0:32] = half * (c + turn(c, 1, 0))
        czp[x + 1] = half * jnp.where(last, c, c + turn(c, -1))
        czm[x + 1] = half * jnp.where(first, c, c + turn(c, 1))
    tz[TH] = t_h
    send(ENTH)

    pl.semaphore_wait(wave.at[0], 4)
    signal(wave.at[1], [beside((0, 2, 0)), beside((0, -2, 0))])
    pl.semaphore_wait(wave.at[3], 2)
    signal(wave.at[4], [beside((0, 0, 2)), beside((0, 0, -2))])

    def low_high(v):
        return v[0:8], v[8:24], v[24:32]

    def y_ends(v, f, x):
        a, m, z = low_high(v)
        a = a + jnp.where(sub8 == 0, 0.5 * field[f, x + 2, 7:8, :], 0.0)
        z = z - jnp.where(sub8 == 7, 0.5 * field[f, x + 2, 40:41, :], 0.0)
        return jnp.concatenate([a, m, z], axis=0)

    has_z = jnp.where(low_lane, has[zm_side].astype(jnp.float32), has[zp_side].astype(jnp.float32))

    def z_inside(t):
        return jnp.where(low_lane, turn(t, -1), turn(t, 1))

    def z_around_x(v, before, after):
        return (
            jnp.where(lane8 >= 112, turn(after, -16), turn(v, -16)),
            jnp.where(lane8 < 16, turn(before, 16), turn(v, 16)),
        )

    def z_around_y(v, before, after):
        up = jnp.where(y_group == 3, turn(after, 12), turn(v, -4))
        down = jnp.where(y_group == 0, turn(before, -12), turn(v, 4))
        return (
            turn(jnp.where(sub8 == 0, up, v), -1, 0),
            turn(jnp.where(sub8 == 7, down, v), 1, 0),
        )

    zero = jnp.zeros((8, BZ), jnp.float32)
    receive(FIRST)
    after, before = z_around_x(zero, diagonal(xm_side, 0), diagonal(xp_side, 0))
    b = pair(tlo[TB], thi[TB]) - 0.5 * (after - before)
    after, before = z_around_y(zero, diagonal(ym_side, 1), diagonal(yp_side, 1))
    b = b - 0.5 * (after - before) + jnp.where(low_lane, -0.5, 0.5) * z_inside(tz[TU2])
    s_w0 = swap(has_z * b)

    for x, own, sign, side, inside in ((-1, 0, -0.5, xm_side, 7), (BX, BX - 1, 0.5, xp_side, 0)):
        b = centre(BP, x) + sign * centre(U0, own)
        b = y_ends(b, U1, x) + ends_half32 * ends(swap(diagonal(side, 1)), inside)
        field[W0, x + 2, ROWS, :] = jnp.where(has[side], b, 0.0)
    for r, own, sign, side in ((7, 8, -0.5, ym_side), (40, 39, 0.5, yp_side)):
        b = row_of_field(BP, r) + sign * row_of_field(U1, own)
        b = b + jnp.where(sub8 == 0, 0.5 * field[U0, 1, r : r + 1, :], 0.0)
        b = b - jnp.where(sub8 == 7, 0.5 * field[U0, 10, r : r + 1, :], 0.0)
        b = b + ends_half * ends_row(swap(diagonal(side, 0)), side[1])
        b = jnp.where(has[side], b, 0.0)
        for x in range(BX):
            field[W0, x + 2, r : r + 1, :] = b[x : x + 1]
    s_u2 = swap(pair(tlo[TU2], thi[TU2]))
    s_c = swap(pair(tlo[TC], thi[TC]))
    for x in range(BX):
        b = centre(BP, x) + ends_half32 * ends(s_u2, x)
        b = y_ends(b, U1, x)
        if x == 0:
            b = b + 0.5 * field[U0, 1, ROWS, :]
        if x == BX - 1:
            b = b - 0.5 * field[U0, 10, ROWS, :]
        field[W0, x + 2, ROWS, :] = b
        c = centre(C, x)
        e = ends(s_c, x)
        czp[x + 1] = czp[x + 1] + jnp.where(last, half * e, 0.0)
        czm[x + 1] = czm[x + 1] + jnp.where(first, half * e, 0.0)
        cy[x + 1, 0:1] = half * (c[0:1] + field[C, x + 2, 7:8, :])
        cy[x + 1, 32:33] = half * (c[31:32] + field[C, x + 2, 40:41, :])
    cx[1] = half * (centre(C, 0) + centre(C, -1))
    cx[9] = half * (centre(C, 7) + centre(C, 8))
    def operator(f, x, e):
        v = centre(f, x)
        yp, ym = around_y(f, x)
        zp, zm = around_z(v, e)
        out = cx[x + 2] * (v - centre(f, x + 1)) + cx[x + 1] * (v - centre(f, x - 1))
        out = out + (cy[x + 1, 1:33] * (v - yp) + cy[x + 1, 0:32] * (v - ym))
        return out + (czp[x + 1] * (v - zp) + czm[x + 1] * (v - zm))

    t_w = None
    for x in range(BX):
        out = operator(W0, x, ends(s_w0, x))
        field[W1, x + 2, ROWS, :] = out
        t_w = pack(out, t_w, x)
    tz[TW] = t_w
    send(IMAGE)
    pl.semaphore_wait(wave.at[1], 2)
    signal(wave.at[2], [in_plane(i, 0) for i in range(1, NGX)])

    @pl.when(in_layer)
    def _():
        pl.semaphore_wait(wave.at[4], 2)
        signal(ready, [in_column(k, 0) for k in range(1, NGZ)])


    def fold(v):
        return (v[0:8] + v[8:16]) + (v[16:24] + v[24:32])

    def plus(acc, v):
        v = fold(v)
        return v if acc is None else acc + v

    m = [None] * 6
    for x in range(BX):
        v, out = centre(W0, x), centre(W1, x)
        m[0], m[1], m[2] = plus(m[0], v * v), plus(m[1], v * out), plus(m[2], out * out)
    receive(OUTER)
    for x, side, inside in ((-1, xm_side, 7), (BX, xp_side, 0)):
        c = centre(C, x)
        if x < 0:
            cx[0] = half * (c + centre(C, -2))
        else:
            cx[10] = half * (c + centre(C, 9))
        after, before = around_y(C, x)
        cy[x + 1, 0:32] = half * (c + before)
        cy[x + 1, 32:33] = half * (c[31:32] + after[31:32])
        after, before = around_z(c, ends(swap(diagonal(side, 2)), inside))
        czp[x + 1] = half * (c + after)
        czm[x + 1] = half * (c + before)
    z_edge = jnp.where(has[zm_side], 0.0, 1.0)
    y_edge = jnp.where(has[ym_side], 0.0, 1.0)
    x_edge = jnp.where(has[xm_side], 0.0, 1.0)
    for x in range(BX):
        low = jnp.where(first, czm[x + 1], 0.0) * z_edge
        low = low + jnp.where(row32 == 0, cy[x + 1, 0:32], 0.0) * y_edge
        if x == 0:
            low = low + cx[1] * x_edge
        zlow[x] = low

    def face_values(t, qx, qy):
        lo, hi, own = tlo[t], thi[t], tz[t]
        v = pair(lo, hi)
        outer = jnp.where(low_lane, turn(lo, 1), turn(hi, -1))
        return (
            (v, outer, z_inside(own))
            + z_around_x(v, diagonal(xm_side, qx), diagonal(xp_side, qx))
            + z_around_y(v, diagonal(ym_side, qy), diagonal(yp_side, qy))
        )

    def row_values(f, q, r, beyond, own, side):
        v = row_of_field(f, r)
        after = jnp.where(sub8 == 7, field[f, 10, r : r + 1, :], turn(v, -1, 0))
        before = jnp.where(sub8 == 0, field[f, 1, r : r + 1, :], turn(v, 1, 0))
        zp, zm = around_z(v, ends_row(swap(diagonal(side, q)), side[1]))
        return v, row_of_field(f, beyond), row_of_field(f, own), after, before, zp, zm

    def weights(values, mask):
        c, *near_c = values
        return [mask * (half * (c + cn)) for cn in near_c]

    def applied(weight, values):
        v, *near_v = values
        terms = [w * (v - vn) for w, vn in zip(weight, near_v)]
        return ((terms[0] + terms[1]) + (terms[2] + terms[3])) + (terms[4] + terms[5])

    face_weights = weights(face_values(TC, 2, 2), has_z)
    rows_beyond = ((7, 6, 8, ym_side), (40, 41, 39, yp_side))
    row_weights = [weights(row_values(C, 2, *at), has[at[3]].astype(jnp.float32)) for at in rows_beyond]

    def image_row(at):
        out = applied(row_weights[at], row_values(W1, 4, *rows_beyond[at]))
        r = rows_beyond[at][0]
        for x in range(BX):
            field[W2, x + 2, r : r + 1, :] = out[x : x + 1]


    receive(IMAGE)
    s_w2 = swap(applied(face_weights, face_values(TW, 4, 4)))
    image_row(1)
    s_w1 = swap(pair(tlo[TW], thi[TW]))
    for x in range(BX):
        out = operator(W1, x, ends(s_w1, x))
        field[W2, x + 2, ROWS, :] = out
        v = centre(W1, x)
        m[3], m[4] = plus(m[3], v * out), plus(m[4], out * out)

    def image_plane(x, side, inside):
        out = operator(W1, x, ends(swap(diagonal(side, 4)), inside))
        field[W2, x + 2, ROWS, :] = jnp.where(has[side], out, 0.0)

    image_plane(BX, xp_side, 0)
    for x in range(BX):
        v = centre(W2, x)
        dx = v - centre(W2, x + 1)
        dy = v - field[W2, x + 2, 9:41, :]
        dz_ = v - jnp.where(last, ends(s_w2, x), turn(v, -1))
        m[5] = plus(
            m[5],
            (cx[x + 2] * (dx * dx) + cy[x + 1, 1:33] * (dy * dy)) + (czp[x + 1] * (dz_ * dz_) + zlow[x] * (v * v)),
        )

    row = jnp.zeros((1, BZ), jnp.float32)
    for i in range(6):
        row = jnp.where(lane8[0:1] == i, jnp.sum(m[i], keepdims=True), row)

    def sum_copy(phase, slot, partner):
        return pltpu.make_async_remote_copy(
            src_ref=reduce.at[phase, pl.ds(0, 1)], dst_ref=reduce.at[phase, pl.ds(slot + 1, 1)],
            send_sem=sum_send.at[phase], recv_sem=sum_recv.at[phase], device_id=partner, device_id_type=MESH,
        )

    def sum_whole(phase, count):
        ref = tally.at[pl.ds(0, count)]
        return pltpu.make_async_remote_copy(
            src_ref=ref, dst_ref=ref, send_sem=sum_send.at[phase], recv_sem=sum_recv.at[phase],
            device_id=plane[0], device_id_type=MESH,
        )

    def start_sum(phase, group):
        for slot, partner in enumerate(group):
            sum_copy(phase, slot, partner).start()

    me = (gx * NGY + gy) * NGZ + gz
    to_early = [
        pltpu.make_async_remote_copy(
            src_ref=reduce.at[0, pl.ds(0, 1)], dst_ref=direct.at[pl.ds(me, 1)], send_sem=sum_send.at[2],
            recv_sem=sum_recv.at[2], device_id=device, device_id_type=MESH,
        )
        for device in EARLY
    ]
    reduce[0, 0:1, :] = row

    pl.semaphore_wait(wave.at[2], NGX - 1)
    start_sum(0, plane)

    @pl.when(jnp.logical_not(in_layer))
    def _():
        pl.semaphore_wait(wave.at[4], 2)
        pl.semaphore_wait(ready, 1)

    for device, copy in zip(EARLY, to_early):
        pl.when((gx != device[0]) | (gy != device[1]) | (gz != device[2]))(copy.start)
    signal(wave.at[5], [in_column(0, 1)])

    image_plane(-1, xm_side, 7)
    image_row(0)
    copy_u = pltpu.make_async_copy(field.at[(U0,) + inner], u_out.at[0], copy_sem.at[0])
    copy_u.start()
    copy_v = pltpu.make_async_copy(field.at[(pl.ds(U1, 2),) + inner], u_out.at[pl.ds(1, 2)], copy_sem.at[2])
    copy_v.start()
    copy_w = pltpu.make_async_copy(field.at[(pl.ds(W0, 3),) + inner], w_out, copy_sem.at[1])
    copy_w.start()
    for i, (f, swapped) in enumerate(((W0, s_w0), (W1, s_w1), (W2, s_w2))):
        for x in range(BX):
            c = (0.5 / SCALE) * centre(C, x)
            g_out[i, 0, x] = c * (centre(f, x + 1) - centre(f, x - 1))
            after, before = around_y(f, x)
            g_out[i, 1, x] = c * (after - before)
            after, before = around_z(centre(f, x), ends(swapped, x))
            g_out[i, 2, x] = c * (after - before)
    receive(ENTH)
    s_h = swap(pair(tlo[TH], thi[TH]))
    for x in range(BX):
        h = centre(H, x)
        hyp, hym = around_y(H, x)
        hzp, hzm = around_z(h, ends(s_h, x))
        laplace = centre(H, x + 1) + centre(H, x - 1) + hyp + hym + hzp + hzm - 6.0 * h
        h_out[x] = h + DIFFUSE * laplace + HEATING * heat[x]
    copy_u.wait()
    copy_v.wait()
    copy_w.wait()
    for kind in range(4):
        whole(kind).wait_send()

    pl.semaphore_wait(wave.at[5], 1)
    sum_whole(0, 15).wait_recv()
    high, low = row_total(reduce[0])
    reduce[1, 0:1, :] = jnp.where(lane8 < 8, high, turn(low, 8))[0:1]

    @pl.when(jnp.logical_not(in_early_column))
    def _():
        start_sum(1, column)

    @pl.when(in_early_column)
    def _():
        for slot, partner in enumerate(column):
            pl.when(partner[2] != 0)(sum_copy(1, slot, partner).start)

    @pl.when(is_early)
    def _():
        direct[pl.ds(me, 1), :] = row
        sum_whole(2, DEVICES - 1).wait_recv()
        high, low = row_total(direct[...])
        total[0] = high
        total[1] = low

    @pl.when(jnp.logical_not(is_early))
    def _():
        sum_whole(1, 15).wait_recv()
        high, low = row_total(reduce[1])
        total[0] = high
        total[1] = low + turn(high, -8)

    high, low = total[0], total[1]
    high, low = quick_sum(high, low)

    def spread(v, i):
        return jnp.broadcast_to(v[:, i : i + 1], (8, BZ))

    moments = [(spread(high, i), spread(low, i)) for i in range(6)]
    for i, v in enumerate(solve_moments(moments)):
        c_out[i] = v
    sum_whole(0, 15).wait_send()

    @pl.when(jnp.logical_not(in_early_column))
    def _():
        sum_whole(1, 15).wait_send()
        sum_whole(2, len(EARLY)).wait_send()

    @pl.when(in_early_column & in_layer)
    def _():
        sum_whole(1, 14).wait_send()
        sum_whole(2, len(EARLY) - 1).wait_send()

    @pl.when(in_early_column & jnp.logical_not(in_layer))
    def _():
        sum_whole(1, 13).wait_send()
        sum_whole(2, len(EARLY)).wait_send()


def finish(w, g, u, h, c, vel_out, p_out, h_out, vel, p, sem):
    copy_h = pltpu.make_async_copy(h, h_out, sem.at[0])
    copy_h.start()
    c0, c1, c2 = (jnp.concatenate([c[i]] * 4, axis=0) for i in range(3))
    copies = [copy_h]
    for i in range(3):
        for x in range(BX):
            vel[i, x] = u[i, x] - (c0 * g[0, i, x] + c1 * g[1, i, x] + c2 * g[2, i, x])
        copy = pltpu.make_async_copy(vel.at[i], vel_out.at[i], sem.at[1 + i])
        copy.start()
        copies.append(copy)
    scaled = tuple(v * (1.0 / SCALE) for v in (c0, c1, c2))
    for x in range(BX):
        p[x] = scaled[0] * w[0, x] + scaled[1] * w[1, x] + scaled[2] * w[2, x]
    copy_p = pltpu.make_async_copy(p, p_out, sem.at[4])
    copy_p.start()
    for copy in copies + [copy_p]:
        copy.wait()


def shards(*args):
    block = (BX, BY, BZ)
    f32 = jnp.float32
    any_ref = pl.BlockSpec(memory_space=pl.ANY)
    vmem = pl.BlockSpec(memory_space=pltpu.VMEM)
    results = pl.pallas_call(
        kernel,
        out_shape=(
            jax.ShapeDtypeStruct((3,) + block, f32),
            jax.ShapeDtypeStruct((3, 3) + block, f32),
            jax.ShapeDtypeStruct((3,) + block, f32),
            jax.ShapeDtypeStruct(block, f32),
            jax.ShapeDtypeStruct((3, 8, BZ), f32),
        ),
        in_specs=[any_ref] * 7,
        out_specs=(vmem,) * 5,
        scratch_shapes=[
            pltpu.VMEM((FIELDS, BX + 4, BY + 16, BZ), f32),
            pltpu.VMEM((7, 8, BZ), f32),
            pltpu.VMEM((7, 8, BZ), f32),
            pltpu.VMEM((7, 8, BZ), f32),
            pltpu.VMEM((8, 5, 8, BZ), f32),
            pltpu.VMEM((BX + 3, BY, BZ), f32),
            pltpu.VMEM((BX + 2, BY + 8, BZ), f32),
            pltpu.VMEM((BX + 2, BY, BZ), f32),
            pltpu.VMEM((BX + 2, BY, BZ), f32),
            pltpu.VMEM(block, f32),
            pltpu.VMEM(block, f32),
            pltpu.VMEM((SLOTS, BZ), jnp.int32),
            pltpu.VMEM((SLOTS, BZ), jnp.int32),
            pltpu.VMEM((SLOTS, BZ), jnp.int32),
            pltpu.VMEM((BX * BY, SLOTS * BZ), jnp.bfloat16),
            pltpu.VMEM((BZ, SLOTS * BZ), jnp.bfloat16),
            pltpu.VMEM((BX * BY, BZ), f32),
            pltpu.VMEM(block, f32),
            pltpu.VMEM((2, 16, BZ), f32),
            pltpu.VMEM((DEVICES, BZ), f32),
            pltpu.VMEM((2, 8, BZ), f32),
            pltpu.VMEM((1024, BZ), f32),
            pltpu.SemaphoreType.DMA((8,)),
            pltpu.SemaphoreType.DMA((3,)),
            pltpu.SemaphoreType.DMA((4,)),
            pltpu.SemaphoreType.DMA((4,)),
            pltpu.SemaphoreType.DMA((3,)),
            pltpu.SemaphoreType.DMA((3,)),
            pltpu.SemaphoreType.REGULAR,
            pltpu.SemaphoreType.REGULAR((6,)),
        ],
        compiler_params=pltpu.CompilerParams(
            collective_id=0, has_side_effects=True, vmem_limit_bytes=32 * 1024 * 1024
        ),
        name="simple_step",
    )(*[pltpu.with_memory_space_constraint(a, pltpu.HBM) for a in args])
    results = [pltpu.with_memory_space_constraint(r, pltpu.VMEM) for r in results]
    return tuple(
        pl.pallas_call(
            finish,
            out_shape=(
                jax.ShapeDtypeStruct((3,) + block, f32),
                jax.ShapeDtypeStruct(block, f32),
                jax.ShapeDtypeStruct(block, f32),
            ),
            in_specs=[vmem] * 5,
            out_specs=(pl.BlockSpec(memory_space=pltpu.HBM),) * 3,
            scratch_shapes=[
                pltpu.VMEM((3,) + block, f32),
                pltpu.VMEM(block, f32),
                pltpu.SemaphoreType.DMA((5,)),
            ],
            compiler_params=pltpu.CompilerParams(vmem_limit_bytes=8 * 1024 * 1024),
            name="finish",
        )(*results)
    )


def solution(mesh):
    in_specs = (
        P(None, "gx", "gy", "gz"),
        P("gx", "gy", "gz"),
        P("gx", "gy", "gz"),
        P("gx", "gy", "gz"),
        P(("gx", "gy", "gz"), None),
        P(("gx", "gy", "gz"), None),
        P(("gx", "gy", "gz"), None),
    )
    out_specs = (P(None, "gx", "gy", "gz"), P("gx", "gy", "gz"), P("gx", "gy", "gz"))
    return jax.shard_map(shards, mesh=mesh, in_specs=in_specs, out_specs=out_specs, check_vma=False)
```
